256 devices in a mesh: dp: 32 (over y, z), col: 8 (over x, core).
Axes of the slice: x: 4, y: 4, z: 8, core: 2. Of those that a mesh axis runs over, the one named last changes fastest.
Arguments:
- grads: bfloat16 [65536, 4096], P('dp', 'col'), may hold values from -6 to 6
- signs: int32 [65536], P('dp'), may hold values from -1 to 1, as said below
- picks: int32 [128], replicated, may hold values from 0 to 511, as said below
Outputs:
- gram: float32 [4096, 4096], P('dp', 'col')
The draws below stay inside these ranges and needn't reach their ends.
Inputs may be any that keep to these rules, and one draw needn't show every extreme that they name: `signs`: each entry is +1 or -1. `picks`: the 128 indices are distinct; both 0 and 511 are always among them.
All inputs are finite; a program needn't handle non-finite values.
Results may differ from the reference program's by a relative error of at most 0.0026.
Values may be sent and summed in bfloat16 or wider, within the bound.
No kernel may reach another device: no remote copies, remote signals or barrier semaphores. Data moves between devices by JAX's collectives and lax.ppermute only.
A program may use at most 128 MiB of HBM per device.

```python
import math
import jax
import jax.numpy as jnp
from jax import lax

C = 4096
BLOCK = 128
ROWS_DEV = 2048
ROWS = 65536
BLOCKS = 512
SAMPLES = 128
SKETCH_ROWS = 16384
N_DP = 32
N_COL = 8


def draw_signs(key, part):
    key = jax.random.fold_in(key, 11)
    coins = jax.random.randint(key, (ROWS,), 0, 2)
    return (coins * 2 - 1).astype(jnp.int32)


def draw_picks(key, part):
    key = jax.random.fold_in(key, 23)
    first_key, order_key = jax.random.split(key)
    middle = jax.random.permutation(first_key, BLOCKS - 2)[:SAMPLES - 2] + 1
    chosen = jnp.concatenate([jnp.array([0, BLOCKS - 1], dtype=jnp.int32), middle.astype(jnp.int32)])
    order = jax.random.permutation(order_key, SAMPLES)
    return chosen[order].astype(jnp.int32)


def shard_levels(key, dims, cuts, least, largest):
    gain, own = 1.0, jax.random.fold_in(key, 6)
    for position, parts in cuts:
        steps = jnp.exp(jax.random.uniform(jax.random.fold_in(own, position), (parts,), jnp.float32, least / len(cuts), largest / len(cuts)))
        gain = gain * jnp.repeat(steps, dims[position] // parts).reshape([-1 if axis == position else 1 for axis in range(len(dims))])
    return gain


def gaussian(own_key, shape, width, reach, cuts=(), kind=jnp.bfloat16):
    result = jax.random.normal(own_key, shape, jnp.float32) * width
    if len(cuts) > 0:
        result = shard_levels(own_key, shape, cuts, -0.22, 0.18) * result
    return jnp.clip(result, min=-reach, max=reach).astype(kind)


def setup_inputs(seed: int = 0) -> dict:
    seeds = jax.random.split(jax.random.key(seed), 4)
    grads = gaussian(seeds[0], (ROWS, C), 1.0, 6.0, ((0, 32), (1, 8)))
    signs = draw_signs(jax.random.fold_in(seeds[3], 71), 0)
    picks = draw_picks(jax.random.fold_in(seeds[3], 71), 0)
    return dict(grads=grads, signs=signs, picks=picks)


def parity_sign(left, right):
    both = jnp.bitwise_and(left, right)
    count = jnp.zeros_like(both)
    for shift_bit in range(16):
        count = count + jnp.bitwise_and(jnp.right_shift(both, shift_bit), 1)
    return 1 - 2 * jnp.bitwise_and(count, 1)

def hadamard_table(order):
    index = jnp.arange(order, dtype=jnp.int32)
    return parity_sign(index[:, None], index[None, :])

def reference(grads, signs, picks):
    rows = ROWS_DEV * N_DP
    table = hadamard_table(ROWS_DEV).astype(jnp.float32)
    outer = hadamard_table(N_DP).astype(jnp.float32)
    flipped = grads * signs.astype(jnp.bfloat16)[:, None]
    panels = flipped.reshape(rows, N_COL, C // N_COL).transpose(1, 0, 2)
    scale = 1.0 / math.sqrt(rows)

    def one_panel(panel):
        blocks = panel.reshape(N_DP, ROWS_DEV, C // N_COL).astype(jnp.float32)
        local = jnp.einsum('ij,djc->dic', table, blocks, precision=lax.Precision.HIGHEST).astype(jnp.bfloat16)
        mixed = jnp.einsum('de,eic->dic', outer, local.astype(jnp.float32), precision=lax.Precision.HIGHEST)
        scaled = (mixed * scale).reshape(BLOCKS, BLOCK, C // N_COL)
        return scaled[picks].astype(jnp.bfloat16).reshape(SKETCH_ROWS, C // N_COL)
    sketch = lax.map(one_panel, panels).transpose(1, 0, 2).reshape(SKETCH_ROWS, C)
    gram = jnp.dot(sketch.T, sketch, preferred_element_type=jnp.float32)
    return gram / jnp.float32(SKETCH_ROWS)
```

```python
import jax
import jax.numpy as jnp
from jax import lax
from jax.experimental import pallas as pl
from jax.experimental.pallas import tpu as pltpu
from jax.sharding import PartitionSpec as P

NY, NZ, NX, NCORE = 4, 8, 4, 2
BLOCK = 128
LANES = 128
PER_DEV = 16
N_BLOCKS = 512
CHUNK = BLOCK // NZ
MIB = 1 << 20


def pack_kernel(at, grads_ref, signs_ref, out_ref):
    z = pl.program_id(0)
    for b in range(PER_DEV):
        sign = jnp.broadcast_to(signs_ref[:, b : b + 1], (CHUNK, LANES)).astype(jnp.bfloat16)
        for y in range(NY):
            quarter = lax.rem(z - y + at[0] + NY, NY)
            lanes = pl.ds(pl.multiple_of(quarter * LANES, LANES), LANES)
            out_ref[y, 0, b] = grads_ref[b, :, lanes] * sign


def pack(grads, signs, x):
    blocks = grads.reshape(PER_DEV, BLOCK, NY * LANES)
    columns = signs.reshape(PER_DEV, BLOCK).T.astype(jnp.float32)
    return pl.pallas_call(
        pack_kernel,
        grid_spec=pltpu.PrefetchScalarGridSpec(
            num_scalar_prefetch=1,
            grid=(NZ,),
            in_specs=[
                pl.BlockSpec((PER_DEV, CHUNK, NY * LANES), lambda z, at: (0, z, 0)),
                pl.BlockSpec((CHUNK, PER_DEV), lambda z, at: (z, 0)),
            ],
            out_specs=pl.BlockSpec(
                (NY, 1, PER_DEV, CHUNK, LANES), lambda z, at: (0, z, 0, 0, 0)
            ),
        ),
        out_shape=jax.ShapeDtypeStruct((NY, NZ, PER_DEV, CHUNK, LANES), jnp.bfloat16),
        name="pack",
    )(x.reshape(1), blocks, columns)


def hadamard(parts):
    span = 1
    while span < len(parts):
        done = list(parts)
        for i in range(len(parts)):
            if not i & span:
                done[i] = parts[i] + parts[i + span]
                done[i + span] = parts[i] - parts[i + span]
        parts = done
        span *= 2
    return parts


def mix_kernel(picks_ref, raw_ref, out_ref, work):
    half = N_BLOCKS // 2

    @pl.loop(0, N_BLOCKS // 16)
    def _(d):
        base = d * 16
        parts = [raw_ref[base + b].astype(jnp.float32) for b in range(16)]
        for b, part in enumerate(hadamard(parts)):
            work[base + b] = part

    @pl.loop(0, 32)
    def _(i):
        base = lax.div(i, 16) * half + lax.rem(i, 16)
        parts = [work[base + 16 * e] for e in range(16)]
        for e, part in enumerate(hadamard(parts)):
            work[base + 16 * e] = part

    @pl.loop(0, out_ref.shape[0], unroll=4)
    def _(k):
        pick = picks_ref[k]
        low = lax.rem(pick, half)
        side = (1 - 2 * lax.div(pick, half)).astype(jnp.float32)
        out_ref[k] = (work[low] + side * work[low + half]).astype(out_ref.dtype)


def mix(raw, picks):
    samples = picks.shape[0]
    return pl.pallas_call(
        mix_kernel,
        grid_spec=pltpu.PrefetchScalarGridSpec(
            num_scalar_prefetch=1,
            grid=(1,),
            in_specs=[pl.BlockSpec((N_BLOCKS, CHUNK, LANES), lambda i, p: (0, 0, 0))],
            out_specs=pl.BlockSpec((samples, CHUNK, LANES), lambda i, p: (0, 0, 0)),
            scratch_shapes=[pltpu.VMEM((N_BLOCKS, CHUNK, LANES), jnp.float32)],
        ),
        out_shape=jax.ShapeDtypeStruct((samples, CHUNK, LANES), jnp.bfloat16),
        compiler_params=pltpu.CompilerParams(vmem_limit_bytes=24 * MIB),
        name="mix",
    )(picks, raw)


def gram_kernel(at, *refs):
    cols = refs[:4]
    rows = (refs[4:8], refs[8:12])
    out_ref, flat, right, left, flat_sems, right_sems = refs[12:]
    depth = cols[0].shape[0]
    x, core, turn = at[0], at[1], at[2]
    flat_copies = [
        pltpu.make_async_copy(cols[j], flat.at[j], flat_sems.at[j]) for j in range(NY)
    ]
    right_copies = [
        [
            pltpu.make_async_copy(
                rows[c][j], right.at[j, :, pl.ds(c * LANES, LANES)], right_sems.at[j, c]
            )
            for c in range(NCORE)
        ]
        for j in range(NX)
    ]
    for copy in flat_copies:
        copy.start()
    for pair in right_copies:
        for copy in pair:
            copy.start()
    for j in range(NY):
        flat_copies[j].wait()
        quarter = lax.rem(turn + j, NY)
        where = pl.ds(pl.multiple_of(quarter * LANES, LANES), LANES)
        left[where, :] = flat[j].T
    for j in range(NX):
        for copy in right_copies[j]:
            copy.wait()
        panel = lax.rem(x + NX - j, NX) * NCORE
        for m in range(2):
            part = pl.ds(m * 2 * LANES, 2 * LANES)
            block = jnp.dot(left[part, :], right[j], preferred_element_type=jnp.float32)
            block = block.astype(out_ref.dtype)
            out_ref[panel + core, part, :] = block[:, :LANES]
            out_ref[panel + 1 - core, part, :] = block[:, LANES:]


def gram_part(at, cols, own, other):
    depth = cols[0].shape[0]
    whole = pl.BlockSpec(memory_space=pl.ANY)
    return pl.pallas_call(
        gram_kernel,
        grid_spec=pltpu.PrefetchScalarGridSpec(
            num_scalar_prefetch=1,
            grid=(1,),
            in_specs=[whole] * 12,
            out_specs=pl.BlockSpec((NX * NCORE, NY * LANES, LANES), lambda i, at: (0, 0, 0)),
            scratch_shapes=[
                pltpu.VMEM((NY, depth, LANES), jnp.bfloat16),
                pltpu.VMEM((NX, depth, NCORE * LANES), jnp.bfloat16),
                pltpu.VMEM((NY * LANES, depth), jnp.bfloat16),
                pltpu.SemaphoreType.DMA((NY,)),
                pltpu.SemaphoreType.DMA((NX, NCORE)),
            ],
        ),
        out_shape=jax.ShapeDtypeStruct((NX * NCORE, NY * LANES, LANES), jnp.bfloat16),
        compiler_params=pltpu.CompilerParams(vmem_limit_bytes=32 * MIB),
        name="gram_part",
    )(at, *cols, *own, *other)


def finish_kernel(scale, parts_ref, out_ref):
    total = parts_ref[0].astype(jnp.float32)
    for k in range(1, parts_ref.shape[0]):
        total = total + parts_ref[k].astype(jnp.float32)
    out_ref[...] = (total * scale).T


def finish(parts, scale):
    count, width, rows = parts.shape
    return pl.pallas_call(
        lambda parts_ref, out_ref: finish_kernel(scale, parts_ref, out_ref),
        grid=(width // LANES,),
        in_specs=[pl.BlockSpec((count, LANES, rows), lambda i: (0, i, 0))],
        out_specs=pl.BlockSpec((rows, LANES), lambda i: (0, i)),
        out_shape=jax.ShapeDtypeStruct((rows, width), jnp.float32),
        name="finish",
    )(parts)


def on_device(grads, signs, picks):
    dp, col = lax.axis_index("dp"), lax.axis_index("col")
    y, z = dp // NZ, dp % NZ
    x, core = col // NCORE, col % NCORE

    outgoing = pack(grads, signs, x).reshape(NY * NZ, PER_DEV, CHUNK, LANES)
    raw = lax.all_to_all(outgoing, "dp", split_axis=0, concat_axis=0, tiled=True)
    sketch = mix(raw.reshape(N_BLOCKS, CHUNK, LANES), picks).reshape(-1, LANES)

    def along_x(value, step):
        return lax.ppermute(value, "col", [(i, (i + NCORE * step) % (NX * NCORE)) for i in range(NX * NCORE)])

    def along_y(value, step):
        return lax.ppermute(value, "dp", [(i, (i + NZ * step) % (NY * NZ)) for i in range(NY * NZ)])

    def swap(value):
        return lax.ppermute(value, "col", [(i, i ^ 1) for i in range(NX * NCORE)])

    own = [sketch] + [along_x(sketch, j) for j in range(1, NX)]
    cols = [sketch] + [along_y(sketch, j) for j in range(1, NY)]
    other = [swap(piece) for piece in own]
    at = jnp.stack([x, core, (z - y + x + NY) % NY]).astype(jnp.int32)
    partial = gram_part(at, cols, own, other)

    groups = [
        [gy * NZ + (s + gy) % NY + NY * half for gy in range(NY) for half in range(NZ // NY)]
        for s in range(NY)
    ]
    parts = lax.all_to_all(
        partial, "dp", split_axis=0, concat_axis=0, axis_index_groups=groups, tiled=True
    )
    total_rows = grads.shape[0] * NY * NZ
    scale = BLOCK / (total_rows * picks.shape[0] * BLOCK)
    return finish(parts, scale)


def solution(mesh):
    placed = (P("dp", "col"), P("dp"), P())
    return jax.shard_map(
        on_device, mesh=mesh, in_specs=placed, out_specs=P("dp", "col"), check_vma=False
    )
```

```python
import jax
import jax.numpy as jnp
from jax import lax
from jax.experimental import pallas as pl
from jax.experimental.pallas import tpu as pltpu
from jax.sharding import PartitionSpec as P

NY, NZ, NX, NCORE = 4, 8, 4, 2
BLOCK = 128
LANES = 128
PER_DEV = 16
N_BLOCKS = 512
CHUNK = BLOCK // NZ
MIB = 1 << 20


SCALARS = pl.BlockSpec(memory_space=pltpu.SMEM)
LOCAL = pl.BlockSpec(memory_space=pltpu.VMEM)


def pack_kernel(at, grads_ref, signs_ref, out_ref):
    columns = signs_ref[...].astype(jnp.float32).T
    for z in range(NZ):
        for y in range(NY):
            quarter = lax.rem(z - y + at[0] + NY, NY)
            lanes = pl.ds(pl.multiple_of(quarter * LANES, LANES), LANES)
            for b in range(PER_DEV):
                sign = columns[z * CHUNK : (z + 1) * CHUNK, b : b + 1]
                sign = jnp.broadcast_to(sign, (CHUNK, LANES)).astype(jnp.bfloat16)
                rows = pl.ds(z * CHUNK, CHUNK)
                out_ref[y, z, b] = grads_ref[b, rows, lanes] * sign


def pack(grads, signs, at):
    blocks = grads.reshape(PER_DEV, BLOCK, NY * LANES)
    return pl.pallas_call(
        pack_kernel,
        in_specs=[SCALARS, LOCAL, LOCAL],
        out_specs=LOCAL,
        out_shape=jax.ShapeDtypeStruct((NY, NZ, PER_DEV, CHUNK, LANES), jnp.bfloat16),
        compiler_params=pltpu.CompilerParams(vmem_limit_bytes=16 * MIB),
        name="pack",
    )(at, blocks, signs.reshape(PER_DEV, BLOCK))


def hadamard(parts):
    span = 1
    while span < len(parts):
        done = list(parts)
        for i in range(len(parts)):
            if not i & span:
                done[i] = parts[i] + parts[i + span]
                done[i + span] = parts[i] - parts[i + span]
        parts = done
        span *= 2
    return parts


def mix_kernel(picks_ref, raw_ref, out_ref, work):
    half = N_BLOCKS // 2

    @pl.loop(0, N_BLOCKS // 16)
    def _(d):
        base = d * 16
        parts = [raw_ref[base + b].astype(jnp.float32) for b in range(16)]
        for b, part in enumerate(hadamard(parts)):
            work[base + b] = part

    @pl.loop(0, 32)
    def _(i):
        base = lax.div(i, 16) * half + lax.rem(i, 16)
        parts = [work[base + 16 * e] for e in range(16)]
        for e, part in enumerate(hadamard(parts)):
            work[base + 16 * e] = part

    @pl.loop(0, out_ref.shape[0], unroll=4)
    def _(k):
        pick = picks_ref[k]
        low = lax.rem(pick, half)
        side = (1 - 2 * lax.div(pick, half)).astype(jnp.float32)
        out_ref[k] = (work[low] + side * work[low + half]).astype(out_ref.dtype)


def mix(raw, picks):
    samples = picks.shape[0]
    return pl.pallas_call(
        mix_kernel,
        in_specs=[SCALARS, LOCAL],
        out_specs=LOCAL,
        scratch_shapes=[pltpu.VMEM((N_BLOCKS, CHUNK, LANES), jnp.float32)],
        out_shape=jax.ShapeDtypeStruct((samples, CHUNK, LANES), jnp.bfloat16),
        compiler_params=pltpu.CompilerParams(vmem_limit_bytes=16 * MIB),
        name="mix",
    )(picks, raw)


PIECES = 5


def gram_kernel(at, *refs):
    cols, rows = refs[:PIECES], (refs[PIECES : 2 * PIECES], refs[2 * PIECES : 3 * PIECES])
    out_ref, left = refs[3 * PIECES :]
    half = cols[2].shape[0]
    x, core, turn = at[0], at[1], at[2]
    spots = [(0, 0, 2 * half), (1, 0, 2 * half), (2, 0, half), (2, half, half), (3, 0, 2 * half)]
    for p, (j, start, size) in enumerate(spots):
        quarter = lax.rem(turn + j, NY)
        where = pl.ds(pl.multiple_of(quarter * LANES, LANES), LANES)
        left[where, pl.ds(start, size)] = cols[p][...].T
    for pieces, j in (((0,), 0), ((1,), 1), ((4,), 3), ((2, 3), 2)):
        panel = lax.rem(x + NX - j, NX) * NCORE
        for m in range(2):
            part = pl.ds(m * 2 * LANES, 2 * LANES)
            block = None
            for p in pieces:
                pair = jnp.concatenate([rows[0][p][...], rows[1][p][...]], axis=1)
                depth = pl.ds(spots[p][1], spots[p][2])
                term = jnp.dot(left[part, depth], pair, preferred_element_type=jnp.float32)
                block = term if block is None else block + term
            block = block.astype(out_ref.dtype)
            out_ref[panel + core, part, :] = block[:, :LANES]
            out_ref[panel + 1 - core, part, :] = block[:, LANES:]


def gram_part(at, cols, own, other):
    return pl.pallas_call(
        gram_kernel,
        in_specs=[SCALARS] + [LOCAL] * (3 * PIECES),
        out_specs=LOCAL,
        scratch_shapes=[pltpu.VMEM((NY * LANES, cols[0].shape[0]), jnp.bfloat16)],
        out_shape=jax.ShapeDtypeStruct((NX * NCORE, NY * LANES, LANES), jnp.bfloat16),
        compiler_params=pltpu.CompilerParams(vmem_limit_bytes=24 * MIB),
        name="gram_part",
    )(at, *cols, *own, *other)


def finish_kernel(scale, parts_ref, out_ref):
    for i in range(out_ref.shape[1] // LANES):
        part = pl.ds(i * LANES, LANES)
        total = parts_ref[0, part].astype(jnp.float32)
        for k in range(1, parts_ref.shape[0]):
            total = total + parts_ref[k, part].astype(jnp.float32)
        out_ref[:, part] = (total * scale).T


def finish(parts, scale):
    count, width, rows = parts.shape
    return pl.pallas_call(
        lambda parts_ref, out_ref: finish_kernel(scale, parts_ref, out_ref),
        out_shape=jax.ShapeDtypeStruct((rows, width), jnp.float32),
        compiler_params=pltpu.CompilerParams(vmem_limit_bytes=16 * MIB),
        name="finish",
    )(parts)


def on_device(grads, signs, picks):
    dp, col = lax.axis_index("dp"), lax.axis_index("col")
    y, z = lax.div(dp, NZ), lax.rem(dp, NZ)
    x, core = lax.div(col, NCORE), lax.rem(col, NCORE)
    at = jnp.stack([x, core, lax.rem(z - y + x + NY, NY)])

    outgoing = pack(grads, signs, at).reshape(NY * NZ, PER_DEV, CHUNK, LANES)
    raw = lax.all_to_all(outgoing, "dp", split_axis=0, concat_axis=0, tiled=True)
    sketch = mix(raw.reshape(N_BLOCKS, CHUNK, LANES), picks).reshape(-1, LANES)

    def along_x(value, step):
        return lax.ppermute(value, "col", [(i, (i + NCORE * step) % (NX * NCORE)) for i in range(NX * NCORE)])

    def along_y(value, step):
        return lax.ppermute(value, "dp", [(i, (i + NZ * step) % (NY * NZ)) for i in range(NY * NZ)])

    def swap(value):
        return lax.ppermute(value, "col", [(i, i ^ 1) for i in range(NX * NCORE)])

    depth = sketch.shape[0] // 2
    x_up, x_down = along_x(sketch, 1), along_x(sketch, -1)
    y_up, y_down = along_y(sketch, 1), along_y(sketch, -1)
    x_far = (along_x(x_up[:depth], 1), along_x(x_down[depth:], -1))
    y_far = (along_y(y_up[:depth], 1), along_y(y_down[depth:], -1))
    own = [sketch, x_up, *x_far, x_down]
    cols = [sketch, y_up, *y_far, y_down]
    other = [swap(piece) for piece in own]
    partial = gram_part(at, cols, own, other)

    groups = [
        [gy * NZ + (s + gy) % NY + NY * half for gy in range(NY) for half in range(NZ // NY)]
        for s in range(NY)
    ]
    parts = lax.all_to_all(
        partial, "dp", split_axis=0, concat_axis=0, axis_index_groups=groups, tiled=True
    )
    total_rows = grads.shape[0] * NY * NZ
    scale = BLOCK / (total_rows * picks.shape[0] * BLOCK)
    return finish(parts, scale)


def solution(mesh):
    placed = (P("dp", "col"), P("dp"), P())
    return jax.shard_map(
        on_device, mesh=mesh, in_specs=placed, out_specs=P("dp", "col"), check_vma=False
    )
```

```python
import functools

import jax
import jax.numpy as jnp
from jax import lax
from jax.experimental import pallas as pl
from jax.experimental.pallas import tpu as pltpu
from jax.sharding import PartitionSpec as P

NY, NZ, NX, NCORE = 4, 8, 4, 2
BLOCK = 128
LANES = 128
PER_DEV = 16
N_BLOCKS = 512
CHUNK = BLOCK // NZ
MIB = 1 << 20
PACK_STEPS = 4


SCALARS = pl.BlockSpec(memory_space=pltpu.SMEM)
LOCAL = pl.BlockSpec(memory_space=pltpu.VMEM)


def pack_kernel(at, grads_ref, signs_ref, out_ref, taken, packed, signs, in_sems, out_sems):
    step = PER_DEV // PACK_STEPS
    parts = [pl.ds(i * step, step) for i in range(PACK_STEPS)]
    reads = [
        pltpu.make_async_copy(grads_ref.at[part], taken.at[part], in_sems.at[i])
        for i, part in enumerate(parts)
    ]
    writes = [
        pltpu.make_async_copy(packed.at[:, :, part], out_ref.at[:, :, part], out_sems.at[i])
        for i, part in enumerate(parts)
    ]
    sign_read = pltpu.make_async_copy(signs_ref, signs, in_sems.at[PACK_STEPS])
    sign_read.start()
    for read in reads:
        read.start()
    sign_read.wait()
    columns = signs[...].astype(jnp.float32).T
    for b in range(PER_DEV):
        if b % step == 0:
            reads[b // step].wait()
        for z in range(NZ):
            sign = columns[z * CHUNK : (z + 1) * CHUNK, b : b + 1]
            sign = jnp.broadcast_to(sign, (CHUNK, LANES)).astype(jnp.bfloat16)
            for y in range(NY):
                quarter = lax.rem(z - y + at[0] + NY, NY)
                lanes = pl.ds(pl.multiple_of(quarter * LANES, LANES), LANES)
                packed[y, z, b] = taken[b, pl.ds(z * CHUNK, CHUNK), lanes] * sign
        if b % step == step - 1:
            writes[b // step].start()
    for write in writes:
        write.wait()


def pack(grads, signs, at):
    blocks = grads.reshape(PER_DEV, BLOCK, NY * LANES)
    packed = jax.ShapeDtypeStruct((NY, NZ, PER_DEV, CHUNK, LANES), jnp.bfloat16)
    whole = pl.BlockSpec(memory_space=pl.ANY)
    return pl.pallas_call(
        pack_kernel,
        in_specs=[SCALARS, whole, whole],
        out_specs=whole,
        out_shape=packed,
        scratch_shapes=[
            pltpu.VMEM(blocks.shape, jnp.bfloat16),
            pltpu.VMEM(packed.shape, jnp.bfloat16),
            pltpu.VMEM((PER_DEV, BLOCK), jnp.int32),
            pltpu.SemaphoreType.DMA((PACK_STEPS + 1,)),
            pltpu.SemaphoreType.DMA((PACK_STEPS,)),
        ],
        compiler_params=pltpu.CompilerParams(vmem_limit_bytes=62 * MIB),
        name="pack",
    )(at, blocks, signs.reshape(PER_DEV, BLOCK))


def hadamard(parts):
    span = 1
    while span < len(parts):
        done = list(parts)
        for i in range(len(parts)):
            if not i & span:
                done[i] = parts[i] + parts[i + span]
                done[i + span] = parts[i] - parts[i + span]
        parts = done
        span *= 2
    return parts


def mix_kernel(at, picks_ref, raw_ref, kept_ref, given_ref, work):
    half = N_BLOCKS // 2

    @pl.loop(0, N_BLOCKS // 16)
    def _(d):
        base = d * 16
        parts = [raw_ref[base + b].astype(jnp.float32) for b in range(16)]
        for b, part in enumerate(hadamard(parts)):
            work[base + b] = part

    @pl.loop(0, 32)
    def _(i):
        base = lax.div(i, 16) * half + lax.rem(i, 16)
        parts = [work[base + 16 * e] for e in range(16)]
        for e, part in enumerate(hadamard(parts)):
            work[base + 16 * e] = part

    def sample(k):
        pick = picks_ref[k]
        low = lax.rem(pick, half)
        side = (1 - 2 * lax.div(pick, half)).astype(jnp.float32)
        return (work[low] + side * work[low + half]).astype(kept_ref.dtype)

    count = kept_ref.shape[0]

    @pl.loop(0, count, unroll=4)
    def _(k):
        kept_ref[k] = sample(at[1] * count + k)
        given_ref[k] = sample((1 - at[1]) * count + k)


def mix(at, raw, picks):
    part = jax.ShapeDtypeStruct((picks.shape[0] // NCORE, CHUNK, LANES), jnp.bfloat16)
    return pl.pallas_call(
        mix_kernel,
        in_specs=[SCALARS, SCALARS, LOCAL],
        out_specs=[LOCAL, LOCAL],
        scratch_shapes=[pltpu.VMEM((N_BLOCKS, CHUNK, LANES), jnp.float32)],
        out_shape=[part, part],
        compiler_params=pltpu.CompilerParams(vmem_limit_bytes=16 * MIB),
        name="mix",
    )(at, picks, raw)


def gram_kernel(which, at, *refs):
    cols, rows, (out_ref, left) = refs[:5], refs[5:10], refs[10:]
    x, core, turn = at[0], at[1], at[2]
    for j in range(NY):
        piece = (cols[0], cols[1], cols[2 + which], cols[4])[j]
        quarter = lax.rem(turn + j, NY)
        where = pl.ds(pl.multiple_of(quarter * LANES, LANES), LANES)
        left[where, :] = (piece[...] if j == 2 else piece[which]).T
    for j in range(NX):
        if j == 2:
            pair = [rows[2][...], rows[3][...]]
        else:
            piece = (rows[0], rows[1], None, rows[4])[j]
            pair = [piece[0], piece[1]]
        pair = jnp.concatenate(pair, axis=1)
        panel = lax.rem(x + NX - j, NX) * NCORE
        for m in range(2):
            part = pl.ds(m * 2 * LANES, 2 * LANES)
            block = jnp.dot(left[part, :], pair, preferred_element_type=jnp.float32)
            block = block.astype(out_ref.dtype)
            out_ref[panel + core, part, :] = block[:, :LANES]
            out_ref[panel + 1 - core, part, :] = block[:, LANES:]


def gram_part(which, at, cols, rows, dtype):
    depth = cols[0].shape[1]
    flops = 2 * depth * NY * LANES * NX * NCORE * LANES
    return pl.pallas_call(
        functools.partial(gram_kernel, which),
        in_specs=[SCALARS] + [LOCAL] * 10,
        out_specs=LOCAL,
        scratch_shapes=[pltpu.VMEM((NY * LANES, depth), jnp.bfloat16)],
        out_shape=jax.ShapeDtypeStruct((NX * NCORE, NY * LANES, LANES), dtype),
        compiler_params=pltpu.CompilerParams(vmem_limit_bytes=16 * MIB),
        cost_estimate=pl.CostEstimate(flops=flops, bytes_accessed=8 * MIB, transcendentals=0),
        name="gram_other" if which else "gram_own",
    )(at, *cols, *rows)


def finish_kernel(scale, parts_ref, out_ref):
    for i in range(out_ref.shape[1] // LANES):
        part = pl.ds(i * LANES, LANES)
        total = parts_ref[0, part].astype(jnp.float32)
        for k in range(1, parts_ref.shape[0]):
            total = total + parts_ref[k, part].astype(jnp.float32)
        out_ref[:, part] = (total * scale).T


def finish(parts, scale):
    count, width, rows = parts.shape
    return pl.pallas_call(
        lambda parts_ref, out_ref: finish_kernel(scale, parts_ref, out_ref),
        out_shape=jax.ShapeDtypeStruct((rows, width), jnp.float32),
        compiler_params=pltpu.CompilerParams(vmem_limit_bytes=16 * MIB),
        name="finish",
    )(parts)


def on_device(grads, signs, picks):
    dp, col = lax.axis_index("dp"), lax.axis_index("col")
    y, z = lax.div(dp, NZ), lax.rem(dp, NZ)
    x, core = lax.div(col, NCORE), lax.rem(col, NCORE)
    at = jnp.stack([x, core, lax.rem(z - y + x + NY, NY)])

    outgoing = pack(grads, signs, at).reshape(NY * NZ, PER_DEV, CHUNK, LANES)
    raw = lax.all_to_all(outgoing, "dp", split_axis=0, concat_axis=0, tiled=True)
    kept, given = mix(at, raw.reshape(N_BLOCKS, CHUNK, LANES), picks)

    def along_x(value, step):
        return lax.ppermute(value, "col", [(i, (i + NCORE * step) % (NX * NCORE)) for i in range(NX * NCORE)])

    def along_y(value, step):
        return lax.ppermute(value, "dp", [(i, (i + NZ * step) % (NY * NZ)) for i in range(NY * NZ)])

    def swap(value):
        return lax.ppermute(value, "col", [(i, i ^ 1) for i in range(NX * NCORE)])

    sketch = jnp.stack([kept, swap(given)]).reshape(NCORE, -1, LANES)
    x_up, x_down = along_x(sketch, 1), along_x(sketch, -1)
    y_up, y_down = along_y(sketch, 1), along_y(sketch, -1)
    rows = [sketch, x_up, along_x(x_up[0], 1), along_x(x_down[1], -1), x_down]
    cols = [sketch, y_up, along_y(y_up[0], 1), along_y(y_down[1], -1), y_down]
    away = swap(gram_part(1, at, cols, rows, jnp.bfloat16))
    partial = gram_part(0, at, cols, rows, jnp.float32)
    partial = (partial + away.astype(jnp.float32)).astype(jnp.bfloat16)

    groups = [
        [gy * NZ + (s + gy) % NY + NY * half for gy in range(NY) for half in range(NZ // NY)]
        for s in range(NY)
    ]
    parts = lax.all_to_all(
        partial, "dp", split_axis=0, concat_axis=0, axis_index_groups=groups, tiled=True
    )
    total_rows = grads.shape[0] * NY * NZ
    scale = BLOCK / (total_rows * picks.shape[0] * BLOCK)
    return finish(parts, scale)


def solution(mesh):
    placed = (P("dp", "col"), P("dp"), P())
    return jax.shard_map(
        on_device, mesh=mesh, in_specs=placed, out_specs=P("dp", "col"), check_vma=False
    )
```

```python
import functools

import jax
import jax.numpy as jnp
from jax import lax
from jax.experimental import pallas as pl
from jax.experimental.pallas import tpu as pltpu
from jax.sharding import PartitionSpec as P

NY, NZ, NX, NCORE = 4, 8, 4, 2
BLOCK = 128
LANES = 128
PER_DEV = 16
N_BLOCKS = 512
CHUNK = BLOCK // NZ
MIB = 1 << 20


SCALARS = pl.BlockSpec(memory_space=pltpu.SMEM)
LOCAL = pl.BlockSpec(memory_space=pltpu.VMEM)


def pack_kernel(at, grads_ref, signs_ref, out_ref):
    columns = signs_ref[...].astype(jnp.float32).T
    for z in range(NZ):
        for y in range(NY):
            quarter = lax.rem(z - y + at[0] + NY, NY)
            lanes = pl.ds(pl.multiple_of(quarter * LANES, LANES), LANES)
            for b in range(PER_DEV):
                sign = columns[z * CHUNK : (z + 1) * CHUNK, b : b + 1]
                sign = jnp.broadcast_to(sign, (CHUNK, LANES)).astype(jnp.bfloat16)
                rows = pl.ds(z * CHUNK, CHUNK)
                out_ref[y, z, b] = grads_ref[b, rows, lanes] * sign


def pack(grads, signs, at):
    blocks = grads.reshape(PER_DEV, BLOCK, NY * LANES)
    return pl.pallas_call(
        pack_kernel,
        in_specs=[SCALARS, LOCAL, LOCAL],
        out_specs=LOCAL,
        out_shape=jax.ShapeDtypeStruct((NY, NZ, PER_DEV, CHUNK, LANES), jnp.bfloat16),
        compiler_params=pltpu.CompilerParams(vmem_limit_bytes=16 * MIB),
        name="pack",
    )(at, blocks, signs.reshape(PER_DEV, BLOCK))


def hadamard(parts):
    span = 1
    while span < len(parts):
        done = list(parts)
        for i in range(len(parts)):
            if not i & span:
                done[i] = parts[i] + parts[i + span]
                done[i + span] = parts[i] - parts[i + span]
        parts = done
        span *= 2
    return parts


def mix_kernel(at, picks_ref, raw_ref, kept_ref, given_ref, work):
    half = N_BLOCKS // 2

    @pl.loop(0, N_BLOCKS // 16, unroll=2)
    def _(d):
        base = d * 16
        parts = [raw_ref[base + b].astype(jnp.float32) for b in range(16)]
        for b, part in enumerate(hadamard(parts)):
            work[base + b] = part

    @pl.loop(0, 32, unroll=2)
    def _(i):
        base = lax.div(i, 16) * half + lax.rem(i, 16)
        parts = [work[base + 16 * e] for e in range(16)]
        for e, part in enumerate(hadamard(parts)):
            work[base + 16 * e] = part

    def sample(k):
        pick = picks_ref[k]
        low = lax.rem(pick, half)
        side = (1 - 2 * lax.div(pick, half)).astype(jnp.float32)
        return (work[low] + side * work[low + half]).astype(kept_ref.dtype)

    count = kept_ref.shape[0]

    @pl.loop(0, count, unroll=4)
    def _(k):
        kept_ref[k] = sample(at[1] * count + k)
        given_ref[k] = sample((1 - at[1]) * count + k)


def mix(at, raw, picks):
    part = jax.ShapeDtypeStruct((picks.shape[0] // NCORE, CHUNK, LANES), jnp.bfloat16)
    return pl.pallas_call(
        mix_kernel,
        in_specs=[SCALARS, SCALARS, LOCAL],
        out_specs=[LOCAL, LOCAL],
        scratch_shapes=[pltpu.VMEM((N_BLOCKS, CHUNK, LANES), jnp.float32)],
        out_shape=[part, part],
        compiler_params=pltpu.CompilerParams(vmem_limit_bytes=16 * MIB),
        name="mix",
    )(at, picks, raw)


NEAR = (0, 1, 3)


def near_kernel(*refs):
    cols, rows, (left, other_ref, own_ref) = refs[:3], (refs[0], refs[3], refs[4]), refs[5:]
    for which, out_ref in ((1, other_ref), (0, own_ref)):
        for j in range(len(NEAR)):
            left[which, pl.ds(j * LANES, LANES), :] = cols[j][which].T
        for j in range(len(NEAR)):
            pair = jnp.concatenate([rows[j][0], rows[j][1]], axis=1)
            block = jnp.dot(left[which], pair, preferred_element_type=jnp.float32)
            out_ref[j] = block.astype(out_ref.dtype)


def gram_near(sketch, x_up, x_down, y_up, y_down):
    depth, near = sketch.shape[1], len(NEAR)
    shape = (near, near * LANES, NCORE * LANES)
    flops = 2 * depth * NCORE * near * near * LANES * NCORE * LANES
    return pl.pallas_call(
        near_kernel,
        in_specs=[LOCAL] * 5,
        out_specs=[LOCAL] * 3,
        out_shape=[
            jax.ShapeDtypeStruct((NCORE, near * LANES, depth), jnp.bfloat16),
            jax.ShapeDtypeStruct(shape, jnp.bfloat16),
            jax.ShapeDtypeStruct(shape, jnp.float32),
        ],
        compiler_params=pltpu.CompilerParams(vmem_limit_bytes=16 * MIB),
        cost_estimate=pl.CostEstimate(flops=flops, bytes_accessed=8 * MIB, transcendentals=0),
        name="gram_near",
    )(sketch, y_up, y_down, x_up, x_down)


def far_kernel(which, at, near_ref, left, far_cols_0, far_cols_1, own, up, down, far_own, far_other, out_ref):
    x, core, turn = at[0], at[1], at[2]
    rows = (own, up, down)

    def put(step_x, step_y, block):
        panel = lax.rem(x + NX - step_x, NX) * NCORE
        quarter = pl.multiple_of(lax.rem(turn + step_y, NY) * LANES, LANES)
        block = block.astype(out_ref.dtype)
        out_ref[panel + core, pl.ds(quarter, LANES), :] = block[:, :LANES]
        out_ref[panel + 1 - core, pl.ds(quarter, LANES), :] = block[:, LANES:]

    last = (far_cols_1 if which else far_cols_0)[...].T
    pair = jnp.concatenate([far_own[...], far_other[...]], axis=1)
    block = jnp.dot(left[which], pair, preferred_element_type=jnp.float32)
    for j, step in enumerate(NEAR):
        put(2, step, block[j * LANES : (j + 1) * LANES])
    put(2, 2, jnp.dot(last, pair, preferred_element_type=jnp.float32))
    for i, step_x in enumerate(NEAR):
        pair = jnp.concatenate([rows[i][0], rows[i][1]], axis=1)
        put(step_x, 2, jnp.dot(last, pair, preferred_element_type=jnp.float32))
        for j, step_y in enumerate(NEAR):
            put(step_x, step_y, near_ref[i, pl.ds(j * LANES, LANES), :])


def gram_far(which, at, near, left, far_cols, rows):
    depth = far_cols[0].shape[0]
    flops = 2 * depth * 7 * LANES * NCORE * LANES
    return pl.pallas_call(
        functools.partial(far_kernel, which),
        in_specs=[SCALARS] + [LOCAL] * 9,
        out_specs=LOCAL,
        out_shape=jax.ShapeDtypeStruct((NX * NCORE, NY * LANES, LANES), near.dtype),
        compiler_params=pltpu.CompilerParams(vmem_limit_bytes=16 * MIB),
        cost_estimate=pl.CostEstimate(flops=flops, bytes_accessed=6 * MIB, transcendentals=0),
        name="gram_other" if which else "gram_own",
    )(at, near, left, *far_cols, *rows)


def finish_kernel(scale, parts_ref, out_ref):
    for i in range(out_ref.shape[1] // LANES):
        part = pl.ds(i * LANES, LANES)
        total = parts_ref[0, part].astype(jnp.float32)
        for k in range(1, parts_ref.shape[0]):
            total = total + parts_ref[k, part].astype(jnp.float32)
        out_ref[:, part] = (total * scale).T


def finish(parts, scale):
    count, width, rows = parts.shape
    return pl.pallas_call(
        lambda parts_ref, out_ref: finish_kernel(scale, parts_ref, out_ref),
        out_shape=jax.ShapeDtypeStruct((rows, width), jnp.float32),
        compiler_params=pltpu.CompilerParams(vmem_limit_bytes=16 * MIB),
        name="finish",
    )(parts)


def on_device(grads, signs, picks):
    dp, col = lax.axis_index("dp"), lax.axis_index("col")
    y, z = lax.div(dp, NZ), lax.rem(dp, NZ)
    x, core = lax.div(col, NCORE), lax.rem(col, NCORE)
    at = jnp.stack([x, core, lax.rem(z - y + x + NY, NY)])

    outgoing = pack(grads, signs, at).reshape(NY * NZ, PER_DEV, CHUNK, LANES)
    raw = lax.all_to_all(outgoing, "dp", split_axis=0, concat_axis=0, tiled=True)
    kept, given = mix(at, raw.reshape(N_BLOCKS, CHUNK, LANES), picks)

    def along_x(value, step):
        return lax.ppermute(value, "col", [(i, (i + NCORE * step) % (NX * NCORE)) for i in range(NX * NCORE)])

    def along_y(value, step):
        return lax.ppermute(value, "dp", [(i, (i + NZ * step) % (NY * NZ)) for i in range(NY * NZ)])

    def swap(value):
        return lax.ppermute(value, "col", [(i, i ^ 1) for i in range(NX * NCORE)])

    sketch = jnp.stack([kept, swap(given)]).reshape(NCORE, -1, LANES)
    x_up, x_down = along_x(sketch, 1), along_x(sketch, -1)
    y_up, y_down = along_y(sketch, 1), along_y(sketch, -1)
    x_far = (along_x(x_up[0], 1), along_x(x_down[1], -1))
    y_far = (along_y(y_up[0], 1), along_y(y_down[1], -1))
    left, near_other, near_own = gram_near(sketch, x_up, x_down, y_up, y_down)
    rows = (sketch, x_up, x_down, *x_far)
    away = swap(gram_far(1, at, near_other, left, y_far, rows))
    partial = gram_far(0, at, near_own, left, y_far, rows)
    partial = (partial + away.astype(jnp.float32)).astype(jnp.bfloat16)

    groups = [
        [gy * NZ + (s + gy) % NY + NY * half for gy in range(NY) for half in range(NZ // NY)]
        for s in range(NY)
    ]
    parts = lax.all_to_all(
        partial, "dp", split_axis=0, concat_axis=0, axis_index_groups=groups, tiled=True
    )
    total_rows = grads.shape[0] * NY * NZ
    scale = BLOCK / (total_rows * picks.shape[0] * BLOCK)
    return finish(parts, scale)


def solution(mesh):
    placed = (P("dp", "col"), P("dp"), P())
    return jax.shard_map(
        on_device, mesh=mesh, in_specs=placed, out_specs=P("dp", "col"), check_vma=False
    )
```

```python
import functools

import jax
import jax.numpy as jnp
from jax import lax
from jax.experimental import pallas as pl
from jax.experimental.pallas import tpu as pltpu
from jax.sharding import PartitionSpec as P

NY, NZ, NX, NCORE = 4, 8, 4, 2
BLOCK = 128
LANES = 128
PER_DEV = 16
N_BLOCKS = 512
CHUNK = BLOCK // NZ
MIB = 1 << 20


SCALARS = pl.BlockSpec(memory_space=pltpu.SMEM)
LOCAL = pl.BlockSpec(memory_space=pltpu.VMEM)


def pack_kernel(at, grads_ref, signs_ref, out_ref):
    columns = signs_ref[...].astype(jnp.float32).T
    for z in range(NZ):
        for y in range(NY):
            quarter = lax.rem(z - y + at[0] + NY, NY)
            lanes = pl.ds(pl.multiple_of(quarter * LANES, LANES), LANES)
            for b in range(PER_DEV):
                sign = columns[z * CHUNK : (z + 1) * CHUNK, b : b + 1]
                sign = jnp.broadcast_to(sign, (CHUNK, LANES)).astype(jnp.bfloat16)
                rows = pl.ds(z * CHUNK, CHUNK)
                out_ref[y, z, b] = grads_ref[b, rows, lanes] * sign


def pack(grads, signs, at):
    blocks = grads.reshape(PER_DEV, BLOCK, NY * LANES)
    return pl.pallas_call(
        pack_kernel,
        in_specs=[SCALARS, LOCAL, LOCAL],
        out_specs=LOCAL,
        out_shape=jax.ShapeDtypeStruct((NY, NZ, PER_DEV, CHUNK, LANES), jnp.bfloat16),
        compiler_params=pltpu.CompilerParams(vmem_limit_bytes=16 * MIB),
        name="pack",
    )(at, blocks, signs.reshape(PER_DEV, BLOCK))


def hadamard(parts):
    span = 1
    while span < len(parts):
        done = list(parts)
        for i in range(len(parts)):
            if not i & span:
                done[i] = parts[i] + parts[i + span]
                done[i + span] = parts[i] - parts[i + span]
        parts = done
        span *= 2
    return parts


def mix_kernel(picks_ref, raw_ref, out_ref, work):
    half = N_BLOCKS // 2

    @pl.loop(0, N_BLOCKS // 16, unroll=2)
    def _(d):
        base = d * 16
        parts = [raw_ref[base + b].astype(jnp.float32) for b in range(16)]
        for b, part in enumerate(hadamard(parts)):
            work[base + b] = part

    @pl.loop(0, 32, unroll=2)
    def _(i):
        base = lax.div(i, 16) * half + lax.rem(i, 16)
        parts = [work[base + 16 * e] for e in range(16)]
        for e, part in enumerate(hadamard(parts)):
            work[base + 16 * e] = part

    @pl.loop(0, out_ref.shape[0], unroll=4)
    def _(k):
        pick = picks_ref[k]
        low = lax.rem(pick, half)
        side = (1 - 2 * lax.div(pick, half)).astype(jnp.float32)
        out_ref[k] = (work[low] + side * work[low + half]).astype(out_ref.dtype)


def mix(raw, picks):
    return pl.pallas_call(
        mix_kernel,
        in_specs=[SCALARS, LOCAL],
        out_specs=LOCAL,
        scratch_shapes=[pltpu.VMEM((N_BLOCKS, CHUNK, LANES), jnp.float32)],
        out_shape=jax.ShapeDtypeStruct((picks.shape[0], CHUNK, LANES), jnp.bfloat16),
        compiler_params=pltpu.CompilerParams(vmem_limit_bytes=16 * MIB),
        name="mix",
    )(picks, raw)


NEAR = (0, 1, 3)


def halves_kernel(*refs):
    pieces, outs = refs[:4], refs[4:]
    depth = outs[0].shape[0]
    for i, out in enumerate(outs):
        out[...] = pieces[i][pl.ds(i % 2 * depth, depth), :]


def halves(*pieces):
    part = jax.ShapeDtypeStruct((pieces[0].shape[0] // 2, LANES), pieces[0].dtype)
    return pl.pallas_call(
        halves_kernel,
        in_specs=[LOCAL] * 4,
        out_specs=[LOCAL] * 4,
        out_shape=[part] * 4,
        compiler_params=pltpu.CompilerParams(vmem_limit_bytes=16 * MIB),
        cost_estimate=pl.CostEstimate(flops=0, bytes_accessed=2 * MIB, transcendentals=0),
        name="halves",
    )(*pieces)


def pair_dot(left, own, other):
    return jnp.dot(left, jnp.concatenate([own, other], axis=1), preferred_element_type=jnp.float32)


def near_kernel(*refs):
    cols, own, other, (left, out_ref) = refs[:3], refs[3:6], refs[6:9], refs[9:]
    for j in range(len(NEAR)):
        left[pl.ds(j * LANES, LANES), :] = cols[j][...].T
    for j in range(len(NEAR)):
        out_ref[j] = pair_dot(left[...], own[j][...], other[j][...]).astype(out_ref.dtype)


def cost(depth, blocks):
    flops = 2 * depth * blocks * LANES * NCORE * LANES
    return pl.CostEstimate(flops=flops, bytes_accessed=8 * MIB, transcendentals=0)


def gram_near(cols, own, other):
    depth, near = cols[0].shape[0], len(NEAR)
    return pl.pallas_call(
        near_kernel,
        in_specs=[LOCAL] * 9,
        out_specs=[LOCAL] * 2,
        out_shape=[
            jax.ShapeDtypeStruct((near * LANES, depth), jnp.bfloat16),
            jax.ShapeDtypeStruct((near, near * LANES, NCORE * LANES), jnp.bfloat16),
        ],
        compiler_params=pltpu.CompilerParams(vmem_limit_bytes=16 * MIB),
        cost_estimate=cost(depth, near * near),
        name="gram_near",
    )(*cols, *own, *other)


def side_kernel(*refs):
    col, own, other, (last, out_ref) = refs[0], refs[1:4], refs[4:7], refs[7:]
    last[...] = col[...].T
    for j in range(len(NEAR)):
        out_ref[j] = pair_dot(last[...], own[j][...], other[j][...]).astype(out_ref.dtype)


def gram_side(col, own, other):
    depth, near = col.shape[0], len(NEAR)
    return pl.pallas_call(
        side_kernel,
        in_specs=[LOCAL] * 7,
        out_specs=[LOCAL] * 2,
        out_shape=[
            jax.ShapeDtypeStruct((LANES, depth), jnp.bfloat16),
            jax.ShapeDtypeStruct((near, LANES, NCORE * LANES), jnp.bfloat16),
        ],
        compiler_params=pltpu.CompilerParams(vmem_limit_bytes=16 * MIB),
        cost_estimate=cost(depth, near),
        name="gram_side",
    )(col, *own, *other)


def far_kernel(at, near_ref, side_ref, left, last, own, other, out_ref):
    x, core, turn = at[0], at[1], at[2]

    def put(step_x, step_y, block):
        panel = lax.rem(x + NX - step_x, NX) * NCORE
        quarter = pl.multiple_of(lax.rem(turn + step_y, NY) * LANES, LANES)
        out_ref[panel + core, pl.ds(quarter, LANES), :] = block[:, :LANES]
        out_ref[panel + 1 - core, pl.ds(quarter, LANES), :] = block[:, LANES:]

    block = pair_dot(left[...], own[...], other[...]).astype(out_ref.dtype)
    for j, step in enumerate(NEAR):
        put(2, step, block[j * LANES : (j + 1) * LANES])
    put(2, 2, pair_dot(last[...], own[...], other[...]).astype(out_ref.dtype))
    for i, step_x in enumerate(NEAR):
        put(step_x, 2, side_ref[i])
        for j, step_y in enumerate(NEAR):
            put(step_x, step_y, near_ref[i, pl.ds(j * LANES, LANES), :])


def gram_far(at, near, side, left, last, own, other):
    return pl.pallas_call(
        far_kernel,
        in_specs=[SCALARS] + [LOCAL] * 6,
        out_specs=LOCAL,
        out_shape=jax.ShapeDtypeStruct((NX * NCORE, NY * LANES, LANES), near.dtype),
        compiler_params=pltpu.CompilerParams(vmem_limit_bytes=16 * MIB),
        cost_estimate=cost(own.shape[0], NY),
        name="gram_far",
    )(at, near, side, left, last, own, other)


def finish_kernel(scale, parts_ref, out_ref):
    for i in range(out_ref.shape[1] // LANES):
        part = pl.ds(i * LANES, LANES)
        total = parts_ref[0, part].astype(jnp.float32)
        for k in range(1, parts_ref.shape[0]):
            total = total + parts_ref[k, part].astype(jnp.float32)
        out_ref[:, part] = (total * scale).T


def finish(parts, scale):
    count, width, rows = parts.shape
    return pl.pallas_call(
        lambda parts_ref, out_ref: finish_kernel(scale, parts_ref, out_ref),
        out_shape=jax.ShapeDtypeStruct((rows, width), jnp.float32),
        compiler_params=pltpu.CompilerParams(vmem_limit_bytes=16 * MIB),
        name="finish",
    )(parts)


def on_device(grads, signs, picks):
    dp, col = lax.axis_index("dp"), lax.axis_index("col")
    y, z = lax.div(dp, NZ), lax.rem(dp, NZ)
    x, core = lax.div(col, NCORE), lax.rem(col, NCORE)
    at = jnp.stack([x, core, lax.rem(z - y + x + NY, NY)])

    outgoing = pack(grads, signs, at).reshape(NY * NZ, PER_DEV, CHUNK, LANES)
    raw = lax.all_to_all(outgoing, "dp", split_axis=0, concat_axis=0, tiled=True)
    sketch = mix(raw.reshape(N_BLOCKS, CHUNK, LANES), picks).reshape(-1, LANES)

    def along_x(value, step):
        return lax.ppermute(value, "col", [(i, (i + NCORE * step) % (NX * NCORE)) for i in range(NX * NCORE)])

    def along_y(value, step):
        return lax.ppermute(value, "dp", [(i, (i + NZ * step) % (NY * NZ)) for i in range(NY * NZ)])

    def swap(value):
        return lax.ppermute(value, "col", [(i, i ^ 1) for i in range(NX * NCORE)])

    x_up, x_down = along_x(sketch, 1), along_x(sketch, -1)
    y_up, y_down = along_y(sketch, 1), along_y(sketch, -1)
    x_low, x_high, y_low, y_high = halves(x_up, x_down, y_up, y_down)
    x_far = jnp.concatenate([along_x(x_low, 1), along_x(x_high, -1)])
    y_far = jnp.concatenate([along_y(y_low, 1), along_y(y_high, -1)])
    own = (sketch, x_up, x_down)
    other = tuple(swap(piece) for piece in own)
    left, near = gram_near((sketch, y_up, y_down), own, other)
    last, side = gram_side(y_far, own, other)
    partial = gram_far(at, near, side, left, last, x_far, swap(x_far))

    groups = [
        [gy * NZ + (s + gy) % NY + NY * half for gy in range(NY) for half in range(NZ // NY)]
        for s in range(NY)
    ]
    parts = lax.all_to_all(
        partial, "dp", split_axis=0, concat_axis=0, axis_index_groups=groups, tiled=True
    )
    total_rows = grads.shape[0] * NY * NZ
    scale = BLOCK / (total_rows * picks.shape[0] * BLOCK)
    return finish(parts, scale)


def solution(mesh):
    placed = (P("dp", "col"), P("dp"), P())
    return jax.shard_map(
        on_device, mesh=mesh, in_specs=placed, out_specs=P("dp", "col"), check_vma=False
    )
```

```python
import functools

import jax
import jax.numpy as jnp
from jax import lax
from jax.experimental import pallas as pl
from jax.experimental.pallas import tpu as pltpu
from jax.sharding import PartitionSpec as P

NY, NZ, NX, NCORE = 4, 8, 4, 2
BLOCK = 128
LANES = 128
PER_DEV = 16
N_BLOCKS = 512
CHUNK = BLOCK // NZ
MIB = 1 << 20


SCALARS = pl.BlockSpec(memory_space=pltpu.SMEM)
LOCAL = pl.BlockSpec(memory_space=pltpu.VMEM)


def pack_kernel(at, grads_ref, signs_ref, out_ref):
    columns = signs_ref[...].astype(jnp.float32).T
    for z in range(NZ):
        for y in range(NY):
            quarter = lax.rem(z - y + at[0] + NY, NY)
            lanes = pl.ds(pl.multiple_of(quarter * LANES, LANES), LANES)
            for b in range(PER_DEV):
                sign = columns[z * CHUNK : (z + 1) * CHUNK, b : b + 1]
                sign = jnp.broadcast_to(sign, (CHUNK, LANES)).astype(jnp.bfloat16)
                rows = pl.ds(z * CHUNK, CHUNK)
                out_ref[y, z, b] = grads_ref[b, rows, lanes] * sign


def pack(grads, signs, at):
    blocks = grads.reshape(PER_DEV, BLOCK, NY * LANES)
    return pl.pallas_call(
        pack_kernel,
        in_specs=[SCALARS, LOCAL, LOCAL],
        out_specs=LOCAL,
        out_shape=jax.ShapeDtypeStruct((NY, NZ, PER_DEV, CHUNK, LANES), jnp.bfloat16),
        compiler_params=pltpu.CompilerParams(vmem_limit_bytes=16 * MIB),
        name="pack",
    )(at, blocks, signs.reshape(PER_DEV, BLOCK))


def hadamard(parts):
    span = 1
    while span < len(parts):
        done = list(parts)
        for i in range(len(parts)):
            if not i & span:
                done[i] = parts[i] + parts[i + span]
                done[i + span] = parts[i] - parts[i + span]
        parts = done
        span *= 2
    return parts


def mix_kernel(picks_ref, raw_ref, out_ref, work):
    half = N_BLOCKS // 2

    @pl.loop(0, N_BLOCKS // 16, unroll=2)
    def _(d):
        base = d * 16
        parts = [raw_ref[base + b].astype(jnp.float32) for b in range(16)]
        for b, part in enumerate(hadamard(parts)):
            work[base + b] = part

    @pl.loop(0, 32, unroll=2)
    def _(i):
        base = lax.div(i, 16) * half + lax.rem(i, 16)
        parts = [work[base + 16 * e] for e in range(16)]
        for e, part in enumerate(hadamard(parts)):
            work[base + 16 * e] = part

    @pl.loop(0, out_ref.shape[0], unroll=4)
    def _(k):
        pick = picks_ref[k]
        low = lax.rem(pick, half)
        side = (1 - 2 * lax.div(pick, half)).astype(jnp.float32)
        out_ref[k] = (work[low] + side * work[low + half]).astype(out_ref.dtype)


def mix(raw, picks):
    return pl.pallas_call(
        mix_kernel,
        in_specs=[SCALARS, LOCAL],
        out_specs=LOCAL,
        scratch_shapes=[pltpu.VMEM((N_BLOCKS, CHUNK, LANES), jnp.float32)],
        out_shape=jax.ShapeDtypeStruct((picks.shape[0], CHUNK, LANES), jnp.bfloat16),
        compiler_params=pltpu.CompilerParams(vmem_limit_bytes=16 * MIB),
        name="mix",
    )(picks, raw)


NEAR = (0, 1, 3)


def after_kernel(value_ref, *refs):
    refs[-1][...] = value_ref[...]


def after(value, *others):
    return pl.pallas_call(
        after_kernel,
        in_specs=[LOCAL] * (1 + len(others)),
        out_specs=LOCAL,
        out_shape=jax.ShapeDtypeStruct(value.shape, value.dtype),
        compiler_params=pltpu.CompilerParams(vmem_limit_bytes=16 * MIB),
        cost_estimate=pl.CostEstimate(flops=0, bytes_accessed=MIB, transcendentals=0),
        name="after",
    )(value, *others)


def pair_dot(left, own, other):
    return jnp.dot(left, jnp.concatenate([own, other], axis=1), preferred_element_type=jnp.float32)


def near_kernel(*refs):
    cols, own, other, (left, out_ref) = refs[:3], refs[3:6], refs[6:9], refs[9:]
    for j in range(len(NEAR)):
        left[pl.ds(j * LANES, LANES), :] = cols[j][...].T
    for j in range(len(NEAR)):
        out_ref[j] = pair_dot(left[...], own[j][...], other[j][...]).astype(out_ref.dtype)


def cost(depth, blocks):
    flops = 2 * depth * blocks * LANES * NCORE * LANES
    return pl.CostEstimate(flops=flops, bytes_accessed=8 * MIB, transcendentals=0)


def gram_near(cols, own, other):
    depth, near = cols[0].shape[0], len(NEAR)
    return pl.pallas_call(
        near_kernel,
        in_specs=[LOCAL] * 9,
        out_specs=[LOCAL] * 2,
        out_shape=[
            jax.ShapeDtypeStruct((near * LANES, depth), jnp.bfloat16),
            jax.ShapeDtypeStruct((near, near * LANES, NCORE * LANES), jnp.bfloat16),
        ],
        compiler_params=pltpu.CompilerParams(vmem_limit_bytes=16 * MIB),
        cost_estimate=cost(depth, near * near),
        name="gram_near",
    )(*cols, *own, *other)


def side_kernel(*refs):
    other, own, col, (last, out_ref) = refs[:3], refs[3:6], refs[6], refs[7:]
    last[...] = col[...].T
    for j in range(len(NEAR)):
        out_ref[j] = pair_dot(last[...], own[j][...], other[j][...]).astype(out_ref.dtype)


def gram_side(col, own, other):
    depth, near = col.shape[0], len(NEAR)
    return pl.pallas_call(
        side_kernel,
        in_specs=[LOCAL] * 7,
        out_specs=[LOCAL] * 2,
        out_shape=[
            jax.ShapeDtypeStruct((LANES, depth), jnp.bfloat16),
            jax.ShapeDtypeStruct((near, LANES, NCORE * LANES), jnp.bfloat16),
        ],
        compiler_params=pltpu.CompilerParams(vmem_limit_bytes=16 * MIB),
        cost_estimate=cost(depth, near),
        name="gram_side",
    )(*other, *own, col)


def far_kernel(at, last, side_ref, left, near_ref, own, other, out_ref):
    x, core, turn = at[0], at[1], at[2]

    def put(step_x, step_y, block):
        panel = lax.rem(x + NX - step_x, NX) * NCORE
        quarter = pl.multiple_of(lax.rem(turn + step_y, NY) * LANES, LANES)
        out_ref[panel + core, pl.ds(quarter, LANES), :] = block[:, :LANES]
        out_ref[panel + 1 - core, pl.ds(quarter, LANES), :] = block[:, LANES:]

    block = pair_dot(left[...], own[...], other[...]).astype(out_ref.dtype)
    for j, step in enumerate(NEAR):
        put(2, step, block[j * LANES : (j + 1) * LANES])
    put(2, 2, pair_dot(last[...], own[...], other[...]).astype(out_ref.dtype))
    for i, step_x in enumerate(NEAR):
        put(step_x, 2, side_ref[i])
        for j, step_y in enumerate(NEAR):
            put(step_x, step_y, near_ref[i, pl.ds(j * LANES, LANES), :])


def gram_far(at, last, side, left, near, own, other):
    return pl.pallas_call(
        far_kernel,
        in_specs=[SCALARS] + [LOCAL] * 6,
        out_specs=LOCAL,
        out_shape=jax.ShapeDtypeStruct((NX * NCORE, NY * LANES, LANES), near.dtype),
        compiler_params=pltpu.CompilerParams(vmem_limit_bytes=16 * MIB),
        cost_estimate=cost(own.shape[0], NY),
        name="gram_far",
    )(at, last, side, left, near, own, other)


def finish_kernel(scale, parts_ref, out_ref):
    for i in range(out_ref.shape[1] // LANES):
        part = pl.ds(i * LANES, LANES)
        total = parts_ref[0, part].astype(jnp.float32)
        for k in range(1, parts_ref.shape[0]):
            total = total + parts_ref[k, part].astype(jnp.float32)
        out_ref[:, part] = (total * scale).T


def finish(parts, scale):
    count, width, rows = parts.shape
    return pl.pallas_call(
        lambda parts_ref, out_ref: finish_kernel(scale, parts_ref, out_ref),
        out_shape=jax.ShapeDtypeStruct((rows, width), jnp.float32),
        compiler_params=pltpu.CompilerParams(vmem_limit_bytes=16 * MIB),
        name="finish",
    )(parts)


def on_device(grads, signs, picks):
    dp, col = lax.axis_index("dp"), lax.axis_index("col")
    y, z = lax.div(dp, NZ), lax.rem(dp, NZ)
    x, core = lax.div(col, NCORE), lax.rem(col, NCORE)
    at = jnp.stack([x, core, lax.rem(z - y + x + NY, NY)])

    outgoing = pack(grads, signs, at).reshape(NY * NZ, PER_DEV, CHUNK, LANES)
    raw = lax.all_to_all(outgoing, "dp", split_axis=0, concat_axis=0, tiled=True)
    sketch = mix(raw.reshape(N_BLOCKS, CHUNK, LANES), picks).reshape(-1, LANES)

    def along_x(value, step):
        return lax.ppermute(value, "col", [(i, (i + NCORE * step) % (NX * NCORE)) for i in range(NX * NCORE)])

    def along_y(value, step):
        return lax.ppermute(value, "dp", [(i, (i + NZ * step) % (NY * NZ)) for i in range(NY * NZ)])

    def swap(value):
        return lax.ppermute(value, "col", [(i, i ^ 1) for i in range(NX * NCORE)])

    x_up, x_down = along_x(sketch, 1), along_x(sketch, -1)
    y_up, y_down = along_y(sketch, 1), along_y(sketch, -1)
    x_far, y_far = along_x(sketch, 2), along_y(sketch, 2)
    own = (sketch, x_up, x_down)
    gate = after(sketch, y_up, y_down, x_up, x_down)
    other = (swap(gate), swap(after(x_up, gate)), swap(after(x_down, gate)))
    last, side = gram_side(y_far, own, other)
    left, near = gram_near((sketch, y_up, y_down), own, other)
    partial = gram_far(at, last, side, left, near, x_far, swap(x_far))

    groups = [
        [gy * NZ + (s + gy) % NY + NY * half for gy in range(NY) for half in range(NZ // NY)]
        for s in range(NY)
    ]
    parts = lax.all_to_all(
        partial, "dp", split_axis=0, concat_axis=0, axis_index_groups=groups, tiled=True
    )
    total_rows = grads.shape[0] * NY * NZ
    scale = BLOCK / (total_rows * picks.shape[0] * BLOCK)
    return finish(parts, scale)


def solution(mesh):
    placed = (P("dp", "col"), P("dp"), P())
    return jax.shard_map(
        on_device, mesh=mesh, in_specs=placed, out_specs=P("dp", "col"), check_vma=False
    )
```

```python
import functools

import jax
import jax.numpy as jnp
from jax import lax
from jax.experimental import pallas as pl
from jax.experimental.pallas import tpu as pltpu
from jax.sharding import PartitionSpec as P

NY, NZ, NX, NCORE = 4, 8, 4, 2
BLOCK = 128
LANES = 128
PER_DEV = 16
N_BLOCKS = 512
CHUNK = BLOCK // NZ
MIB = 1 << 20


SCALARS = pl.BlockSpec(memory_space=pltpu.SMEM)
LOCAL = pl.BlockSpec(memory_space=pltpu.VMEM)


def pack_kernel(at, grads_ref, signs_ref, out_ref):
    columns = signs_ref[...].astype(jnp.float32).T
    for z in range(NZ):
        for y in range(NY):
            quarter = lax.rem(z - y + at[0] + NY, NY)
            lanes = pl.ds(pl.multiple_of(quarter * LANES, LANES), LANES)
            for b in range(PER_DEV):
                sign = columns[z * CHUNK : (z + 1) * CHUNK, b : b + 1]
                sign = jnp.broadcast_to(sign, (CHUNK, LANES)).astype(jnp.bfloat16)
                rows = pl.ds(z * CHUNK, CHUNK)
                out_ref[y, z, b] = grads_ref[b, rows, lanes] * sign


def pack(grads, signs, at):
    blocks = grads.reshape(PER_DEV, BLOCK, NY * LANES)
    return pl.pallas_call(
        pack_kernel,
        in_specs=[SCALARS, LOCAL, LOCAL],
        out_specs=LOCAL,
        out_shape=jax.ShapeDtypeStruct((NY, NZ, PER_DEV, CHUNK, LANES), jnp.bfloat16),
        compiler_params=pltpu.CompilerParams(vmem_limit_bytes=16 * MIB),
        name="pack",
    )(at, blocks, signs.reshape(PER_DEV, BLOCK))


def hadamard(parts):
    span = 1
    while span < len(parts):
        done = list(parts)
        for i in range(len(parts)):
            if not i & span:
                done[i] = parts[i] + parts[i + span]
                done[i + span] = parts[i] - parts[i + span]
        parts = done
        span *= 2
    return parts


def mix_kernel(picks_ref, raw_ref, out_ref, work):
    half = N_BLOCKS // 2

    @pl.loop(0, N_BLOCKS // 16, unroll=2)
    def _(d):
        base = d * 16
        parts = [raw_ref[base + b].astype(jnp.float32) for b in range(16)]
        for b, part in enumerate(hadamard(parts)):
            work[base + b] = part

    @pl.loop(0, 32, unroll=2)
    def _(i):
        base = lax.div(i, 16) * half + lax.rem(i, 16)
        parts = [work[base + 16 * e] for e in range(16)]
        for e, part in enumerate(hadamard(parts)):
            work[base + 16 * e] = part

    @pl.loop(0, out_ref.shape[0], unroll=4)
    def _(k):
        pick = picks_ref[k]
        low = lax.rem(pick, half)
        side = (1 - 2 * lax.div(pick, half)).astype(jnp.float32)
        out_ref[k] = (work[low] + side * work[low + half]).astype(out_ref.dtype)


def mix(raw, picks):
    return pl.pallas_call(
        mix_kernel,
        in_specs=[SCALARS, LOCAL],
        out_specs=LOCAL,
        scratch_shapes=[pltpu.VMEM((N_BLOCKS, CHUNK, LANES), jnp.float32)],
        out_shape=jax.ShapeDtypeStruct((picks.shape[0], CHUNK, LANES), jnp.bfloat16),
        compiler_params=pltpu.CompilerParams(vmem_limit_bytes=16 * MIB),
        name="mix",
    )(picks, raw)


NEAR = (0, 1, 3)


def share_kernel(own, x_up, x_down, y_up, y_down, joined, *halves):
    for j, piece in enumerate((own, x_up, x_down)):
        joined[j] = piece[...]
    half = halves[0].shape[0]
    for i, piece in enumerate((x_up, x_down, y_up, y_down)):
        halves[i][...] = piece[pl.ds(i % 2 * half, half), :]


def share(own, x_up, x_down, y_up, y_down):
    rows, width = own.shape
    half = jax.ShapeDtypeStruct((rows // 2, width), own.dtype)
    return pl.pallas_call(
        share_kernel,
        in_specs=[LOCAL] * 5,
        out_specs=[LOCAL] * 5,
        out_shape=[jax.ShapeDtypeStruct((len(NEAR), rows, width), own.dtype)] + [half] * 4,
        compiler_params=pltpu.CompilerParams(vmem_limit_bytes=16 * MIB),
        cost_estimate=pl.CostEstimate(flops=0, bytes_accessed=2 * MIB, transcendentals=0),
        name="share",
    )(own, x_up, x_down, y_up, y_down)


def pair_dot(left, own, other):
    return jnp.dot(left, jnp.concatenate([own, other], axis=1), preferred_element_type=jnp.float32)


def near_kernel(*refs):
    cols, own, (other, left, out_ref) = refs[:3], refs[3:6], refs[6:]
    for j in range(len(NEAR)):
        left[pl.ds(j * LANES, LANES), :] = cols[j][...].T
    for j in range(len(NEAR)):
        out_ref[j] = pair_dot(left[...], own[j][...], other[j]).astype(out_ref.dtype)


def cost(depth, blocks):
    flops = 2 * depth * blocks * LANES * NCORE * LANES
    return pl.CostEstimate(flops=flops, bytes_accessed=8 * MIB, transcendentals=0)


def gram_near(cols, own, other):
    depth, near = cols[0].shape[0], len(NEAR)
    return pl.pallas_call(
        near_kernel,
        in_specs=[LOCAL] * 7,
        out_specs=[LOCAL] * 2,
        out_shape=[
            jax.ShapeDtypeStruct((near * LANES, depth), jnp.bfloat16),
            jax.ShapeDtypeStruct((near, near * LANES, NCORE * LANES), jnp.bfloat16),
        ],
        compiler_params=pltpu.CompilerParams(vmem_limit_bytes=16 * MIB),
        cost_estimate=cost(depth, near * near),
        name="gram_near",
    )(*cols, *own, other)


def side_kernel(*refs):
    other, own, (col, last, out_ref) = refs[0], refs[1:4], refs[4:]
    last[...] = col[...].T
    for j in range(len(NEAR)):
        out_ref[j] = pair_dot(last[...], own[j][...], other[j]).astype(out_ref.dtype)


def gram_side(col, own, other):
    depth, near = col.shape[0], len(NEAR)
    return pl.pallas_call(
        side_kernel,
        in_specs=[LOCAL] * 5,
        out_specs=[LOCAL] * 2,
        out_shape=[
            jax.ShapeDtypeStruct((LANES, depth), jnp.bfloat16),
            jax.ShapeDtypeStruct((near, LANES, NCORE * LANES), jnp.bfloat16),
        ],
        compiler_params=pltpu.CompilerParams(vmem_limit_bytes=16 * MIB),
        cost_estimate=cost(depth, near),
        name="gram_side",
    )(other, *own, col)


def far_kernel(at, last, side_ref, left, near_ref, own, other, out_ref):
    x, core, turn = at[0], at[1], at[2]

    def put(step_x, step_y, block):
        panel = lax.rem(x + NX - step_x, NX) * NCORE
        quarter = pl.multiple_of(lax.rem(turn + step_y, NY) * LANES, LANES)
        out_ref[panel + core, pl.ds(quarter, LANES), :] = block[:, :LANES]
        out_ref[panel + 1 - core, pl.ds(quarter, LANES), :] = block[:, LANES:]

    block = pair_dot(left[...], own[...], other[...]).astype(out_ref.dtype)
    for j, step in enumerate(NEAR):
        put(2, step, block[j * LANES : (j + 1) * LANES])
    put(2, 2, pair_dot(last[...], own[...], other[...]).astype(out_ref.dtype))
    for i, step_x in enumerate(NEAR):
        put(step_x, 2, side_ref[i])
        for j, step_y in enumerate(NEAR):
            put(step_x, step_y, near_ref[i, pl.ds(j * LANES, LANES), :])


def gram_far(at, last, side, left, near, own, other):
    return pl.pallas_call(
        far_kernel,
        in_specs=[SCALARS] + [LOCAL] * 6,
        out_specs=LOCAL,
        out_shape=jax.ShapeDtypeStruct((NX * NCORE, NY * LANES, LANES), near.dtype),
        compiler_params=pltpu.CompilerParams(vmem_limit_bytes=16 * MIB),
        cost_estimate=cost(own.shape[0], NY),
        name="gram_far",
    )(at, last, side, left, near, own, other)


def finish_kernel(scale, parts_ref, out_ref):
    for i in range(out_ref.shape[1] // LANES):
        part = pl.ds(i * LANES, LANES)
        total = parts_ref[0, part].astype(jnp.float32)
        for k in range(1, parts_ref.shape[0]):
            total = total + parts_ref[k, part].astype(jnp.float32)
        out_ref[:, part] = (total * scale).T


def finish(parts, scale):
    count, width, rows = parts.shape
    return pl.pallas_call(
        lambda parts_ref, out_ref: finish_kernel(scale, parts_ref, out_ref),
        out_shape=jax.ShapeDtypeStruct((rows, width), jnp.float32),
        compiler_params=pltpu.CompilerParams(vmem_limit_bytes=16 * MIB),
        name="finish",
    )(parts)


def on_device(grads, signs, picks):
    dp, col = lax.axis_index("dp"), lax.axis_index("col")
    y, z = lax.div(dp, NZ), lax.rem(dp, NZ)
    x, core = lax.div(col, NCORE), lax.rem(col, NCORE)
    at = jnp.stack([x, core, lax.rem(z - y + x + NY, NY)])

    outgoing = pack(grads, signs, at).reshape(NY * NZ, PER_DEV, CHUNK, LANES)
    raw = lax.all_to_all(outgoing, "dp", split_axis=0, concat_axis=0, tiled=True)
    sketch = mix(raw.reshape(N_BLOCKS, CHUNK, LANES), picks).reshape(-1, LANES)

    def along_x(value, step):
        return lax.ppermute(value, "col", [(i, (i + NCORE * step) % (NX * NCORE)) for i in range(NX * NCORE)])

    def along_y(value, step):
        return lax.ppermute(value, "dp", [(i, (i + NZ * step) % (NY * NZ)) for i in range(NY * NZ)])

    def swap(value):
        return lax.ppermute(value, "col", [(i, i ^ 1) for i in range(NX * NCORE)])

    x_up, x_down = along_x(sketch, 1), along_x(sketch, -1)
    y_up, y_down = along_y(sketch, 1), along_y(sketch, -1)
    joined, x_low, x_high, y_low, y_high = share(sketch, x_up, x_down, y_up, y_down)
    x_far = jnp.concatenate([along_x(x_low, 1), along_x(x_high, -1)])
    y_far = jnp.concatenate([along_y(y_low, 1), along_y(y_high, -1)])
    own, other = (sketch, x_up, x_down), swap(joined)
    last, side = gram_side(y_far, own, other)
    left, near = gram_near((sketch, y_up, y_down), own, other)
    partial = gram_far(at, last, side, left, near, x_far, swap(x_far))

    groups = [
        [gy * NZ + (s + gy) % NY + NY * half for gy in range(NY) for half in range(NZ // NY)]
        for s in range(NY)
    ]
    parts = lax.all_to_all(
        partial, "dp", split_axis=0, concat_axis=0, axis_index_groups=groups, tiled=True
    )
    total_rows = grads.shape[0] * NY * NZ
    scale = BLOCK / (total_rows * picks.shape[0] * BLOCK)
    return finish(parts, scale)


def solution(mesh):
    placed = (P("dp", "col"), P("dp"), P())
    return jax.shard_map(
        on_device, mesh=mesh, in_specs=placed, out_specs=P("dp", "col"), check_vma=False
    )
```

```python
import functools

import jax
import jax.numpy as jnp
from jax import lax
from jax.experimental import pallas as pl
from jax.experimental.pallas import tpu as pltpu
from jax.sharding import PartitionSpec as P

NY, NZ, NX, NCORE = 4, 8, 4, 2
BLOCK = 128
LANES = 128
PER_DEV = 16
N_BLOCKS = 512
CHUNK = BLOCK // NZ
MIB = 1 << 20


SCALARS = pl.BlockSpec(memory_space=pltpu.SMEM)
LOCAL = pl.BlockSpec(memory_space=pltpu.VMEM)


def pack_kernel(at, grads_ref, signs_ref, out_ref):
    columns = signs_ref[...].astype(jnp.float32).T
    for z in range(NZ):
        for y in range(NY):
            quarter = lax.rem(z - y + at[0] + NY, NY)
            lanes = pl.ds(pl.multiple_of(quarter * LANES, LANES), LANES)
            for b in range(PER_DEV):
                sign = columns[z * CHUNK : (z + 1) * CHUNK, b : b + 1]
                sign = jnp.broadcast_to(sign, (CHUNK, LANES)).astype(jnp.bfloat16)
                rows = pl.ds(z * CHUNK, CHUNK)
                out_ref[y, z, b] = grads_ref[b, rows, lanes] * sign


def pack(grads, signs, at):
    blocks = grads.reshape(PER_DEV, BLOCK, NY * LANES)
    return pl.pallas_call(
        pack_kernel,
        in_specs=[SCALARS, LOCAL, LOCAL],
        out_specs=LOCAL,
        out_shape=jax.ShapeDtypeStruct((NY, NZ, PER_DEV, CHUNK, LANES), jnp.bfloat16),
        compiler_params=pltpu.CompilerParams(vmem_limit_bytes=16 * MIB),
        name="pack",
    )(at, blocks, signs.reshape(PER_DEV, BLOCK))


def hadamard(parts):
    span = 1
    while span < len(parts):
        done = list(parts)
        for i in range(len(parts)):
            if not i & span:
                done[i] = parts[i] + parts[i + span]
                done[i + span] = parts[i] - parts[i + span]
        parts = done
        span *= 2
    return parts


def mix_kernel(picks_ref, raw_ref, out_ref, work):
    half = N_BLOCKS // 2

    for base in range(0, N_BLOCKS, 16):
        parts = [raw_ref[base + b].astype(jnp.float32) for b in range(16)]
        for b, part in enumerate(hadamard(parts)):
            work[base + b] = part
    for base in [*range(16), *range(half, half + 16)]:
        parts = [work[base + 16 * e] for e in range(16)]
        for e, part in enumerate(hadamard(parts)):
            work[base + 16 * e] = part

    @pl.loop(0, out_ref.shape[0], unroll=4)
    def _(k):
        pick = picks_ref[k]
        low = lax.rem(pick, half)
        side = (1 - 2 * lax.div(pick, half)).astype(jnp.float32)
        out_ref[k] = (work[low] + side * work[low + half]).astype(out_ref.dtype)


def mix(raw, picks):
    return pl.pallas_call(
        mix_kernel,
        in_specs=[SCALARS, LOCAL],
        out_specs=LOCAL,
        scratch_shapes=[pltpu.VMEM((N_BLOCKS, CHUNK, LANES), jnp.float32)],
        out_shape=jax.ShapeDtypeStruct((picks.shape[0], CHUNK, LANES), jnp.bfloat16),
        compiler_params=pltpu.CompilerParams(vmem_limit_bytes=16 * MIB),
        name="mix",
    )(picks, raw)


NEAR = 3


def share_kernel(near_x, near_y, joined, far_x, far_y):
    joined[0], joined[1], joined[2] = near_x[0], near_x[1], near_y[1]
    far_x[...] = near_x[0]
    far_y[...] = near_y[0]


def share(near_x, near_y):
    _, rows, width = near_x.shape
    piece = jax.ShapeDtypeStruct((rows, width), near_x.dtype)
    return pl.pallas_call(
        share_kernel,
        in_specs=[LOCAL] * 2,
        out_specs=[LOCAL] * 3,
        out_shape=[jax.ShapeDtypeStruct((3, rows, width), near_x.dtype), piece, piece],
        compiler_params=pltpu.CompilerParams(vmem_limit_bytes=16 * MIB),
        cost_estimate=pl.CostEstimate(flops=0, bytes_accessed=2 * MIB, transcendentals=0),
        name="share",
    )(near_x, near_y)


def pair_dot(left, own, other):
    pair = jnp.concatenate([own, other], axis=1)
    return jnp.dot(left, pair, preferred_element_type=jnp.float32).astype(jnp.bfloat16)


def row_pairs(home, near_x, swapped):
    return (home[0], home[1]), (near_x[0], near_x[1]), (swapped[1], swapped[0])


def near_kernel(home, near_x, near_y, swapped, left, out_ref):
    for j, col in enumerate((home[0], near_y[0], swapped[2])):
        left[pl.ds(j * LANES, LANES), :] = col.T
    for j, pair in enumerate(row_pairs(home, near_x, swapped)):
        out_ref[j] = pair_dot(left[...], *pair)


def cost(depth, blocks):
    flops = 2 * depth * blocks * LANES * NCORE * LANES
    return pl.CostEstimate(flops=flops, bytes_accessed=8 * MIB, transcendentals=0)


def gram_near(home, near_x, near_y, swapped):
    depth = home.shape[1]
    return pl.pallas_call(
        near_kernel,
        in_specs=[LOCAL] * 4,
        out_specs=[LOCAL] * 2,
        out_shape=[
            jax.ShapeDtypeStruct((NEAR * LANES, depth), jnp.bfloat16),
            jax.ShapeDtypeStruct((NEAR, NEAR * LANES, NCORE * LANES), jnp.bfloat16),
        ],
        compiler_params=pltpu.CompilerParams(vmem_limit_bytes=16 * MIB),
        cost_estimate=cost(depth, NEAR * NEAR),
        name="gram_near",
    )(home, near_x, near_y, swapped)


def side_kernel(col, home, near_x, swapped, last, out_ref):
    last[...] = col[...].T
    for j, pair in enumerate(row_pairs(home, near_x, swapped)):
        out_ref[j] = pair_dot(last[...], *pair)


def gram_side(col, home, near_x, swapped):
    depth = col.shape[0]
    return pl.pallas_call(
        side_kernel,
        in_specs=[LOCAL] * 4,
        out_specs=[LOCAL] * 2,
        out_shape=[
            jax.ShapeDtypeStruct((LANES, depth), jnp.bfloat16),
            jax.ShapeDtypeStruct((NEAR, LANES, NCORE * LANES), jnp.bfloat16),
        ],
        compiler_params=pltpu.CompilerParams(vmem_limit_bytes=16 * MIB),
        cost_estimate=cost(depth, NEAR),
        name="gram_side",
    )(col, home, near_x, swapped)


def far_kernel(at, near_ref, side_ref, left, last, own, other, out_ref):
    x, core, turn = at[0], at[1], at[2]
    steps = (0, 1 + 2 * core, 3 - 2 * core)

    def put(step_x, step_y, block):
        panel = lax.rem(x + NX - step_x, NX) * NCORE
        quarter = pl.multiple_of(lax.rem(turn + step_y, NY) * LANES, LANES)
        out_ref[panel + core, pl.ds(quarter, LANES), :] = block[:, :LANES]
        out_ref[panel + 1 - core, pl.ds(quarter, LANES), :] = block[:, LANES:]

    block = pair_dot(left[...], own[...], other[...])
    for j, step in enumerate(steps):
        put(2, step, block[j * LANES : (j + 1) * LANES])
    put(2, 2, pair_dot(last[...], own[...], other[...]))
    for i, step_x in enumerate(steps):
        put(step_x, 2, side_ref[i])
        for j, step_y in enumerate(steps):
            put(step_x, step_y, near_ref[i, pl.ds(j * LANES, LANES), :])


def gram_far(at, near, side, left, last, own, other):
    return pl.pallas_call(
        far_kernel,
        in_specs=[SCALARS] + [LOCAL] * 6,
        out_specs=LOCAL,
        out_shape=jax.ShapeDtypeStruct((NX * NCORE, NY * LANES, LANES), near.dtype),
        compiler_params=pltpu.CompilerParams(vmem_limit_bytes=16 * MIB),
        cost_estimate=cost(own.shape[0], NY),
        name="gram_far",
    )(at, near, side, left, last, own, other)


def finish_kernel(scale, parts_ref, out_ref):
    for i in range(out_ref.shape[1] // LANES):
        part = pl.ds(i * LANES, LANES)
        total = parts_ref[0, part].astype(jnp.float32)
        for k in range(1, parts_ref.shape[0]):
            total = total + parts_ref[k, part].astype(jnp.float32)
        out_ref[:, part] = (total * scale).T


def finish(parts, scale):
    count, width, rows = parts.shape
    return pl.pallas_call(
        lambda parts_ref, out_ref: finish_kernel(scale, parts_ref, out_ref),
        out_shape=jax.ShapeDtypeStruct((rows, width), jnp.float32),
        compiler_params=pltpu.CompilerParams(vmem_limit_bytes=16 * MIB),
        name="finish",
    )(parts)


def on_device(grads, signs, picks):
    dp, col = lax.axis_index("dp"), lax.axis_index("col")
    y, z = lax.div(dp, NZ), lax.rem(dp, NZ)
    x, core = lax.div(col, NCORE), lax.rem(col, NCORE)
    at = jnp.stack([x, core, lax.rem(z - y + x + NY, NY)])

    outgoing = pack(grads, signs, at).reshape(NY * NZ, PER_DEV, CHUNK, LANES)
    raw = lax.all_to_all(outgoing, "dp", split_axis=0, concat_axis=0, tiled=True)
    sketch = mix(raw.reshape(N_BLOCKS, CHUNK, LANES), picks).reshape(-1, LANES)

    def ring(value, axis):
        pairs = []
        for i in range(NY * NZ * NX * NCORE):
            (here, rest), down = divmod(i, NZ * NX * NCORE), i % NCORE
            step = 1 - 2 * down
            if axis == "y":
                to = (here + step) % NY * NZ * NX * NCORE + rest
            else:
                side = (i // NCORE % NX + step) % NX
                to = i // (NX * NCORE) * (NX * NCORE) + side * NCORE + down
            pairs.append((i, to))
        return lax.ppermute(value, ("dp", "col"), pairs)

    def swap(value):
        return lax.ppermute(value, "col", [(i, i ^ 1) for i in range(NX * NCORE)])

    home = jnp.stack([sketch, swap(sketch)])
    near_x, near_y = ring(home, "x"), ring(home, "y")
    joined, far_x, far_y = share(near_x, near_y)
    far_x, far_y, swapped = ring(far_x, "x"), ring(far_y, "y"), swap(joined)
    left, near = gram_near(home, near_x, near_y, swapped)
    last, side = gram_side(far_y, home, near_x, swapped)
    partial = gram_far(at, near, side, left, last, far_x, swap(far_x))

    groups = [
        [gy * NZ + (s + gy) % NY + NY * half for gy in range(NY) for half in range(NZ // NY)]
        for s in range(NY)
    ]
    parts = lax.all_to_all(
        partial, "dp", split_axis=0, concat_axis=0, axis_index_groups=groups, tiled=True
    )
    total_rows = grads.shape[0] * NY * NZ
    scale = BLOCK / (total_rows * picks.shape[0] * BLOCK)
    return finish(parts, scale)


def solution(mesh):
    placed = (P("dp", "col"), P("dp"), P())
    return jax.shard_map(
        on_device, mesh=mesh, in_specs=placed, out_specs=P("dp", "col"), check_vma=False
    )
```

```python
import functools

import jax
import jax.numpy as jnp
from jax import lax
from jax.experimental import pallas as pl
from jax.experimental.pallas import tpu as pltpu
from jax.sharding import PartitionSpec as P

NY, NZ, NX, NCORE = 4, 8, 4, 2
BLOCK = 128
LANES = 128
PER_DEV = 16
N_BLOCKS = 512
CHUNK = BLOCK // NZ
MIB = 1 << 20


SCALARS = pl.BlockSpec(memory_space=pltpu.SMEM)
LOCAL = pl.BlockSpec(memory_space=pltpu.VMEM)


def pack_kernel(at, grads_ref, signs_ref, out_ref):
    columns = signs_ref[...].astype(jnp.float32).T
    for z in range(NZ):
        for y in range(NY):
            quarter = lax.rem(z - y + at[0] + NY, NY)
            lanes = pl.ds(pl.multiple_of(quarter * LANES, LANES), LANES)
            for b in range(PER_DEV):
                sign = columns[z * CHUNK : (z + 1) * CHUNK, b : b + 1]
                sign = jnp.broadcast_to(sign, (CHUNK, LANES)).astype(jnp.bfloat16)
                rows = pl.ds(z * CHUNK, CHUNK)
                out_ref[y, z, b] = grads_ref[b, rows, lanes] * sign


def pack(grads, signs, at):
    blocks = grads.reshape(PER_DEV, BLOCK, NY * LANES)
    return pl.pallas_call(
        pack_kernel,
        in_specs=[SCALARS, LOCAL, LOCAL],
        out_specs=LOCAL,
        out_shape=jax.ShapeDtypeStruct((NY, NZ, PER_DEV, CHUNK, LANES), jnp.bfloat16),
        compiler_params=pltpu.CompilerParams(vmem_limit_bytes=16 * MIB),
        name="pack",
    )(at, blocks, signs.reshape(PER_DEV, BLOCK))


def hadamard(parts):
    span = 1
    while span < len(parts):
        done = list(parts)
        for i in range(len(parts)):
            if not i & span:
                done[i] = parts[i] + parts[i + span]
                done[i + span] = parts[i] - parts[i + span]
        parts = done
        span *= 2
    return parts


def mix_kernel(picks_ref, raw_ref, out_ref, work):
    half = N_BLOCKS // 2

    for base in range(0, N_BLOCKS, 16):
        parts = [raw_ref[base + b].astype(jnp.float32) for b in range(16)]
        for b, part in enumerate(hadamard(parts)):
            work[base + b] = part
    for base in [*range(16), *range(half, half + 16)]:
        parts = [work[base + 16 * e] for e in range(16)]
        for e, part in enumerate(hadamard(parts)):
            work[base + 16 * e] = part

    @pl.loop(0, out_ref.shape[0], unroll=4)
    def _(k):
        pick = picks_ref[k]
        low = lax.rem(pick, half)
        side = (1 - 2 * lax.div(pick, half)).astype(jnp.float32)
        out_ref[k] = (work[low] + side * work[low + half]).astype(out_ref.dtype)


def mix(raw, picks):
    return pl.pallas_call(
        mix_kernel,
        in_specs=[SCALARS, LOCAL],
        out_specs=LOCAL,
        scratch_shapes=[pltpu.VMEM((N_BLOCKS, CHUNK, LANES), jnp.float32)],
        out_shape=jax.ShapeDtypeStruct((picks.shape[0], CHUNK, LANES), jnp.bfloat16),
        compiler_params=pltpu.CompilerParams(vmem_limit_bytes=16 * MIB),
        name="mix",
    )(picks, raw)


NEAR = (0, 1, 3)


def halves_kernel(*refs):
    pieces, outs = refs[:4], refs[-4:]
    depth = outs[0].shape[0]
    for i, out in enumerate(outs):
        out[...] = pieces[i][pl.ds(i % 2 * depth, depth), :]


def halves(pieces, after):
    part = jax.ShapeDtypeStruct((pieces[0].shape[0] // 2, LANES), pieces[0].dtype)
    return pl.pallas_call(
        halves_kernel,
        in_specs=[LOCAL] * (4 + len(after)),
        out_specs=[LOCAL] * 4,
        out_shape=[part] * 4,
        compiler_params=pltpu.CompilerParams(vmem_limit_bytes=16 * MIB),
        cost_estimate=pl.CostEstimate(flops=0, bytes_accessed=2 * MIB, transcendentals=0),
        name="halves",
    )(*pieces, *after)


def pair_dot(left, own, other):
    return jnp.dot(left, jnp.concatenate([own, other], axis=1), preferred_element_type=jnp.float32)


def near_kernel(*refs):
    cols, own, other, (left, out_ref) = refs[:3], refs[3:6], refs[6:9], refs[9:]
    for j in range(len(NEAR)):
        left[pl.ds(j * LANES, LANES), :] = cols[j][...].T
    for j in range(len(NEAR)):
        out_ref[j] = pair_dot(left[...], own[j][...], other[j][...]).astype(out_ref.dtype)


def cost(depth, blocks):
    flops = 2 * depth * blocks * LANES * NCORE * LANES
    return pl.CostEstimate(flops=flops, bytes_accessed=8 * MIB, transcendentals=0)


def gram_near(cols, own, other):
    depth, near = cols[0].shape[0], len(NEAR)
    return pl.pallas_call(
        near_kernel,
        in_specs=[LOCAL] * 9,
        out_specs=[LOCAL] * 2,
        out_shape=[
            jax.ShapeDtypeStruct((near * LANES, depth), jnp.bfloat16),
            jax.ShapeDtypeStruct((near, near * LANES, NCORE * LANES), jnp.bfloat16),
        ],
        compiler_params=pltpu.CompilerParams(vmem_limit_bytes=16 * MIB),
        cost_estimate=cost(depth, near * near),
        name="gram_near",
    )(*cols, *own, *other)


def side_kernel(*refs):
    col, own, other, (last, out_ref) = refs[0], refs[1:4], refs[4:7], refs[7:]
    last[...] = col[...].T
    for j in range(len(NEAR)):
        out_ref[j] = pair_dot(last[...], own[j][...], other[j][...]).astype(out_ref.dtype)


def gram_side(col, own, other):
    depth, near = col.shape[0], len(NEAR)
    return pl.pallas_call(
        side_kernel,
        in_specs=[LOCAL] * 7,
        out_specs=[LOCAL] * 2,
        out_shape=[
            jax.ShapeDtypeStruct((LANES, depth), jnp.bfloat16),
            jax.ShapeDtypeStruct((near, LANES, NCORE * LANES), jnp.bfloat16),
        ],
        compiler_params=pltpu.CompilerParams(vmem_limit_bytes=16 * MIB),
        cost_estimate=cost(depth, near),
        name="gram_side",
    )(col, *own, *other)


def far_kernel(at, near_ref, side_ref, left, last, own, other, out_ref):
    x, core, turn = at[0], at[1], at[2]

    def put(step_x, step_y, block):
        panel = lax.rem(x + NX - step_x, NX) * NCORE
        quarter = pl.multiple_of(lax.rem(turn + step_y, NY) * LANES, LANES)
        out_ref[panel + core, pl.ds(quarter, LANES), :] = block[:, :LANES]
        out_ref[panel + 1 - core, pl.ds(quarter, LANES), :] = block[:, LANES:]

    block = pair_dot(left[...], own[...], other[...]).astype(out_ref.dtype)
    for j, step in enumerate(NEAR):
        put(2, step, block[j * LANES : (j + 1) * LANES])
    put(2, 2, pair_dot(last[...], own[...], other[...]).astype(out_ref.dtype))
    for i, step_x in enumerate(NEAR):
        put(step_x, 2, side_ref[i])
        for j, step_y in enumerate(NEAR):
            put(step_x, step_y, near_ref[i, pl.ds(j * LANES, LANES), :])


def gram_far(at, near, side, left, last, own, other):
    return pl.pallas_call(
        far_kernel,
        in_specs=[SCALARS] + [LOCAL] * 6,
        out_specs=LOCAL,
        out_shape=jax.ShapeDtypeStruct((NX * NCORE, NY * LANES, LANES), near.dtype),
        compiler_params=pltpu.CompilerParams(vmem_limit_bytes=16 * MIB),
        cost_estimate=cost(own.shape[0], NY),
        name="gram_far",
    )(at, near, side, left, last, own, other)


def finish_kernel(scale, parts_ref, out_ref):
    for i in range(out_ref.shape[1] // LANES):
        part = pl.ds(i * LANES, LANES)
        total = parts_ref[0, part].astype(jnp.float32)
        for k in range(1, parts_ref.shape[0]):
            total = total + parts_ref[k, part].astype(jnp.float32)
        out_ref[:, part] = (total * scale).T


def finish(parts, scale):
    count, width, rows = parts.shape
    return pl.pallas_call(
        lambda parts_ref, out_ref: finish_kernel(scale, parts_ref, out_ref),
        out_shape=jax.ShapeDtypeStruct((rows, width), jnp.float32),
        compiler_params=pltpu.CompilerParams(vmem_limit_bytes=16 * MIB),
        name="finish",
    )(parts)


def on_device(grads, signs, picks):
    dp, col = lax.axis_index("dp"), lax.axis_index("col")
    y, z = lax.div(dp, NZ), lax.rem(dp, NZ)
    x, core = lax.div(col, NCORE), lax.rem(col, NCORE)
    at = jnp.stack([x, core, lax.rem(z - y + x + NY, NY)])

    outgoing = pack(grads, signs, at).reshape(NY * NZ, PER_DEV, CHUNK, LANES)
    raw = lax.all_to_all(outgoing, "dp", split_axis=0, concat_axis=0, tiled=True)
    sketch = mix(raw.reshape(N_BLOCKS, CHUNK, LANES), picks).reshape(-1, LANES)

    def along_x(value, step):
        return lax.ppermute(value, "col", [(i, (i + NCORE * step) % (NX * NCORE)) for i in range(NX * NCORE)])

    def along_y(value, step):
        return lax.ppermute(value, "dp", [(i, (i + NZ * step) % (NY * NZ)) for i in range(NY * NZ)])

    def swap(value):
        return lax.ppermute(value, "col", [(i, i ^ 1) for i in range(NX * NCORE)])

    x_up, x_down = along_x(sketch, 1), along_x(sketch, -1)
    y_up, y_down = along_y(sketch, 1), along_y(sketch, -1)
    home = swap(sketch)
    x_low, x_high, y_low, y_high = halves((x_up, x_down, y_up, y_down), (home,))
    x_far = jnp.concatenate([along_x(x_low, 1), along_x(x_high, -1)])
    y_far = jnp.concatenate([along_y(y_low, 1), along_y(y_high, -1)])
    own, other = (sketch, x_up, x_down), (home, swap(x_up), swap(x_down))
    left, near = gram_near((sketch, y_up, y_down), own, other)
    last, side = gram_side(y_far, own, other)
    partial = gram_far(at, near, side, left, last, x_far, swap(x_far))

    groups = [
        [gy * NZ + (s + gy) % NY + NY * half for gy in range(NY) for half in range(NZ // NY)]
        for s in range(NY)
    ]
    parts = lax.all_to_all(
        partial, "dp", split_axis=0, concat_axis=0, axis_index_groups=groups, tiled=True
    )
    total_rows = grads.shape[0] * NY * NZ
    scale = BLOCK / (total_rows * picks.shape[0] * BLOCK)
    return finish(parts, scale)


def solution(mesh):
    placed = (P("dp", "col"), P("dp"), P())
    return jax.shard_map(
        on_device, mesh=mesh, in_specs=placed, out_specs=P("dp", "col"), check_vma=False
    )
```

```python
import functools

import jax
import jax.numpy as jnp
from jax import lax
from jax.experimental import pallas as pl
from jax.experimental.pallas import tpu as pltpu
from jax.sharding import PartitionSpec as P

NY, NZ, NX, NCORE = 4, 8, 4, 2
BLOCK = 128
LANES = 128
PER_DEV = 16
N_BLOCKS = 512
CHUNK = BLOCK // NZ
MIB = 1 << 20


SCALARS = pl.BlockSpec(memory_space=pltpu.SMEM)
LOCAL = pl.BlockSpec(memory_space=pltpu.VMEM)


def pack_kernel(at, grads_ref, signs_ref, out_ref):
    columns = signs_ref[...].astype(jnp.float32).T
    for z in range(NZ):
        for y in range(NY):
            quarter = lax.rem(z - y + at[0] + NY, NY)
            lanes = pl.ds(pl.multiple_of(quarter * LANES, LANES), LANES)
            for b in range(PER_DEV):
                sign = columns[z * CHUNK : (z + 1) * CHUNK, b : b + 1]
                sign = jnp.broadcast_to(sign, (CHUNK, LANES)).astype(jnp.bfloat16)
                rows = pl.ds(z * CHUNK, CHUNK)
                out_ref[y, z, b] = grads_ref[b, rows, lanes] * sign


def pack(grads, signs, at):
    blocks = grads.reshape(PER_DEV, BLOCK, NY * LANES)
    return pl.pallas_call(
        pack_kernel,
        in_specs=[SCALARS, LOCAL, LOCAL],
        out_specs=LOCAL,
        out_shape=jax.ShapeDtypeStruct((NY, NZ, PER_DEV, CHUNK, LANES), jnp.bfloat16),
        compiler_params=pltpu.CompilerParams(vmem_limit_bytes=16 * MIB),
        name="pack",
    )(at, blocks, signs.reshape(PER_DEV, BLOCK))


def hadamard(parts):
    span = 1
    while span < len(parts):
        done = list(parts)
        for i in range(len(parts)):
            if not i & span:
                done[i] = parts[i] + parts[i + span]
                done[i + span] = parts[i] - parts[i + span]
        parts = done
        span *= 2
    return parts


def mix_kernel(picks_ref, raw_ref, out_ref, work):
    half = N_BLOCKS // 2

    for base in range(0, N_BLOCKS, 16):
        parts = [raw_ref[base + b].astype(jnp.float32) for b in range(16)]
        for b, part in enumerate(hadamard(parts)):
            work[base + b] = part
    for base in [*range(16), *range(half, half + 16)]:
        parts = [work[base + 16 * e] for e in range(16)]
        for e, part in enumerate(hadamard(parts)):
            work[base + 16 * e] = part

    @pl.loop(0, out_ref.shape[0], unroll=4)
    def _(k):
        pick = picks_ref[k]
        low = lax.rem(pick, half)
        side = (1 - 2 * lax.div(pick, half)).astype(jnp.float32)
        out_ref[k] = (work[low] + side * work[low + half]).astype(out_ref.dtype)


def mix(raw, picks):
    return pl.pallas_call(
        mix_kernel,
        in_specs=[SCALARS, LOCAL],
        out_specs=LOCAL,
        scratch_shapes=[pltpu.VMEM((N_BLOCKS, CHUNK, LANES), jnp.float32)],
        out_shape=jax.ShapeDtypeStruct((picks.shape[0], CHUNK, LANES), jnp.bfloat16),
        compiler_params=pltpu.CompilerParams(vmem_limit_bytes=16 * MIB),
        name="mix",
    )(picks, raw)


NEAR = (0, 1, 3)


def halves_kernel(up, down, *refs):
    low, high = refs[-2:]
    depth = low.shape[0]
    low[...] = up[pl.ds(0, depth), :]
    high[...] = down[pl.ds(depth, depth), :]


def halves(up, down, after):
    part = jax.ShapeDtypeStruct((up.shape[0] // 2, LANES), up.dtype)
    return pl.pallas_call(
        halves_kernel,
        in_specs=[LOCAL] * 3,
        out_specs=[LOCAL] * 2,
        out_shape=[part] * 2,
        compiler_params=pltpu.CompilerParams(vmem_limit_bytes=16 * MIB),
        cost_estimate=pl.CostEstimate(flops=0, bytes_accessed=MIB, transcendentals=0),
        name="halves",
    )(up, down, after)


def pair_dot(left, own, other):
    return jnp.dot(left, jnp.concatenate([own, other], axis=1), preferred_element_type=jnp.float32)


def near_kernel(*refs):
    own, other, cols, (left, out_ref) = refs[:3], refs[3:6], refs[6:9], refs[9:]
    for j in range(len(NEAR)):
        left[pl.ds(j * LANES, LANES), :] = cols[j][...].T
    for j in range(len(NEAR)):
        out_ref[j] = pair_dot(left[...], own[j][...], other[j][...]).astype(out_ref.dtype)


def cost(depth, blocks):
    flops = 2 * depth * blocks * LANES * NCORE * LANES
    return pl.CostEstimate(flops=flops, bytes_accessed=8 * MIB, transcendentals=0)


def gram_near(cols, own, other):
    depth, near = cols[0].shape[0], len(NEAR)
    return pl.pallas_call(
        near_kernel,
        in_specs=[LOCAL] * 9,
        out_specs=[LOCAL] * 2,
        out_shape=[
            jax.ShapeDtypeStruct((near * LANES, depth), jnp.bfloat16),
            jax.ShapeDtypeStruct((near, near * LANES, NCORE * LANES), jnp.bfloat16),
        ],
        compiler_params=pltpu.CompilerParams(vmem_limit_bytes=16 * MIB),
        cost_estimate=cost(depth, near * near),
        name="gram_near",
    )(*own, *other, *cols)


def side_kernel(*refs):
    own, other, col, (last, out_ref) = refs[:3], refs[3:6], refs[6], refs[-2:]
    last[...] = col[...].T
    for j in range(len(NEAR)):
        out_ref[j] = pair_dot(last[...], own[j][...], other[j][...]).astype(out_ref.dtype)


def gram_side(col, own, other, left):
    depth, near = col.shape[0], len(NEAR)
    return pl.pallas_call(
        side_kernel,
        in_specs=[LOCAL] * 8,
        out_specs=[LOCAL] * 2,
        out_shape=[
            jax.ShapeDtypeStruct((LANES, depth), jnp.bfloat16),
            jax.ShapeDtypeStruct((near, LANES, NCORE * LANES), jnp.bfloat16),
        ],
        compiler_params=pltpu.CompilerParams(vmem_limit_bytes=16 * MIB),
        cost_estimate=cost(depth, near),
        name="gram_side",
    )(*own, *other, col, left)


def far_kernel(at, near_ref, side_ref, left, last, own, other, out_ref):
    x, core, turn = at[0], at[1], at[2]

    def put(step_x, step_y, block):
        panel = lax.rem(x + NX - step_x, NX) * NCORE
        quarter = pl.multiple_of(lax.rem(turn + step_y, NY) * LANES, LANES)
        out_ref[panel + core, pl.ds(quarter, LANES), :] = block[:, :LANES]
        out_ref[panel + 1 - core, pl.ds(quarter, LANES), :] = block[:, LANES:]

    block = pair_dot(left[...], own[...], other[...]).astype(out_ref.dtype)
    for j, step in enumerate(NEAR):
        put(2, step, block[j * LANES : (j + 1) * LANES])
    put(2, 2, pair_dot(last[...], own[...], other[...]).astype(out_ref.dtype))
    for i, step_x in enumerate(NEAR):
        put(step_x, 2, side_ref[i])
        for j, step_y in enumerate(NEAR):
            put(step_x, step_y, near_ref[i, pl.ds(j * LANES, LANES), :])


def gram_far(at, near, side, left, last, own, other):
    return pl.pallas_call(
        far_kernel,
        in_specs=[SCALARS] + [LOCAL] * 6,
        out_specs=LOCAL,
        out_shape=jax.ShapeDtypeStruct((NX * NCORE, NY * LANES, LANES), near.dtype),
        compiler_params=pltpu.CompilerParams(vmem_limit_bytes=16 * MIB),
        cost_estimate=cost(own.shape[0], NY),
        name="gram_far",
    )(at, near, side, left, last, own, other)


def finish_kernel(scale, parts_ref, out_ref):
    for i in range(out_ref.shape[1] // LANES):
        part = pl.ds(i * LANES, LANES)
        total = parts_ref[0, part].astype(jnp.float32)
        for k in range(1, parts_ref.shape[0]):
            total = total + parts_ref[k, part].astype(jnp.float32)
        out_ref[:, part] = (total * scale).T


def finish(parts, scale):
    count, width, rows = parts.shape
    return pl.pallas_call(
        lambda parts_ref, out_ref: finish_kernel(scale, parts_ref, out_ref),
        out_shape=jax.ShapeDtypeStruct((rows, width), jnp.float32),
        compiler_params=pltpu.CompilerParams(vmem_limit_bytes=16 * MIB),
        name="finish",
    )(parts)


def on_device(grads, signs, picks):
    dp, col = lax.axis_index("dp"), lax.axis_index("col")
    y, z = lax.div(dp, NZ), lax.rem(dp, NZ)
    x, core = lax.div(col, NCORE), lax.rem(col, NCORE)
    at = jnp.stack([x, core, lax.rem(z - y + x + NY, NY)])

    outgoing = pack(grads, signs, at).reshape(NY * NZ, PER_DEV, CHUNK, LANES)
    raw = lax.all_to_all(outgoing, "dp", split_axis=0, concat_axis=0, tiled=True)
    sketch = mix(raw.reshape(N_BLOCKS, CHUNK, LANES), picks).reshape(-1, LANES)

    def along_x(value, step):
        return lax.ppermute(value, "col", [(i, (i + NCORE * step) % (NX * NCORE)) for i in range(NX * NCORE)])

    def along_y(value, step):
        return lax.ppermute(value, "dp", [(i, (i + NZ * step) % (NY * NZ)) for i in range(NY * NZ)])

    def swap(value):
        return lax.ppermute(value, "col", [(i, i ^ 1) for i in range(NX * NCORE)])

    x_up, x_down = along_x(sketch, 1), along_x(sketch, -1)
    y_up, y_down = along_y(sketch, 1), along_y(sketch, -1)
    home = swap(sketch)
    x_low, x_high = halves(x_up, x_down, home)
    y_low, y_high = halves(y_up, y_down, x_low)
    x_far = jnp.concatenate([along_x(x_low, 1), along_x(x_high, -1)])
    y_far = jnp.concatenate([along_y(y_low, 1), along_y(y_high, -1)])
    own, other = (sketch, x_up, x_down), (home, swap(x_up), swap(x_down))
    left, near = gram_near((sketch, y_up, y_down), own, other)
    last, side = gram_side(y_far, own, other, left)
    partial = gram_far(at, near, side, left, last, x_far, swap(x_far))

    groups = [
        [gy * NZ + (s + gy) % NY + NY * half for gy in range(NY) for half in range(NZ // NY)]
        for s in range(NY)
    ]
    parts = lax.all_to_all(
        partial, "dp", split_axis=0, concat_axis=0, axis_index_groups=groups, tiled=True
    )
    total_rows = grads.shape[0] * NY * NZ
    scale = BLOCK / (total_rows * picks.shape[0] * BLOCK)
    return finish(parts, scale)


def solution(mesh):
    placed = (P("dp", "col"), P("dp"), P())
    return jax.shard_map(
        on_device, mesh=mesh, in_specs=placed, out_specs=P("dp", "col"), check_vma=False
    )
```

```python
import functools

import jax
import jax.numpy as jnp
from jax import lax
from jax.experimental import pallas as pl
from jax.experimental.pallas import tpu as pltpu
from jax.sharding import PartitionSpec as P

NY, NZ, NX, NCORE = 4, 8, 4, 2
BLOCK = 128
LANES = 128
PER_DEV = 16
N_BLOCKS = 512
CHUNK = BLOCK // NZ
MIB = 1 << 20


SCALARS = pl.BlockSpec(memory_space=pltpu.SMEM)
LOCAL = pl.BlockSpec(memory_space=pltpu.VMEM)


def pack_kernel(at, grads_ref, signs_ref, out_ref):
    columns = signs_ref[...].astype(jnp.float32).T
    for z in range(NZ):
        for y in range(NY):
            quarter = lax.rem(z - y + at[0] + NY, NY)
            lanes = pl.ds(pl.multiple_of(quarter * LANES, LANES), LANES)
            for b in range(PER_DEV):
                sign = columns[z * CHUNK : (z + 1) * CHUNK, b : b + 1]
                sign = jnp.broadcast_to(sign, (CHUNK, LANES)).astype(jnp.bfloat16)
                rows = pl.ds(z * CHUNK, CHUNK)
                out_ref[y, z, b] = grads_ref[b, rows, lanes] * sign


def pack(grads, signs, at):
    blocks = grads.reshape(PER_DEV, BLOCK, NY * LANES)
    return pl.pallas_call(
        pack_kernel,
        in_specs=[SCALARS, LOCAL, LOCAL],
        out_specs=LOCAL,
        out_shape=jax.ShapeDtypeStruct((NY, NZ, PER_DEV, CHUNK, LANES), jnp.bfloat16),
        compiler_params=pltpu.CompilerParams(vmem_limit_bytes=16 * MIB),
        name="pack",
    )(at, blocks, signs.reshape(PER_DEV, BLOCK))


def hadamard(parts):
    span = 1
    while span < len(parts):
        done = list(parts)
        for i in range(len(parts)):
            if not i & span:
                done[i] = parts[i] + parts[i + span]
                done[i + span] = parts[i] - parts[i + span]
        parts = done
        span *= 2
    return parts


def mix_kernel(picks_ref, raw_ref, out_ref, work):
    half = N_BLOCKS // 2

    for base in range(0, N_BLOCKS, 16):
        parts = [raw_ref[base + b].astype(jnp.float32) for b in range(16)]
        for b, part in enumerate(hadamard(parts)):
            work[base + b] = part
    for base in [*range(16), *range(half, half + 16)]:
        parts = [work[base + 16 * e] for e in range(16)]
        for e, part in enumerate(hadamard(parts)):
            work[base + 16 * e] = part

    @pl.loop(0, out_ref.shape[0], unroll=4)
    def _(k):
        pick = picks_ref[k]
        low = lax.rem(pick, half)
        side = (1 - 2 * lax.div(pick, half)).astype(jnp.float32)
        out_ref[k] = (work[low] + side * work[low + half]).astype(out_ref.dtype)


def mix(raw, picks):
    return pl.pallas_call(
        mix_kernel,
        in_specs=[SCALARS, LOCAL],
        out_specs=LOCAL,
        scratch_shapes=[pltpu.VMEM((N_BLOCKS, CHUNK, LANES), jnp.float32)],
        out_shape=jax.ShapeDtypeStruct((picks.shape[0], CHUNK, LANES), jnp.bfloat16),
        compiler_params=pltpu.CompilerParams(vmem_limit_bytes=16 * MIB),
        name="mix",
    )(picks, raw)


NEAR = (0, 1, 3)


def onward_kernel(at, x_up, x_down, y_up, y_down, home, far_x, far_y):
    @pl.when(at[1] == 0)
    def _():
        far_x[...] = x_up[...]
        far_y[...] = y_up[...]

    @pl.when(at[1] != 0)
    def _():
        far_x[...] = x_down[...]
        far_y[...] = y_down[...]


def onward(at, x_up, x_down, y_up, y_down, home):
    piece = jax.ShapeDtypeStruct(x_up.shape, x_up.dtype)
    return pl.pallas_call(
        onward_kernel,
        in_specs=[SCALARS] + [LOCAL] * 5,
        out_specs=[LOCAL] * 2,
        out_shape=[piece] * 2,
        compiler_params=pltpu.CompilerParams(vmem_limit_bytes=16 * MIB),
        cost_estimate=pl.CostEstimate(flops=0, bytes_accessed=2 * MIB, transcendentals=0),
        name="onward",
    )(at, x_up, x_down, y_up, y_down, home)


def pair_dot(left, own, other):
    return jnp.dot(left, jnp.concatenate([own, other], axis=1), preferred_element_type=jnp.float32)


def near_kernel(*refs):
    cols, own, other, (left, out_ref) = refs[:3], refs[3:6], refs[6:9], refs[9:]
    for j in range(len(NEAR)):
        left[pl.ds(j * LANES, LANES), :] = cols[j][...].T
    for j in range(len(NEAR)):
        out_ref[j] = pair_dot(left[...], own[j][...], other[j][...]).astype(out_ref.dtype)


def cost(depth, blocks):
    flops = 2 * depth * blocks * LANES * NCORE * LANES
    return pl.CostEstimate(flops=flops, bytes_accessed=8 * MIB, transcendentals=0)


def gram_near(cols, own, other):
    depth, near = cols[0].shape[0], len(NEAR)
    return pl.pallas_call(
        near_kernel,
        in_specs=[LOCAL] * 9,
        out_specs=[LOCAL] * 2,
        out_shape=[
            jax.ShapeDtypeStruct((near * LANES, depth), jnp.bfloat16),
            jax.ShapeDtypeStruct((near, near * LANES, NCORE * LANES), jnp.bfloat16),
        ],
        compiler_params=pltpu.CompilerParams(vmem_limit_bytes=16 * MIB),
        cost_estimate=cost(depth, near * near),
        name="gram_near",
    )(*cols, *own, *other)


def side_kernel(*refs):
    last, own, other, out_ref = refs[0], refs[1:4], refs[4:7], refs[7]
    for j in range(len(NEAR)):
        out_ref[j] = pair_dot(last[...], own[j][...], other[j][...]).astype(out_ref.dtype)


def gram_side(last, own, other):
    depth, near = last.shape[1], len(NEAR)
    return pl.pallas_call(
        side_kernel,
        in_specs=[LOCAL] * 7,
        out_specs=LOCAL,
        out_shape=jax.ShapeDtypeStruct((near, LANES, NCORE * LANES), jnp.bfloat16),
        compiler_params=pltpu.CompilerParams(vmem_limit_bytes=16 * MIB),
        cost_estimate=cost(depth, near),
        name="gram_side",
    )(last, *own, *other)


def turn_kernel(col, out_ref):
    out_ref[...] = col[...].T


def turn(col):
    return pl.pallas_call(
        turn_kernel,
        in_specs=[LOCAL],
        out_specs=LOCAL,
        out_shape=jax.ShapeDtypeStruct(col.shape[::-1], col.dtype),
        compiler_params=pltpu.CompilerParams(vmem_limit_bytes=16 * MIB),
        cost_estimate=pl.CostEstimate(flops=0, bytes_accessed=MIB, transcendentals=0),
        name="turn",
    )(col)


def far_kernel(at, near_ref, side_ref, left, last, own, other, out_ref):
    x, core, turn = at[0], at[1], at[2]

    def put(step_x, step_y, block):
        panel = lax.rem(x + NX - step_x, NX) * NCORE
        quarter = pl.multiple_of(lax.rem(turn + step_y, NY) * LANES, LANES)
        out_ref[panel + core, pl.ds(quarter, LANES), :] = block[:, :LANES]
        out_ref[panel + 1 - core, pl.ds(quarter, LANES), :] = block[:, LANES:]

    block = pair_dot(left[...], own[...], other[...]).astype(out_ref.dtype)
    for j, step in enumerate(NEAR):
        put(2, step, block[j * LANES : (j + 1) * LANES])
    put(2, 2, pair_dot(last[...], own[...], other[...]).astype(out_ref.dtype))
    for i, step_x in enumerate(NEAR):
        put(step_x, 2, side_ref[i])
        for j, step_y in enumerate(NEAR):
            put(step_x, step_y, near_ref[i, pl.ds(j * LANES, LANES), :])


def gram_far(at, near, side, left, last, own, other):
    return pl.pallas_call(
        far_kernel,
        in_specs=[SCALARS] + [LOCAL] * 6,
        out_specs=LOCAL,
        out_shape=jax.ShapeDtypeStruct((NX * NCORE, NY * LANES, LANES), near.dtype),
        compiler_params=pltpu.CompilerParams(vmem_limit_bytes=16 * MIB),
        cost_estimate=cost(own.shape[0], NY),
        name="gram_far",
    )(at, near, side, left, last, own, other)


def finish_kernel(scale, parts_ref, out_ref):
    for i in range(out_ref.shape[1] // LANES):
        part = pl.ds(i * LANES, LANES)
        total = parts_ref[0, part].astype(jnp.float32)
        for k in range(1, parts_ref.shape[0]):
            total = total + parts_ref[k, part].astype(jnp.float32)
        out_ref[:, part] = (total * scale).T


def finish(parts, scale):
    count, width, rows = parts.shape
    return pl.pallas_call(
        lambda parts_ref, out_ref: finish_kernel(scale, parts_ref, out_ref),
        out_shape=jax.ShapeDtypeStruct((rows, width), jnp.float32),
        compiler_params=pltpu.CompilerParams(vmem_limit_bytes=16 * MIB),
        name="finish",
    )(parts)


def on_device(grads, signs, picks):
    dp, col = lax.axis_index("dp"), lax.axis_index("col")
    y, z = lax.div(dp, NZ), lax.rem(dp, NZ)
    x, core = lax.div(col, NCORE), lax.rem(col, NCORE)
    at = jnp.stack([x, core, lax.rem(z - y + x + NY, NY)])

    outgoing = pack(grads, signs, at).reshape(NY * NZ, PER_DEV, CHUNK, LANES)
    raw = lax.all_to_all(outgoing, "dp", split_axis=0, concat_axis=0, tiled=True)
    sketch = mix(raw.reshape(N_BLOCKS, CHUNK, LANES), picks).reshape(-1, LANES)

    def along_x(value, step):
        return lax.ppermute(value, "col", [(i, (i + NCORE * step) % (NX * NCORE)) for i in range(NX * NCORE)])

    def along_y(value, step):
        return lax.ppermute(value, "dp", [(i, (i + NZ * step) % (NY * NZ)) for i in range(NY * NZ)])

    def ring(value, axis):
        pairs = []
        for i in range(NY * NZ * NX * NCORE):
            (here, rest), down = divmod(i, NZ * NX * NCORE), i % NCORE
            step = 1 - 2 * down
            if axis == "y":
                to = (here + step) % NY * NZ * NX * NCORE + rest
            else:
                side = (i // NCORE % NX + step) % NX
                to = i // (NX * NCORE) * (NX * NCORE) + side * NCORE + down
            pairs.append((i, to))
        return lax.ppermute(value, ("dp", "col"), pairs)

    def swap(value):
        return lax.ppermute(value, "col", [(i, i ^ 1) for i in range(NX * NCORE)])

    x_up, x_down = along_x(sketch, 1), along_x(sketch, -1)
    y_up, y_down = along_y(sketch, 1), along_y(sketch, -1)
    home = swap(sketch)
    far_x, far_y = onward(at, x_up, x_down, y_up, y_down, home)
    x_far, y_far = ring(far_x, "x"), ring(far_y, "y")
    own, other = (sketch, x_up, x_down), (home, swap(x_up), swap(x_down))
    left, near = gram_near((sketch, y_up, y_down), own, other)
    last = turn(y_far)
    side = gram_side(last, own, other)
    partial = gram_far(at, near, side, left, last, x_far, swap(x_far))

    groups = [
        [gy * NZ + (s + gy) % NY + NY * half for gy in range(NY) for half in range(NZ // NY)]
        for s in range(NY)
    ]
    parts = lax.all_to_all(
        partial, "dp", split_axis=0, concat_axis=0, axis_index_groups=groups, tiled=True
    )
    total_rows = grads.shape[0] * NY * NZ
    scale = BLOCK / (total_rows * picks.shape[0] * BLOCK)
    return finish(parts, scale)


def solution(mesh):
    placed = (P("dp", "col"), P("dp"), P())
    return jax.shard_map(
        on_device, mesh=mesh, in_specs=placed, out_specs=P("dp", "col"), check_vma=False
    )
```

```python
import functools

import jax
import jax.numpy as jnp
from jax import lax
from jax.experimental import pallas as pl
from jax.experimental.pallas import tpu as pltpu
from jax.sharding import PartitionSpec as P

NY, NZ, NX, NCORE = 4, 8, 4, 2
BLOCK = 128
LANES = 128
PER_DEV = 16
N_BLOCKS = 512
CHUNK = BLOCK // NZ
MIB = 1 << 20


SCALARS = pl.BlockSpec(memory_space=pltpu.SMEM)
LOCAL = pl.BlockSpec(memory_space=pltpu.VMEM)


def pack_kernel(at, grads_ref, signs_ref, out_ref):
    columns = signs_ref[...].astype(jnp.float32).T
    for z in range(NZ):
        for y in range(NY):
            quarter = lax.rem(z - y + at[0] + NY, NY)
            lanes = pl.ds(pl.multiple_of(quarter * LANES, LANES), LANES)
            for b in range(PER_DEV):
                sign = columns[z * CHUNK : (z + 1) * CHUNK, b : b + 1]
                sign = jnp.broadcast_to(sign, (CHUNK, LANES)).astype(jnp.bfloat16)
                rows = pl.ds(z * CHUNK, CHUNK)
                out_ref[y, z, b] = grads_ref[b, rows, lanes] * sign


def pack(grads, signs, at):
    blocks = grads.reshape(PER_DEV, BLOCK, NY * LANES)
    return pl.pallas_call(
        pack_kernel,
        in_specs=[SCALARS, LOCAL, LOCAL],
        out_specs=LOCAL,
        out_shape=jax.ShapeDtypeStruct((NY, NZ, PER_DEV, CHUNK, LANES), jnp.bfloat16),
        compiler_params=pltpu.CompilerParams(vmem_limit_bytes=16 * MIB),
        name="pack",
    )(at, blocks, signs.reshape(PER_DEV, BLOCK))


def hadamard(parts):
    span = 1
    while span < len(parts):
        done = list(parts)
        for i in range(len(parts)):
            if not i & span:
                done[i] = parts[i] + parts[i + span]
                done[i + span] = parts[i] - parts[i + span]
        parts = done
        span *= 2
    return parts


def mix_kernel(picks_ref, raw_ref, out_ref, work):
    half = N_BLOCKS // 2

    for base in range(0, N_BLOCKS, 16):
        parts = [raw_ref[base + b].astype(jnp.float32) for b in range(16)]
        for b, part in enumerate(hadamard(parts)):
            work[base + b] = part
    for base in [*range(16), *range(half, half + 16)]:
        parts = [work[base + 16 * e] for e in range(16)]
        for e, part in enumerate(hadamard(parts)):
            work[base + 16 * e] = part

    @pl.loop(0, out_ref.shape[0], unroll=4)
    def _(k):
        pick = picks_ref[k]
        low = lax.rem(pick, half)
        side = (1 - 2 * lax.div(pick, half)).astype(jnp.float32)
        out_ref[k] = (work[low] + side * work[low + half]).astype(out_ref.dtype)


def mix(raw, picks):
    return pl.pallas_call(
        mix_kernel,
        in_specs=[SCALARS, LOCAL],
        out_specs=LOCAL,
        scratch_shapes=[pltpu.VMEM((N_BLOCKS, CHUNK, LANES), jnp.float32)],
        out_shape=jax.ShapeDtypeStruct((picks.shape[0], CHUNK, LANES), jnp.bfloat16),
        compiler_params=pltpu.CompilerParams(vmem_limit_bytes=16 * MIB),
        name="mix",
    )(picks, raw)


NEAR = (0, 1, 3)


def halves_kernel(*refs):
    pieces, outs = refs[:4], refs[-4:]
    depth = outs[0].shape[0]
    for i, out in enumerate(outs):
        out[...] = pieces[i][pl.ds(i % 2 * depth, depth), :]


def halves(pieces, after):
    part = jax.ShapeDtypeStruct((pieces[0].shape[0] // 2, LANES), pieces[0].dtype)
    return pl.pallas_call(
        halves_kernel,
        in_specs=[LOCAL] * (4 + len(after)),
        out_specs=[LOCAL] * 4,
        out_shape=[part] * 4,
        compiler_params=pltpu.CompilerParams(vmem_limit_bytes=16 * MIB),
        cost_estimate=pl.CostEstimate(flops=0, bytes_accessed=2 * MIB, transcendentals=0),
        name="halves",
    )(*pieces, *after)


def join_kernel(first, second, *refs):
    joined, depth = refs[-1], first.shape[0]
    joined[pl.ds(0, depth), :] = first[...]
    joined[pl.ds(depth, depth), :] = second[...]


def join(first, second, *after):
    return pl.pallas_call(
        join_kernel,
        in_specs=[LOCAL] * (2 + len(after)),
        out_specs=LOCAL,
        out_shape=jax.ShapeDtypeStruct((2 * first.shape[0], LANES), first.dtype),
        compiler_params=pltpu.CompilerParams(vmem_limit_bytes=16 * MIB),
        cost_estimate=pl.CostEstimate(flops=0, bytes_accessed=MIB, transcendentals=0),
        name="join",
    )(first, second, *after)


def pair_dot(left, own, other):
    return jnp.dot(left, jnp.concatenate([own, other], axis=1), preferred_element_type=jnp.float32)


def near_kernel(*refs):
    cols, own, other, (left, out_ref) = refs[:3], refs[3:6], refs[6:9], refs[9:]
    for j in range(len(NEAR)):
        left[pl.ds(j * LANES, LANES), :] = cols[j][...].T
    for j in range(len(NEAR)):
        out_ref[j] = pair_dot(left[...], own[j][...], other[j][...]).astype(out_ref.dtype)


def cost(depth, blocks):
    flops = 2 * depth * blocks * LANES * NCORE * LANES
    return pl.CostEstimate(flops=flops, bytes_accessed=8 * MIB, transcendentals=0)


def gram_near(cols, own, other):
    depth, near = cols[0].shape[0], len(NEAR)
    return pl.pallas_call(
        near_kernel,
        in_specs=[LOCAL] * 9,
        out_specs=[LOCAL] * 2,
        out_shape=[
            jax.ShapeDtypeStruct((near * LANES, depth), jnp.bfloat16),
            jax.ShapeDtypeStruct((near, near * LANES, NCORE * LANES), jnp.bfloat16),
        ],
        compiler_params=pltpu.CompilerParams(vmem_limit_bytes=16 * MIB),
        cost_estimate=cost(depth, near * near),
        name="gram_near",
    )(*cols, *own, *other)


def side_kernel(*refs):
    col, own, other, (last, out_ref) = refs[0], refs[1:4], refs[4:7], refs[7:]
    last[...] = col[...].T
    for j in range(len(NEAR)):
        out_ref[j] = pair_dot(last[...], own[j][...], other[j][...]).astype(out_ref.dtype)


def gram_side(col, own, other):
    depth, near = col.shape[0], len(NEAR)
    return pl.pallas_call(
        side_kernel,
        in_specs=[LOCAL] * 7,
        out_specs=[LOCAL] * 2,
        out_shape=[
            jax.ShapeDtypeStruct((LANES, depth), jnp.bfloat16),
            jax.ShapeDtypeStruct((near, LANES, NCORE * LANES), jnp.bfloat16),
        ],
        compiler_params=pltpu.CompilerParams(vmem_limit_bytes=16 * MIB),
        cost_estimate=cost(depth, near),
        name="gram_side",
    )(col, *own, *other)


def far_kernel(at, near_ref, side_ref, left, last, own, other, out_ref):
    x, core, turn = at[0], at[1], at[2]

    def put(step_x, step_y, block):
        panel = lax.rem(x + NX - step_x, NX) * NCORE
        quarter = pl.multiple_of(lax.rem(turn + step_y, NY) * LANES, LANES)
        out_ref[panel + core, pl.ds(quarter, LANES), :] = block[:, :LANES]
        out_ref[panel + 1 - core, pl.ds(quarter, LANES), :] = block[:, LANES:]

    block = pair_dot(left[...], own[...], other[...]).astype(out_ref.dtype)
    for j, step in enumerate(NEAR):
        put(2, step, block[j * LANES : (j + 1) * LANES])
    put(2, 2, pair_dot(last[...], own[...], other[...]).astype(out_ref.dtype))
    for i, step_x in enumerate(NEAR):
        put(step_x, 2, side_ref[i])
        for j, step_y in enumerate(NEAR):
            put(step_x, step_y, near_ref[i, pl.ds(j * LANES, LANES), :])


def gram_far(at, near, side, left, last, own, other):
    return pl.pallas_call(
        far_kernel,
        in_specs=[SCALARS] + [LOCAL] * 6,
        out_specs=LOCAL,
        out_shape=jax.ShapeDtypeStruct((NX * NCORE, NY * LANES, LANES), near.dtype),
        compiler_params=pltpu.CompilerParams(vmem_limit_bytes=16 * MIB),
        cost_estimate=cost(own.shape[0], NY),
        name="gram_far",
    )(at, near, side, left, last, own, other)


def finish_kernel(scale, parts_ref, out_ref):
    for i in range(out_ref.shape[1] // LANES):
        part = pl.ds(i * LANES, LANES)
        total = parts_ref[0, part].astype(jnp.float32)
        for k in range(1, parts_ref.shape[0]):
            total = total + parts_ref[k, part].astype(jnp.float32)
        out_ref[:, part] = (total * scale).T


def finish(parts, scale):
    count, width, rows = parts.shape
    return pl.pallas_call(
        lambda parts_ref, out_ref: finish_kernel(scale, parts_ref, out_ref),
        out_shape=jax.ShapeDtypeStruct((rows, width), jnp.float32),
        compiler_params=pltpu.CompilerParams(vmem_limit_bytes=16 * MIB),
        name="finish",
    )(parts)


def on_device(grads, signs, picks):
    dp, col = lax.axis_index("dp"), lax.axis_index("col")
    y, z = lax.div(dp, NZ), lax.rem(dp, NZ)
    x, core = lax.div(col, NCORE), lax.rem(col, NCORE)
    at = jnp.stack([x, core, lax.rem(z - y + x + NY, NY)])

    outgoing = pack(grads, signs, at).reshape(NY * NZ, PER_DEV, CHUNK, LANES)
    raw = lax.all_to_all(outgoing, "dp", split_axis=0, concat_axis=0, tiled=True)
    sketch = mix(raw.reshape(N_BLOCKS, CHUNK, LANES), picks).reshape(-1, LANES)

    def along_x(value, step):
        return lax.ppermute(value, "col", [(i, (i + NCORE * step) % (NX * NCORE)) for i in range(NX * NCORE)])

    def along_y(value, step):
        return lax.ppermute(value, "dp", [(i, (i + NZ * step) % (NY * NZ)) for i in range(NY * NZ)])

    def swap(value):
        return lax.ppermute(value, "col", [(i, i ^ 1) for i in range(NX * NCORE)])

    x_up, x_down = along_x(sketch, 1), along_x(sketch, -1)
    y_up, y_down = along_y(sketch, 1), along_y(sketch, -1)
    home = swap(sketch)
    x_low, x_high, y_low, y_high = halves((x_up, x_down, y_up, y_down), (home,))
    y_far = jnp.concatenate([along_y(y_low, 1), along_y(y_high, -1)])
    own, other = (sketch, x_up, x_down), (home, swap(x_up), swap(x_down))
    left, near = gram_near((sketch, y_up, y_down), own, other)
    x_far = join(along_x(x_low, 1), along_x(x_high, -1), left)
    last, side = gram_side(y_far, own, other)
    partial = gram_far(at, near, side, left, last, x_far, swap(x_far))

    groups = [
        [gy * NZ + (s + gy) % NY + NY * half for gy in range(NY) for half in range(NZ // NY)]
        for s in range(NY)
    ]
    parts = lax.all_to_all(
        partial, "dp", split_axis=0, concat_axis=0, axis_index_groups=groups, tiled=True
    )
    total_rows = grads.shape[0] * NY * NZ
    scale = BLOCK / (total_rows * picks.shape[0] * BLOCK)
    return finish(parts, scale)


def solution(mesh):
    placed = (P("dp", "col"), P("dp"), P())
    return jax.shard_map(
        on_device, mesh=mesh, in_specs=placed, out_specs=P("dp", "col"), check_vma=False
    )
```

```python
import functools

import jax
import jax.numpy as jnp
from jax import lax
from jax.experimental import pallas as pl
from jax.experimental.pallas import tpu as pltpu
from jax.sharding import PartitionSpec as P

NY, NZ, NX, NCORE = 4, 8, 4, 2
BLOCK = 128
LANES = 128
PER_DEV = 16
N_BLOCKS = 512
CHUNK = BLOCK // NZ
MIB = 1 << 20


SCALARS = pl.BlockSpec(memory_space=pltpu.SMEM)
LOCAL = pl.BlockSpec(memory_space=pltpu.VMEM)


def pack_kernel(at, grads_ref, signs_ref, out_ref):
    columns = signs_ref[...].astype(jnp.float32).T
    for z in range(NZ):
        for y in range(NY):
            quarter = lax.rem(z - y + at[0] + NY, NY)
            lanes = pl.ds(pl.multiple_of(quarter * LANES, LANES), LANES)
            for b in range(PER_DEV):
                sign = columns[z * CHUNK : (z + 1) * CHUNK, b : b + 1]
                sign = jnp.broadcast_to(sign, (CHUNK, LANES)).astype(jnp.bfloat16)
                rows = pl.ds(z * CHUNK, CHUNK)
                out_ref[y, z, b] = grads_ref[b, rows, lanes] * sign


def pack(grads, signs, at):
    blocks = grads.reshape(PER_DEV, BLOCK, NY * LANES)
    return pl.pallas_call(
        pack_kernel,
        in_specs=[SCALARS, LOCAL, LOCAL],
        out_specs=LOCAL,
        out_shape=jax.ShapeDtypeStruct((NY, NZ, PER_DEV, CHUNK, LANES), jnp.bfloat16),
        compiler_params=pltpu.CompilerParams(vmem_limit_bytes=16 * MIB),
        name="pack",
    )(at, blocks, signs.reshape(PER_DEV, BLOCK))


def hadamard(parts):
    span = 1
    while span < len(parts):
        done = list(parts)
        for i in range(len(parts)):
            if not i & span:
                done[i] = parts[i] + parts[i + span]
                done[i + span] = parts[i] - parts[i + span]
        parts = done
        span *= 2
    return parts


def mix_kernel(picks_ref, raw_ref, out_ref, work):
    half = N_BLOCKS // 2

    for base in range(0, N_BLOCKS, 16):
        parts = [raw_ref[base + b].astype(jnp.float32) for b in range(16)]
        for b, part in enumerate(hadamard(parts)):
            work[base + b] = part
    for base in [*range(16), *range(half, half + 16)]:
        parts = [work[base + 16 * e] for e in range(16)]
        for e, part in enumerate(hadamard(parts)):
            work[base + 16 * e] = part

    @pl.loop(0, out_ref.shape[0], unroll=4)
    def _(k):
        pick = picks_ref[k]
        low = lax.rem(pick, half)
        side = (1 - 2 * lax.div(pick, half)).astype(jnp.float32)
        out_ref[k] = (work[low] + side * work[low + half]).astype(out_ref.dtype)


def mix(raw, picks):
    return pl.pallas_call(
        mix_kernel,
        in_specs=[SCALARS, LOCAL],
        out_specs=LOCAL,
        scratch_shapes=[pltpu.VMEM((N_BLOCKS, CHUNK, LANES), jnp.float32)],
        out_shape=jax.ShapeDtypeStruct((picks.shape[0], CHUNK, LANES), jnp.bfloat16),
        compiler_params=pltpu.CompilerParams(vmem_limit_bytes=16 * MIB),
        name="mix",
    )(picks, raw)


NEAR = (0, 1, 3)


def halves_kernel(*refs):
    pieces, outs = refs[:4], refs[-4:]
    depth = outs[0].shape[0]
    for i, out in enumerate(outs):
        out[...] = pieces[i][pl.ds(i % 2 * depth, depth), :]


def halves(pieces, after):
    part = jax.ShapeDtypeStruct((pieces[0].shape[0] // 2, LANES), pieces[0].dtype)
    return pl.pallas_call(
        halves_kernel,
        in_specs=[LOCAL] * (4 + len(after)),
        out_specs=[LOCAL] * 4,
        out_shape=[part] * 4,
        compiler_params=pltpu.CompilerParams(vmem_limit_bytes=16 * MIB),
        cost_estimate=pl.CostEstimate(flops=0, bytes_accessed=2 * MIB, transcendentals=0),
        name="halves",
    )(*pieces, *after)


def join_kernel(first, second, *refs):
    joined, depth = refs[-1], first.shape[0]
    joined[pl.ds(0, depth), :] = first[...]
    joined[pl.ds(depth, depth), :] = second[...]


def join(first, second, *after):
    return pl.pallas_call(
        join_kernel,
        in_specs=[LOCAL] * (2 + len(after)),
        out_specs=LOCAL,
        out_shape=jax.ShapeDtypeStruct((2 * first.shape[0], LANES), first.dtype),
        compiler_params=pltpu.CompilerParams(vmem_limit_bytes=16 * MIB),
        cost_estimate=pl.CostEstimate(flops=0, bytes_accessed=MIB, transcendentals=0),
        name="join",
    )(first, second, *after)


def pair_dot(left, own, other):
    return jnp.dot(left, jnp.concatenate([own, other], axis=1), preferred_element_type=jnp.float32)


def near_kernel(*refs):
    cols, own, other, (left, out_ref) = refs[:3], refs[3:6], refs[6:9], refs[9:]
    for j in range(len(NEAR)):
        left[pl.ds(j * LANES, LANES), :] = cols[j][...].T
    for j in range(len(NEAR)):
        out_ref[j] = pair_dot(left[...], own[j][...], other[j][...]).astype(out_ref.dtype)


def cost(depth, blocks):
    flops = 2 * depth * blocks * LANES * NCORE * LANES
    return pl.CostEstimate(flops=flops, bytes_accessed=8 * MIB, transcendentals=0)


def gram_near(cols, own, other):
    depth, near = cols[0].shape[0], len(NEAR)
    return pl.pallas_call(
        near_kernel,
        in_specs=[LOCAL] * 9,
        out_specs=[LOCAL] * 2,
        out_shape=[
            jax.ShapeDtypeStruct((near * LANES, depth), jnp.bfloat16),
            jax.ShapeDtypeStruct((near, near * LANES, NCORE * LANES), jnp.bfloat16),
        ],
        compiler_params=pltpu.CompilerParams(vmem_limit_bytes=16 * MIB),
        cost_estimate=cost(depth, near * near),
        name="gram_near",
    )(*cols, *own, *other)


def side_kernel(*refs):
    col, own, other, (last, out_ref) = refs[0], refs[1:4], refs[4:7], refs[7:]
    last[...] = col[...].T
    for j in range(len(NEAR)):
        out_ref[j] = pair_dot(last[...], own[j][...], other[j][...]).astype(out_ref.dtype)


def gram_side(col, own, other):
    depth, near = col.shape[0], len(NEAR)
    return pl.pallas_call(
        side_kernel,
        in_specs=[LOCAL] * 7,
        out_specs=[LOCAL] * 2,
        out_shape=[
            jax.ShapeDtypeStruct((LANES, depth), jnp.bfloat16),
            jax.ShapeDtypeStruct((near, LANES, NCORE * LANES), jnp.bfloat16),
        ],
        compiler_params=pltpu.CompilerParams(vmem_limit_bytes=16 * MIB),
        cost_estimate=cost(depth, near),
        name="gram_side",
    )(col, *own, *other)


def far_kernel(at, near_ref, side_ref, left, last, own, other, out_ref):
    x, core, turn, group = at[0], at[1], at[2], at[3]

    def put(step_x, step_y, block):
        panel = lax.rem(x + NX - step_x, NX)
        flip = lax.rem(core + lax.div(group + panel, NY), NCORE)
        quarter = pl.multiple_of(lax.rem(turn + step_y, NY) * LANES, LANES)
        out_ref[panel * NCORE + flip, pl.ds(quarter, LANES), :] = block[:, :LANES]
        out_ref[panel * NCORE + 1 - flip, pl.ds(quarter, LANES), :] = block[:, LANES:]

    block = pair_dot(left[...], own[...], other[...]).astype(out_ref.dtype)
    for j, step in enumerate(NEAR):
        put(2, step, block[j * LANES : (j + 1) * LANES])
    put(2, 2, pair_dot(last[...], own[...], other[...]).astype(out_ref.dtype))
    for i, step_x in enumerate(NEAR):
        put(step_x, 2, side_ref[i])
        for j, step_y in enumerate(NEAR):
            put(step_x, step_y, near_ref[i, pl.ds(j * LANES, LANES), :])


def gram_far(at, near, side, left, last, own, other):
    return pl.pallas_call(
        far_kernel,
        in_specs=[SCALARS] + [LOCAL] * 6,
        out_specs=LOCAL,
        out_shape=jax.ShapeDtypeStruct((NX * NCORE, NY * LANES, LANES), near.dtype),
        compiler_params=pltpu.CompilerParams(vmem_limit_bytes=16 * MIB),
        cost_estimate=cost(own.shape[0], NY),
        name="gram_far",
    )(at, near, side, left, last, own, other)


def finish_kernel(scale, parts_ref, out_ref):
    for i in range(out_ref.shape[1] // LANES):
        part = pl.ds(i * LANES, LANES)
        total = parts_ref[0, part].astype(jnp.float32)
        for k in range(1, parts_ref.shape[0]):
            total = total + parts_ref[k, part].astype(jnp.float32)
        out_ref[:, part] = (total * scale).T


def finish(parts, scale):
    count, width, rows = parts.shape
    return pl.pallas_call(
        lambda parts_ref, out_ref: finish_kernel(scale, parts_ref, out_ref),
        out_shape=jax.ShapeDtypeStruct((rows, width), jnp.float32),
        compiler_params=pltpu.CompilerParams(vmem_limit_bytes=16 * MIB),
        name="finish",
    )(parts)


def on_device(grads, signs, picks):
    dp, col = lax.axis_index("dp"), lax.axis_index("col")
    y, z = lax.div(dp, NZ), lax.rem(dp, NZ)
    x, core = lax.div(col, NCORE), lax.rem(col, NCORE)
    at = jnp.stack([x, core, lax.rem(z - y + x + NY, NY), lax.rem(z - y + NY, NY)])

    outgoing = pack(grads, signs, at).reshape(NY * NZ, PER_DEV, CHUNK, LANES)
    raw = lax.all_to_all(outgoing, "dp", split_axis=0, concat_axis=0, tiled=True)
    sketch = mix(raw.reshape(N_BLOCKS, CHUNK, LANES), picks).reshape(-1, LANES)

    def along_x(value, step):
        return lax.ppermute(value, "col", [(i, (i + NCORE * step) % (NX * NCORE)) for i in range(NX * NCORE)])

    def along_y(value, step):
        return lax.ppermute(value, "dp", [(i, (i + NZ * step) % (NY * NZ)) for i in range(NY * NZ)])

    def swap(value):
        return lax.ppermute(value, "col", [(i, i ^ 1) for i in range(NX * NCORE)])

    x_up, x_down = along_x(sketch, 1), along_x(sketch, -1)
    y_up, y_down = along_y(sketch, 1), along_y(sketch, -1)
    home = swap(sketch)
    x_low, x_high, y_low, y_high = halves((x_up, x_down, y_up, y_down), (home,))
    y_far = jnp.concatenate([along_y(y_low, 1), along_y(y_high, -1)])
    own, other = (sketch, x_up, x_down), (home, swap(x_up), swap(x_down))
    left, near = gram_near((sketch, y_up, y_down), own, other)
    x_far = join(along_x(x_low, 1), along_x(x_high, -1), left)
    last, side = gram_side(y_far, own, other)
    partial = gram_far(at, near, side, left, last, x_far, swap(x_far))

    groups = [
        [gy * NZ + (s + gy + NY * h) % NZ for gy in range(NY) for h in range(NZ // NY)]
        for s in range(NY)
    ]
    parts = lax.all_to_all(
        partial, "dp", split_axis=0, concat_axis=0, axis_index_groups=groups, tiled=True
    )
    total_rows = grads.shape[0] * NY * NZ
    scale = BLOCK / (total_rows * picks.shape[0] * BLOCK)
    return finish(parts, scale)


def solution(mesh):
    placed = (P("dp", "col"), P("dp"), P())
    return jax.shard_map(
        on_device, mesh=mesh, in_specs=placed, out_specs=P("dp", "col"), check_vma=False
    )
```

```python
import functools

import jax
import jax.numpy as jnp
from jax import lax
from jax.experimental import pallas as pl
from jax.experimental.pallas import tpu as pltpu
from jax.sharding import PartitionSpec as P

NY, NZ, NX, NCORE = 4, 8, 4, 2
BLOCK = 128
LANES = 128
PER_DEV = 16
N_BLOCKS = 512
CHUNK = BLOCK // NZ
MIB = 1 << 20
PIECES = 4


SCALARS = pl.BlockSpec(memory_space=pltpu.SMEM)
LOCAL = pl.BlockSpec(memory_space=pltpu.VMEM)


def pack_kernel(at, signs_ref, *refs):
    pieces, out_ref = refs[:-1], refs[-1]
    columns = signs_ref[...].astype(jnp.float32).T
    count = pieces[0].shape[0]
    for b in range(PER_DEV):
        for z in range(NZ):
            sign = columns[z * CHUNK : (z + 1) * CHUNK, b : b + 1]
            sign = jnp.broadcast_to(sign, (CHUNK, LANES)).astype(jnp.bfloat16)
            rows = pl.ds(z * CHUNK, CHUNK)
            for y in range(NY):
                quarter = lax.rem(z - y + at[0] + NY, NY)
                lanes = pl.ds(pl.multiple_of(quarter * LANES, LANES), LANES)
                out_ref[y, z, b] = pieces[b // count][b % count, rows, lanes] * sign


def pack(grads, signs, at):
    blocks = grads.reshape(PER_DEV, BLOCK, NY * LANES)
    count = PER_DEV // PIECES
    pieces = [blocks[i * count : (i + 1) * count] for i in range(PIECES)]
    return pl.pallas_call(
        pack_kernel,
        in_specs=[SCALARS] + [LOCAL] * (1 + PIECES),
        out_specs=LOCAL,
        out_shape=jax.ShapeDtypeStruct((NY, NZ, PER_DEV, CHUNK, LANES), jnp.bfloat16),
        compiler_params=pltpu.CompilerParams(vmem_limit_bytes=16 * MIB),
        name="pack",
    )(at, signs.reshape(PER_DEV, BLOCK), *pieces)


def hadamard(parts):
    span = 1
    while span < len(parts):
        done = list(parts)
        for i in range(len(parts)):
            if not i & span:
                done[i] = parts[i] + parts[i + span]
                done[i + span] = parts[i] - parts[i + span]
        parts = done
        span *= 2
    return parts


def mix_kernel(picks_ref, raw_ref, out_ref, work):
    half = N_BLOCKS // 2

    for base in range(0, N_BLOCKS, 16):
        parts = [raw_ref[base + b].astype(jnp.float32) for b in range(16)]
        for b, part in enumerate(hadamard(parts)):
            work[base + b] = part
    for base in [*range(16), *range(half, half + 16)]:
        parts = [work[base + 16 * e] for e in range(16)]
        for e, part in enumerate(hadamard(parts)):
            work[base + 16 * e] = part

    @pl.loop(0, out_ref.shape[0], unroll=4)
    def _(k):
        pick = picks_ref[k]
        low = lax.rem(pick, half)
        side = (1 - 2 * lax.div(pick, half)).astype(jnp.float32)
        out_ref[k] = (work[low] + side * work[low + half]).astype(out_ref.dtype)


def mix(raw, picks):
    return pl.pallas_call(
        mix_kernel,
        in_specs=[SCALARS, LOCAL],
        out_specs=LOCAL,
        scratch_shapes=[pltpu.VMEM((N_BLOCKS, CHUNK, LANES), jnp.float32)],
        out_shape=jax.ShapeDtypeStruct((picks.shape[0], CHUNK, LANES), jnp.bfloat16),
        compiler_params=pltpu.CompilerParams(vmem_limit_bytes=16 * MIB),
        name="mix",
    )(picks, raw)


NEAR = (0, 1, 3)


def halves_kernel(up, down, *refs):
    low, high = refs[-2:]
    depth = low.shape[0]
    low[...] = up[pl.ds(0, depth), :]
    high[...] = down[pl.ds(depth, depth), :]


def halves(up, down, *after):
    part = jax.ShapeDtypeStruct((up.shape[0] // 2, LANES), up.dtype)
    return pl.pallas_call(
        halves_kernel,
        in_specs=[LOCAL] * (2 + len(after)),
        out_specs=[LOCAL] * 2,
        out_shape=[part] * 2,
        compiler_params=pltpu.CompilerParams(vmem_limit_bytes=16 * MIB),
        cost_estimate=pl.CostEstimate(flops=0, bytes_accessed=MIB, transcendentals=0),
        name="halves",
    )(up, down, *after)


def join_kernel(first, second, *refs):
    joined, depth = refs[-1], first.shape[0]
    joined[pl.ds(0, depth), :] = first[...]
    joined[pl.ds(depth, depth), :] = second[...]


def join(first, second, *after):
    return pl.pallas_call(
        join_kernel,
        in_specs=[LOCAL] * (2 + len(after)),
        out_specs=LOCAL,
        out_shape=jax.ShapeDtypeStruct((2 * first.shape[0], LANES), first.dtype),
        compiler_params=pltpu.CompilerParams(vmem_limit_bytes=16 * MIB),
        cost_estimate=pl.CostEstimate(flops=0, bytes_accessed=MIB, transcendentals=0),
        name="join",
    )(first, second, *after)


def pair_dot(left, own, other):
    return jnp.dot(left, jnp.concatenate([own, other], axis=1), preferred_element_type=jnp.float32)


def near_kernel(*refs):
    cols, own, other, (left, out_ref) = refs[:3], refs[3:6], refs[6:9], refs[9:]
    for j in range(len(NEAR)):
        left[pl.ds(j * LANES, LANES), :] = cols[j][...].T
    for j in range(len(NEAR)):
        out_ref[j] = pair_dot(left[...], own[j][...], other[j][...]).astype(out_ref.dtype)


def cost(depth, blocks):
    flops = 2 * depth * blocks * LANES * NCORE * LANES
    return pl.CostEstimate(flops=flops, bytes_accessed=8 * MIB, transcendentals=0)


def gram_near(cols, own, other):
    depth, near = cols[0].shape[0], len(NEAR)
    return pl.pallas_call(
        near_kernel,
        in_specs=[LOCAL] * 9,
        out_specs=[LOCAL] * 2,
        out_shape=[
            jax.ShapeDtypeStruct((near * LANES, depth), jnp.bfloat16),
            jax.ShapeDtypeStruct((near, near * LANES, NCORE * LANES), jnp.bfloat16),
        ],
        compiler_params=pltpu.CompilerParams(vmem_limit_bytes=16 * MIB),
        cost_estimate=cost(depth, near * near),
        name="gram_near",
    )(*cols, *own, *other)


def side_kernel(*refs):
    col, own, other, (last, out_ref) = refs[0], refs[1:4], refs[4:7], refs[7:]
    last[...] = col[...].T
    for j in range(len(NEAR)):
        out_ref[j] = pair_dot(last[...], own[j][...], other[j][...]).astype(out_ref.dtype)


def gram_side(col, own, other):
    depth, near = col.shape[0], len(NEAR)
    return pl.pallas_call(
        side_kernel,
        in_specs=[LOCAL] * 7,
        out_specs=[LOCAL] * 2,
        out_shape=[
            jax.ShapeDtypeStruct((LANES, depth), jnp.bfloat16),
            jax.ShapeDtypeStruct((near, LANES, NCORE * LANES), jnp.bfloat16),
        ],
        compiler_params=pltpu.CompilerParams(vmem_limit_bytes=16 * MIB),
        cost_estimate=cost(depth, near),
        name="gram_side",
    )(col, *own, *other)


def far_kernel(at, near_ref, side_ref, left, last, own, other, out_ref):
    x, core, turn, group = at[0], at[1], at[2], at[3]

    def put(step_x, step_y, block):
        panel = lax.rem(x + NX - step_x, NX)
        flip = lax.rem(core + lax.div(group + panel, NY), NCORE)
        quarter = pl.multiple_of(lax.rem(turn + step_y, NY) * LANES, LANES)
        out_ref[panel * NCORE + flip, pl.ds(quarter, LANES), :] = block[:, :LANES]
        out_ref[panel * NCORE + 1 - flip, pl.ds(quarter, LANES), :] = block[:, LANES:]

    block = pair_dot(left[...], own[...], other[...]).astype(out_ref.dtype)
    for j, step in enumerate(NEAR):
        put(2, step, block[j * LANES : (j + 1) * LANES])
    put(2, 2, pair_dot(last[...], own[...], other[...]).astype(out_ref.dtype))
    for i, step_x in enumerate(NEAR):
        put(step_x, 2, side_ref[i])
        for j, step_y in enumerate(NEAR):
            put(step_x, step_y, near_ref[i, pl.ds(j * LANES, LANES), :])


def gram_far(at, near, side, left, last, own, other):
    return pl.pallas_call(
        far_kernel,
        in_specs=[SCALARS] + [LOCAL] * 6,
        out_specs=LOCAL,
        out_shape=jax.ShapeDtypeStruct((NX * NCORE, NY * LANES, LANES), near.dtype),
        compiler_params=pltpu.CompilerParams(vmem_limit_bytes=16 * MIB),
        cost_estimate=cost(own.shape[0], NY),
        name="gram_far",
    )(at, near, side, left, last, own, other)


def finish_kernel(scale, parts_ref, out_ref):
    for i in range(out_ref.shape[1] // LANES):
        part = pl.ds(i * LANES, LANES)
        total = parts_ref[0, part].astype(jnp.float32)
        for k in range(1, parts_ref.shape[0]):
            total = total + parts_ref[k, part].astype(jnp.float32)
        out_ref[:, part] = (total * scale).T


def finish(parts, scale):
    count, width, rows = parts.shape
    return pl.pallas_call(
        lambda parts_ref, out_ref: finish_kernel(scale, parts_ref, out_ref),
        out_shape=jax.ShapeDtypeStruct((rows, width), jnp.float32),
        compiler_params=pltpu.CompilerParams(vmem_limit_bytes=16 * MIB),
        name="finish",
    )(parts)


def on_device(grads, signs, picks):
    dp, col = lax.axis_index("dp"), lax.axis_index("col")
    y, z = lax.div(dp, NZ), lax.rem(dp, NZ)
    x, core = lax.div(col, NCORE), lax.rem(col, NCORE)
    at = jnp.stack([x, core, lax.rem(z - y + x + NY, NY), lax.rem(z - y + NY, NY)])

    outgoing = pack(grads, signs, at).reshape(NY * NZ, PER_DEV, CHUNK, LANES)
    raw = lax.all_to_all(outgoing, "dp", split_axis=0, concat_axis=0, tiled=True)
    sketch = mix(raw.reshape(N_BLOCKS, CHUNK, LANES), picks).reshape(-1, LANES)

    def along_x(value, step):
        return lax.ppermute(value, "col", [(i, (i + NCORE * step) % (NX * NCORE)) for i in range(NX * NCORE)])

    def along_y(value, step):
        return lax.ppermute(value, "dp", [(i, (i + NZ * step) % (NY * NZ)) for i in range(NY * NZ)])

    def swap(value):
        return lax.ppermute(value, "col", [(i, i ^ 1) for i in range(NX * NCORE)])

    x_up, x_down = along_x(sketch, 1), along_x(sketch, -1)
    y_up, y_down = along_y(sketch, 1), along_y(sketch, -1)
    home = swap(sketch)
    x_low, x_high = halves(x_up, x_down)
    y_low, y_high = halves(y_up, y_down, home, x_low)
    y_far = jnp.concatenate([along_y(y_low, 1), along_y(y_high, -1)])
    own, other = (sketch, x_up, x_down), (home, swap(x_up), swap(x_down))
    left, near = gram_near((sketch, y_up, y_down), own, other)
    x_far = join(along_x(x_low, 1), along_x(x_high, -1), left)
    last, side = gram_side(y_far, own, other)
    partial = gram_far(at, near, side, left, last, x_far, swap(x_far))

    groups = [
        [gy * NZ + (s + gy + NY * h) % NZ for gy in range(NY) for h in range(NZ // NY)]
        for s in range(NY)
    ]
    parts = lax.all_to_all(
        partial, "dp", split_axis=0, concat_axis=0, axis_index_groups=groups, tiled=True
    )
    total_rows = grads.shape[0] * NY * NZ
    scale = BLOCK / (total_rows * picks.shape[0] * BLOCK)
    return finish(parts, scale)


def solution(mesh):
    placed = (P("dp", "col"), P("dp"), P())
    return jax.shard_map(
        on_device, mesh=mesh, in_specs=placed, out_specs=P("dp", "col"), check_vma=False
    )
```

```python
import functools

import jax
import jax.numpy as jnp
from jax import lax
from jax.experimental import pallas as pl
from jax.experimental.pallas import tpu as pltpu
from jax.sharding import PartitionSpec as P

NY, NZ, NX, NCORE = 4, 8, 4, 2
BLOCK = 128
LANES = 128
PER_DEV = 16
N_BLOCKS = 512
CHUNK = BLOCK // NZ
MIB = 1 << 20
PIECES = 4


SCALARS = pl.BlockSpec(memory_space=pltpu.SMEM)
LOCAL = pl.BlockSpec(memory_space=pltpu.VMEM)


def pack_kernel(at, signs_ref, *refs):
    pieces, out_ref = refs[:-1], refs[-1]
    columns = signs_ref[...].astype(jnp.float32).T
    count = pieces[0].shape[0]
    for z in range(NZ):
        rows = pl.ds(z * CHUNK, CHUNK)
        for y in range(NY):
            quarter = lax.rem(z - y + at[0] + NY, NY)
            lanes = pl.ds(pl.multiple_of(quarter * LANES, LANES), LANES)
            for b in range(PER_DEV):
                sign = columns[z * CHUNK : (z + 1) * CHUNK, b : b + 1]
                sign = jnp.broadcast_to(sign, (CHUNK, LANES)).astype(jnp.bfloat16)
                out_ref[y, z, b] = pieces[b // count][b % count, rows, lanes] * sign


def pack(grads, signs, at):
    blocks = grads.reshape(PER_DEV, BLOCK, NY * LANES)
    count = PER_DEV // PIECES
    pieces = [blocks[i * count : (i + 1) * count] for i in range(PIECES)]
    return pl.pallas_call(
        pack_kernel,
        in_specs=[SCALARS] + [LOCAL] * (1 + PIECES),
        out_specs=LOCAL,
        out_shape=jax.ShapeDtypeStruct((NY, NZ, PER_DEV, CHUNK, LANES), jnp.bfloat16),
        compiler_params=pltpu.CompilerParams(vmem_limit_bytes=16 * MIB),
        name="pack",
    )(at, signs.reshape(PER_DEV, BLOCK), *pieces)


def hadamard(parts):
    span = 1
    while span < len(parts):
        done = list(parts)
        for i in range(len(parts)):
            if not i & span:
                done[i] = parts[i] + parts[i + span]
                done[i + span] = parts[i] - parts[i + span]
        parts = done
        span *= 2
    return parts


def mix_kernel(picks_ref, raw_ref, out_ref, work):
    half = N_BLOCKS // 2

    for base in range(0, N_BLOCKS, 16):
        parts = [raw_ref[base + b].astype(jnp.float32) for b in range(16)]
        for b, part in enumerate(hadamard(parts)):
            work[base + b] = part
    for base in [*range(16), *range(half, half + 16)]:
        parts = [work[base + 16 * e] for e in range(16)]
        for e, part in enumerate(hadamard(parts)):
            work[base + 16 * e] = part

    @pl.loop(0, out_ref.shape[0], unroll=4)
    def _(k):
        pick = picks_ref[k]
        low = lax.rem(pick, half)
        side = (1 - 2 * lax.div(pick, half)).astype(jnp.float32)
        out_ref[k] = (work[low] + side * work[low + half]).astype(out_ref.dtype)


def mix(raw, picks):
    return pl.pallas_call(
        mix_kernel,
        in_specs=[SCALARS, LOCAL],
        out_specs=LOCAL,
        scratch_shapes=[pltpu.VMEM((N_BLOCKS, CHUNK, LANES), jnp.float32)],
        out_shape=jax.ShapeDtypeStruct((picks.shape[0], CHUNK, LANES), jnp.bfloat16),
        compiler_params=pltpu.CompilerParams(vmem_limit_bytes=16 * MIB),
        name="mix",
    )(picks, raw)


NEAR = (0, 1, 3)


def halves_kernel(up, down, *refs):
    low, high = refs[-2:]
    depth = low.shape[0]
    low[...] = up[pl.ds(0, depth), :]
    high[...] = down[pl.ds(depth, depth), :]


def halves(up, down, *after):
    part = jax.ShapeDtypeStruct((up.shape[0] // 2, LANES), up.dtype)
    return pl.pallas_call(
        halves_kernel,
        in_specs=[LOCAL] * (2 + len(after)),
        out_specs=[LOCAL] * 2,
        out_shape=[part] * 2,
        compiler_params=pltpu.CompilerParams(vmem_limit_bytes=16 * MIB),
        cost_estimate=pl.CostEstimate(flops=0, bytes_accessed=MIB, transcendentals=0),
        name="halves",
    )(up, down, *after)


def join_kernel(first, second, *refs):
    joined, depth = refs[-1], first.shape[0]
    joined[pl.ds(0, depth), :] = first[...]
    joined[pl.ds(depth, depth), :] = second[...]


def join(first, second, *after):
    return pl.pallas_call(
        join_kernel,
        in_specs=[LOCAL] * (2 + len(after)),
        out_specs=LOCAL,
        out_shape=jax.ShapeDtypeStruct((2 * first.shape[0], LANES), first.dtype),
        compiler_params=pltpu.CompilerParams(vmem_limit_bytes=16 * MIB),
        cost_estimate=pl.CostEstimate(flops=0, bytes_accessed=MIB, transcendentals=0),
        name="join",
    )(first, second, *after)


def pair_dot(left, own, other):
    return jnp.dot(left, jnp.concatenate([own, other], axis=1), preferred_element_type=jnp.float32)


def near_kernel(*refs):
    cols, own, other, (left, out_ref) = refs[:3], refs[3:6], refs[6:9], refs[9:]
    for j in range(len(NEAR)):
        left[pl.ds(j * LANES, LANES), :] = cols[j][...].T
    for j in range(len(NEAR)):
        out_ref[j] = pair_dot(left[...], own[j][...], other[j][...]).astype(out_ref.dtype)


def cost(depth, blocks):
    flops = 2 * depth * blocks * LANES * NCORE * LANES
    return pl.CostEstimate(flops=flops, bytes_accessed=8 * MIB, transcendentals=0)


def gram_near(cols, own, other):
    depth, near = cols[0].shape[0], len(NEAR)
    return pl.pallas_call(
        near_kernel,
        in_specs=[LOCAL] * 9,
        out_specs=[LOCAL] * 2,
        out_shape=[
            jax.ShapeDtypeStruct((near * LANES, depth), jnp.bfloat16),
            jax.ShapeDtypeStruct((near, near * LANES, NCORE * LANES), jnp.bfloat16),
        ],
        compiler_params=pltpu.CompilerParams(vmem_limit_bytes=16 * MIB),
        cost_estimate=cost(depth, near * near),
        name="gram_near",
    )(*cols, *own, *other)


def side_kernel(*refs):
    col, own, other, (last, out_ref) = refs[0], refs[1:4], refs[4:7], refs[7:]
    last[...] = col[...].T
    for j in range(len(NEAR)):
        out_ref[j] = pair_dot(last[...], own[j][...], other[j][...]).astype(out_ref.dtype)


def gram_side(col, own, other):
    depth, near = col.shape[0], len(NEAR)
    return pl.pallas_call(
        side_kernel,
        in_specs=[LOCAL] * 7,
        out_specs=[LOCAL] * 2,
        out_shape=[
            jax.ShapeDtypeStruct((LANES, depth), jnp.bfloat16),
            jax.ShapeDtypeStruct((near, LANES, NCORE * LANES), jnp.bfloat16),
        ],
        compiler_params=pltpu.CompilerParams(vmem_limit_bytes=16 * MIB),
        cost_estimate=cost(depth, near),
        name="gram_side",
    )(col, *own, *other)


def far_kernel(at, near_ref, side_ref, left, last, own, other, out_ref):
    x, core, turn, group = at[0], at[1], at[2], at[3]

    def put(step_x, step_y, block):
        panel = lax.rem(x + NX - step_x, NX)
        flip = lax.rem(core + lax.div(group + panel, NY), NCORE)
        quarter = pl.multiple_of(lax.rem(turn + step_y, NY) * LANES, LANES)
        out_ref[panel * NCORE + flip, pl.ds(quarter, LANES), :] = block[:, :LANES]
        out_ref[panel * NCORE + 1 - flip, pl.ds(quarter, LANES), :] = block[:, LANES:]

    whole = jnp.concatenate([left[...], last[...]], axis=0)
    block = pair_dot(whole, own[...], other[...]).astype(out_ref.dtype)
    for j, step in enumerate((*NEAR, 2)):
        put(2, step, block[j * LANES : (j + 1) * LANES])
    for i, step_x in enumerate(NEAR):
        put(step_x, 2, side_ref[i])
        for j, step_y in enumerate(NEAR):
            put(step_x, step_y, near_ref[i, pl.ds(j * LANES, LANES), :])


def gram_far(at, near, side, left, last, own, other):
    return pl.pallas_call(
        far_kernel,
        in_specs=[SCALARS] + [LOCAL] * 6,
        out_specs=LOCAL,
        out_shape=jax.ShapeDtypeStruct((NX * NCORE, NY * LANES, LANES), near.dtype),
        compiler_params=pltpu.CompilerParams(vmem_limit_bytes=16 * MIB),
        cost_estimate=cost(own.shape[0], NY),
        name="gram_far",
    )(at, near, side, left, last, own, other)


def finish_kernel(scale, parts_ref, out_ref):
    for i in range(out_ref.shape[1] // LANES):
        part = pl.ds(i * LANES, LANES)
        total = parts_ref[0, part].astype(jnp.float32)
        for k in range(1, parts_ref.shape[0]):
            total = total + parts_ref[k, part].astype(jnp.float32)
        out_ref[:, part] = (total * scale).T


def finish(parts, scale):
    count, width, rows = parts.shape
    return pl.pallas_call(
        lambda parts_ref, out_ref: finish_kernel(scale, parts_ref, out_ref),
        out_shape=jax.ShapeDtypeStruct((rows, width), jnp.float32),
        compiler_params=pltpu.CompilerParams(vmem_limit_bytes=16 * MIB),
        name="finish",
    )(parts)


def on_device(grads, signs, picks):
    dp, col = lax.axis_index("dp"), lax.axis_index("col")
    y, z = lax.div(dp, NZ), lax.rem(dp, NZ)
    x, core = lax.div(col, NCORE), lax.rem(col, NCORE)
    at = jnp.stack([x, core, lax.rem(z - y + x + NY, NY), lax.rem(z - y + NY, NY)])

    outgoing = pack(grads, signs, at).reshape(NY * NZ, PER_DEV, CHUNK, LANES)
    raw = lax.all_to_all(outgoing, "dp", split_axis=0, concat_axis=0, tiled=True)
    sketch = mix(raw.reshape(N_BLOCKS, CHUNK, LANES), picks).reshape(-1, LANES)

    def along_x(value, step):
        return lax.ppermute(value, "col", [(i, (i + NCORE * step) % (NX * NCORE)) for i in range(NX * NCORE)])

    def along_y(value, step):
        return lax.ppermute(value, "dp", [(i, (i + NZ * step) % (NY * NZ)) for i in range(NY * NZ)])

    def swap(value):
        return lax.ppermute(value, "col", [(i, i ^ 1) for i in range(NX * NCORE)])

    x_up, x_down = along_x(sketch, 1), along_x(sketch, -1)
    y_up, y_down = along_y(sketch, 1), along_y(sketch, -1)
    home = swap(sketch)
    x_low, x_high = halves(x_up, x_down)
    y_low, y_high = halves(y_up, y_down, home, x_low)
    y_far = jnp.concatenate([along_y(y_low, 1), along_y(y_high, -1)])
    own, other = (sketch, x_up, x_down), (home, swap(x_up), swap(x_down))
    left, near = gram_near((sketch, y_up, y_down), own, other)
    x_far = join(along_x(x_low, 1), along_x(x_high, -1), left)
    last, side = gram_side(y_far, own, other)
    partial = gram_far(at, near, side, left, last, x_far, swap(x_far))

    groups = [
        [gy * NZ + (s + gy + NY * h) % NZ for gy in range(NY) for h in range(NZ // NY)]
        for s in range(NY)
    ]
    parts = lax.all_to_all(
        partial, "dp", split_axis=0, concat_axis=0, axis_index_groups=groups, tiled=True
    )
    total_rows = grads.shape[0] * NY * NZ
    scale = BLOCK / (total_rows * picks.shape[0] * BLOCK)
    return finish(parts, scale)


def solution(mesh):
    placed = (P("dp", "col"), P("dp"), P())
    return jax.shard_map(
        on_device, mesh=mesh, in_specs=placed, out_specs=P("dp", "col"), check_vma=False
    )
```

```python
import functools

import jax
import jax.numpy as jnp
from jax import lax
from jax.experimental import pallas as pl
from jax.experimental.pallas import tpu as pltpu
from jax.sharding import PartitionSpec as P

NY, NZ, NX, NCORE = 4, 8, 4, 2
BLOCK = 128
LANES = 128
PER_DEV = 16
N_BLOCKS = 512
CHUNK = BLOCK // NZ
MIB = 1 << 20
PIECES = 4


SCALARS = pl.BlockSpec(memory_space=pltpu.SMEM)
LOCAL = pl.BlockSpec(memory_space=pltpu.VMEM)


def pack_kernel(at, signs_ref, *refs):
    pieces, out_ref = refs[:-1], refs[-1]
    columns = signs_ref[...].astype(jnp.float32).T
    count = pieces[0].shape[0]
    for z in range(NZ):
        rows = pl.ds(z * CHUNK, CHUNK)
        for y in range(NY):
            quarter = lax.rem(z - y + at[0] + NY, NY)
            lanes = pl.ds(pl.multiple_of(quarter * LANES, LANES), LANES)
            for b in range(PER_DEV):
                sign = columns[z * CHUNK : (z + 1) * CHUNK, b : b + 1]
                sign = jnp.broadcast_to(sign, (CHUNK, LANES)).astype(jnp.bfloat16)
                out_ref[y, z, b] = pieces[b // count][b % count, rows, lanes] * sign


def pack(grads, signs, at):
    blocks = grads.reshape(PER_DEV, BLOCK, NY * LANES)
    count = PER_DEV // PIECES
    pieces = [blocks[i * count : (i + 1) * count] for i in range(PIECES)]
    return pl.pallas_call(
        pack_kernel,
        in_specs=[SCALARS] + [LOCAL] * (1 + PIECES),
        out_specs=LOCAL,
        out_shape=jax.ShapeDtypeStruct((NY, NZ, PER_DEV, CHUNK, LANES), jnp.bfloat16),
        compiler_params=pltpu.CompilerParams(vmem_limit_bytes=16 * MIB),
        name="pack",
    )(at, signs.reshape(PER_DEV, BLOCK), *pieces)


def hadamard(parts):
    span = 1
    while span < len(parts):
        done = list(parts)
        for i in range(len(parts)):
            if not i & span:
                done[i] = parts[i] + parts[i + span]
                done[i + span] = parts[i] - parts[i + span]
        parts = done
        span *= 2
    return parts


def mix_kernel(picks_ref, raw_ref, out_ref, work):
    half = N_BLOCKS // 2

    for base in range(0, N_BLOCKS, 16):
        parts = [raw_ref[base + b].astype(jnp.float32) for b in range(16)]
        for b, part in enumerate(hadamard(parts)):
            work[base + b] = part
    for base in [*range(16), *range(half, half + 16)]:
        parts = [work[base + 16 * e] for e in range(16)]
        for e, part in enumerate(hadamard(parts)):
            work[base + 16 * e] = part

    @pl.loop(0, out_ref.shape[0], unroll=4)
    def _(k):
        pick = picks_ref[k]
        low = lax.rem(pick, half)
        side = (1 - 2 * lax.div(pick, half)).astype(jnp.float32)
        out_ref[k] = (work[low] + side * work[low + half]).astype(out_ref.dtype)


def mix(raw, picks):
    return pl.pallas_call(
        mix_kernel,
        in_specs=[SCALARS, LOCAL],
        out_specs=LOCAL,
        scratch_shapes=[pltpu.VMEM((N_BLOCKS, CHUNK, LANES), jnp.float32)],
        out_shape=jax.ShapeDtypeStruct((picks.shape[0], CHUNK, LANES), jnp.bfloat16),
        compiler_params=pltpu.CompilerParams(vmem_limit_bytes=16 * MIB),
        name="mix",
    )(picks, raw)


NEAR = (0, 1, 3)


def share_kernel(*refs):
    pieces, outs, joined = refs[:4], refs[-5:-1], refs[-1]
    depth = outs[0].shape[0]
    for i, out in enumerate(outs):
        out[...] = pieces[i][pl.ds(i % 2 * depth, depth), :]
    for i in range(2):
        joined[pl.ds(i * 2 * depth, 2 * depth), :] = pieces[i][...]


def share(pieces, *after):
    rows = pieces[0].shape[0]
    part = jax.ShapeDtypeStruct((rows // 2, LANES), pieces[0].dtype)
    return pl.pallas_call(
        share_kernel,
        in_specs=[LOCAL] * (4 + len(after)),
        out_specs=[LOCAL] * 5,
        out_shape=[part] * 4 + [jax.ShapeDtypeStruct((2 * rows, LANES), part.dtype)],
        compiler_params=pltpu.CompilerParams(vmem_limit_bytes=16 * MIB),
        cost_estimate=pl.CostEstimate(flops=0, bytes_accessed=MIB, transcendentals=0),
        name="share",
    )(*pieces, *after)


def join_kernel(first, second, *refs):
    joined, depth = refs[-1], first.shape[0]
    joined[pl.ds(0, depth), :] = first[...]
    joined[pl.ds(depth, depth), :] = second[...]


def join(first, second, *after):
    return pl.pallas_call(
        join_kernel,
        in_specs=[LOCAL] * (2 + len(after)),
        out_specs=LOCAL,
        out_shape=jax.ShapeDtypeStruct((2 * first.shape[0], LANES), first.dtype),
        compiler_params=pltpu.CompilerParams(vmem_limit_bytes=16 * MIB),
        cost_estimate=pl.CostEstimate(flops=0, bytes_accessed=MIB, transcendentals=0),
        name="join",
    )(first, second, *after)


def pair_dot(left, own, other):
    return jnp.dot(left, jnp.concatenate([own, other], axis=1), preferred_element_type=jnp.float32)


def others(home, swapped):
    half = home.shape[0]
    return home[...], swapped[pl.ds(0, half), :], swapped[pl.ds(half, half), :]


def near_kernel(*refs):
    cols, own, other, (left, out_ref) = refs[:3], refs[3:6], others(*refs[6:8]), refs[8:]
    for j in range(len(NEAR)):
        left[pl.ds(j * LANES, LANES), :] = cols[j][...].T
    for j in range(len(NEAR)):
        out_ref[j] = pair_dot(left[...], own[j][...], other[j]).astype(out_ref.dtype)


def cost(depth, blocks):
    flops = 2 * depth * blocks * LANES * NCORE * LANES
    return pl.CostEstimate(flops=flops, bytes_accessed=8 * MIB, transcendentals=0)


def gram_near(cols, own, other):
    depth, near = cols[0].shape[0], len(NEAR)
    return pl.pallas_call(
        near_kernel,
        in_specs=[LOCAL] * 8,
        out_specs=[LOCAL] * 2,
        out_shape=[
            jax.ShapeDtypeStruct((near * LANES, depth), jnp.bfloat16),
            jax.ShapeDtypeStruct((near, near * LANES, NCORE * LANES), jnp.bfloat16),
        ],
        compiler_params=pltpu.CompilerParams(vmem_limit_bytes=16 * MIB),
        cost_estimate=cost(depth, near * near),
        name="gram_near",
    )(*cols, *own, *other)


def side_kernel(*refs):
    col, own, other, (last, out_ref) = refs[0], refs[1:4], others(*refs[4:6]), refs[6:]
    last[...] = col[...].T
    for j in range(len(NEAR)):
        out_ref[j] = pair_dot(last[...], own[j][...], other[j]).astype(out_ref.dtype)


def gram_side(col, own, other):
    depth, near = col.shape[0], len(NEAR)
    return pl.pallas_call(
        side_kernel,
        in_specs=[LOCAL] * 6,
        out_specs=[LOCAL] * 2,
        out_shape=[
            jax.ShapeDtypeStruct((LANES, depth), jnp.bfloat16),
            jax.ShapeDtypeStruct((near, LANES, NCORE * LANES), jnp.bfloat16),
        ],
        compiler_params=pltpu.CompilerParams(vmem_limit_bytes=16 * MIB),
        cost_estimate=cost(depth, near),
        name="gram_side",
    )(col, *own, *other)


def far_kernel(at, near_ref, side_ref, left, last, own, other, out_ref):
    x, core, turn, group = at[0], at[1], at[2], at[3]

    def put(step_x, step_y, block):
        panel = lax.rem(x + NX - step_x, NX)
        flip = lax.rem(core + lax.div(group + panel, NY), NCORE)
        quarter = pl.multiple_of(lax.rem(turn + step_y, NY) * LANES, LANES)
        out_ref[panel * NCORE + flip, pl.ds(quarter, LANES), :] = block[:, :LANES]
        out_ref[panel * NCORE + 1 - flip, pl.ds(quarter, LANES), :] = block[:, LANES:]

    whole = jnp.concatenate([left[...], last[...]], axis=0)
    block = pair_dot(whole, own[...], other[...]).astype(out_ref.dtype)
    for j, step in enumerate((*NEAR, 2)):
        put(2, step, block[j * LANES : (j + 1) * LANES])
    for i, step_x in enumerate(NEAR):
        put(step_x, 2, side_ref[i])
        for j, step_y in enumerate(NEAR):
            put(step_x, step_y, near_ref[i, pl.ds(j * LANES, LANES), :])


def gram_far(at, near, side, left, last, own, other):
    return pl.pallas_call(
        far_kernel,
        in_specs=[SCALARS] + [LOCAL] * 6,
        out_specs=LOCAL,
        out_shape=jax.ShapeDtypeStruct((NX * NCORE, NY * LANES, LANES), near.dtype),
        compiler_params=pltpu.CompilerParams(vmem_limit_bytes=16 * MIB),
        cost_estimate=cost(own.shape[0], NY),
        name="gram_far",
    )(at, near, side, left, last, own, other)


def finish_kernel(scale, parts_ref, out_ref):
    for i in range(out_ref.shape[1] // LANES):
        part = pl.ds(i * LANES, LANES)
        total = parts_ref[0, part].astype(jnp.float32)
        for k in range(1, parts_ref.shape[0]):
            total = total + parts_ref[k, part].astype(jnp.float32)
        out_ref[:, part] = (total * scale).T


def finish(parts, scale):
    count, width, rows = parts.shape
    return pl.pallas_call(
        lambda parts_ref, out_ref: finish_kernel(scale, parts_ref, out_ref),
        out_shape=jax.ShapeDtypeStruct((rows, width), jnp.float32),
        compiler_params=pltpu.CompilerParams(vmem_limit_bytes=16 * MIB),
        name="finish",
    )(parts)


def on_device(grads, signs, picks):
    dp, col = lax.axis_index("dp"), lax.axis_index("col")
    y, z = lax.div(dp, NZ), lax.rem(dp, NZ)
    x, core = lax.div(col, NCORE), lax.rem(col, NCORE)
    at = jnp.stack([x, core, lax.rem(z - y + x + NY, NY), lax.rem(z - y + NY, NY)])

    outgoing = pack(grads, signs, at).reshape(NY * NZ, PER_DEV, CHUNK, LANES)
    raw = lax.all_to_all(outgoing, "dp", split_axis=0, concat_axis=0, tiled=True)
    sketch = mix(raw.reshape(N_BLOCKS, CHUNK, LANES), picks).reshape(-1, LANES)

    def along_x(value, step):
        return lax.ppermute(value, "col", [(i, (i + NCORE * step) % (NX * NCORE)) for i in range(NX * NCORE)])

    def along_y(value, step):
        return lax.ppermute(value, "dp", [(i, (i + NZ * step) % (NY * NZ)) for i in range(NY * NZ)])

    def swap(value):
        return lax.ppermute(value, "col", [(i, i ^ 1) for i in range(NX * NCORE)])

    x_up, x_down = along_x(sketch, 1), along_x(sketch, -1)
    y_up, y_down = along_y(sketch, 1), along_y(sketch, -1)
    home = swap(sketch)
    x_low, x_high, y_low, y_high, joined = share((x_up, x_down, y_up, y_down), home)
    y_far = jnp.concatenate([along_y(y_low, 1), along_y(y_high, -1)])
    own, other = (sketch, x_up, x_down), (home, swap(joined))
    left, near = gram_near((sketch, y_up, y_down), own, other)
    x_far = join(along_x(x_low, 1), along_x(x_high, -1), left)
    last, side = gram_side(y_far, own, other)
    partial = gram_far(at, near, side, left, last, x_far, swap(x_far))

    groups = [
        [gy * NZ + (s + gy + NY * h) % NZ for gy in range(NY) for h in range(NZ // NY)]
        for s in range(NY)
    ]
    parts = lax.all_to_all(
        partial, "dp", split_axis=0, concat_axis=0, axis_index_groups=groups, tiled=True
    )
    total_rows = grads.shape[0] * NY * NZ
    scale = BLOCK / (total_rows * picks.shape[0] * BLOCK)
    return finish(parts, scale)


def solution(mesh):
    placed = (P("dp", "col"), P("dp"), P())
    return jax.shard_map(
        on_device, mesh=mesh, in_specs=placed, out_specs=P("dp", "col"), check_vma=False
    )
```

```python
import functools

import jax
import jax.numpy as jnp
from jax import lax
from jax.experimental import pallas as pl
from jax.experimental.pallas import tpu as pltpu
from jax.sharding import PartitionSpec as P

NY, NZ, NX, NCORE = 4, 8, 4, 2
BLOCK = 128
LANES = 128
PER_DEV = 16
N_BLOCKS = 512
CHUNK = BLOCK // NZ
MIB = 1 << 20
PIECES = 4


SCALARS = pl.BlockSpec(memory_space=pltpu.SMEM)
LOCAL = pl.BlockSpec(memory_space=pltpu.VMEM)


def pack_kernel(at, signs_ref, *refs):
    pieces, out_ref = refs[:-1], refs[-1]
    columns = signs_ref[...].astype(jnp.float32).T
    count = pieces[0].shape[0]
    for z in range(NZ):
        rows = pl.ds(z * CHUNK, CHUNK)
        for y in range(NY):
            quarter = lax.rem(z - y + at[0] + NY, NY)
            lanes = pl.ds(pl.multiple_of(quarter * LANES, LANES), LANES)
            for b in range(PER_DEV):
                sign = columns[z * CHUNK : (z + 1) * CHUNK, b : b + 1]
                sign = jnp.broadcast_to(sign, (CHUNK, LANES)).astype(jnp.bfloat16)
                out_ref[y, z, b] = pieces[b // count][b % count, rows, lanes] * sign


def pack(grads, signs, at):
    blocks = grads.reshape(PER_DEV, BLOCK, NY * LANES)
    count = PER_DEV // PIECES
    pieces = [blocks[i * count : (i + 1) * count] for i in range(PIECES)]
    return pl.pallas_call(
        pack_kernel,
        in_specs=[SCALARS] + [LOCAL] * (1 + PIECES),
        out_specs=LOCAL,
        out_shape=jax.ShapeDtypeStruct((NY, NZ, PER_DEV, CHUNK, LANES), jnp.bfloat16),
        compiler_params=pltpu.CompilerParams(vmem_limit_bytes=16 * MIB),
        name="pack",
    )(at, signs.reshape(PER_DEV, BLOCK), *pieces)


def hadamard(parts):
    span = 1
    while span < len(parts):
        done = list(parts)
        for i in range(len(parts)):
            if not i & span:
                done[i] = parts[i] + parts[i + span]
                done[i + span] = parts[i] - parts[i + span]
        parts = done
        span *= 2
    return parts


def mix_kernel(picks_ref, raw_ref, out_ref, work):
    half = N_BLOCKS // 2

    for base in range(0, N_BLOCKS, 16):
        parts = [raw_ref[base + b].astype(jnp.float32) for b in range(16)]
        for b, part in enumerate(hadamard(parts)):
            work[base + b] = part
    for base in [*range(16), *range(half, half + 16)]:
        parts = [work[base + 16 * e] for e in range(16)]
        for e, part in enumerate(hadamard(parts)):
            work[base + 16 * e] = part

    @pl.loop(0, out_ref.shape[0], unroll=16)
    def _(k):
        pick = picks_ref[k]
        low = jnp.bitwise_and(pick, half - 1)
        side = jnp.where(pick < half, 1.0, -1.0).astype(jnp.float32)
        out_ref[k] = (work[low] + side * work[low + half]).astype(out_ref.dtype)


def mix(raw, picks):
    return pl.pallas_call(
        mix_kernel,
        in_specs=[SCALARS, LOCAL],
        out_specs=LOCAL,
        scratch_shapes=[pltpu.VMEM((N_BLOCKS, CHUNK, LANES), jnp.float32)],
        out_shape=jax.ShapeDtypeStruct((picks.shape[0], CHUNK, LANES), jnp.bfloat16),
        compiler_params=pltpu.CompilerParams(vmem_limit_bytes=16 * MIB),
        name="mix",
    )(picks, raw)


NEAR = (0, 1, 3)


def halves_kernel(up, down, *refs):
    low, high = refs[-2:]
    depth = low.shape[0]
    low[...] = up[pl.ds(0, depth), :]
    high[...] = down[pl.ds(depth, depth), :]


def halves(up, down, *after):
    part = jax.ShapeDtypeStruct((up.shape[0] // 2, LANES), up.dtype)
    return pl.pallas_call(
        halves_kernel,
        in_specs=[LOCAL] * (2 + len(after)),
        out_specs=[LOCAL] * 2,
        out_shape=[part] * 2,
        compiler_params=pltpu.CompilerParams(vmem_limit_bytes=16 * MIB),
        cost_estimate=pl.CostEstimate(flops=0, bytes_accessed=MIB, transcendentals=0),
        name="halves",
    )(up, down, *after)


def join_kernel(first, second, *refs):
    joined, depth = refs[-1], first.shape[0]
    joined[pl.ds(0, depth), :] = first[...]
    joined[pl.ds(depth, depth), :] = second[...]


def join(first, second, *after):
    return pl.pallas_call(
        join_kernel,
        in_specs=[LOCAL] * (2 + len(after)),
        out_specs=LOCAL,
        out_shape=jax.ShapeDtypeStruct((2 * first.shape[0], LANES), first.dtype),
        compiler_params=pltpu.CompilerParams(vmem_limit_bytes=16 * MIB),
        cost_estimate=pl.CostEstimate(flops=0, bytes_accessed=MIB, transcendentals=0),
        name="join",
    )(first, second, *after)


def pair_dot(left, own, other):
    return jnp.dot(left, jnp.concatenate([own, other], axis=1), preferred_element_type=jnp.float32)


def near_kernel(*refs):
    cols, own, other, (left, out_ref) = refs[:3], refs[3:6], refs[6:9], refs[9:]
    for j in range(len(NEAR)):
        left[pl.ds(j * LANES, LANES), :] = cols[j][...].T
    for j in range(len(NEAR)):
        out_ref[j] = pair_dot(left[...], own[j][...], other[j][...]).astype(out_ref.dtype)


def cost(depth, blocks):
    flops = 2 * depth * blocks * LANES * NCORE * LANES
    return pl.CostEstimate(flops=flops, bytes_accessed=8 * MIB, transcendentals=0)


def gram_near(cols, own, other):
    depth, near = cols[0].shape[0], len(NEAR)
    return pl.pallas_call(
        near_kernel,
        in_specs=[LOCAL] * 9,
        out_specs=[LOCAL] * 2,
        out_shape=[
            jax.ShapeDtypeStruct((near * LANES, depth), jnp.bfloat16),
            jax.ShapeDtypeStruct((near, near * LANES, NCORE * LANES), jnp.bfloat16),
        ],
        compiler_params=pltpu.CompilerParams(vmem_limit_bytes=16 * MIB),
        cost_estimate=cost(depth, near * near),
        name="gram_near",
    )(*cols, *own, *other)


def side_kernel(*refs):
    col, own, other, (last, out_ref) = refs[0], refs[1:4], refs[4:7], refs[7:]
    last[...] = col[...].T
    for j in range(len(NEAR)):
        out_ref[j] = pair_dot(last[...], own[j][...], other[j][...]).astype(out_ref.dtype)


def gram_side(col, own, other):
    depth, near = col.shape[0], len(NEAR)
    return pl.pallas_call(
        side_kernel,
        in_specs=[LOCAL] * 7,
        out_specs=[LOCAL] * 2,
        out_shape=[
            jax.ShapeDtypeStruct((LANES, depth), jnp.bfloat16),
            jax.ShapeDtypeStruct((near, LANES, NCORE * LANES), jnp.bfloat16),
        ],
        compiler_params=pltpu.CompilerParams(vmem_limit_bytes=16 * MIB),
        cost_estimate=cost(depth, near),
        name="gram_side",
    )(col, *own, *other)


def far_kernel(at, near_ref, side_ref, left, last, own, other, out_ref):
    x, core, turn, group = at[0], at[1], at[2], at[3]

    def put(step_x, step_y, block):
        panel = lax.rem(x + NX - step_x, NX)
        flip = lax.rem(core + lax.div(group + panel, NY), NCORE)
        quarter = pl.multiple_of(lax.rem(turn + step_y, NY) * LANES, LANES)
        out_ref[panel * NCORE + flip, pl.ds(quarter, LANES), :] = block[:, :LANES]
        out_ref[panel * NCORE + 1 - flip, pl.ds(quarter, LANES), :] = block[:, LANES:]

    whole = jnp.concatenate([left[...], last[...]], axis=0)
    block = pair_dot(whole, own[...], other[...]).astype(out_ref.dtype)
    for j, step in enumerate((*NEAR, 2)):
        put(2, step, block[j * LANES : (j + 1) * LANES])
    for i, step_x in enumerate(NEAR):
        put(step_x, 2, side_ref[i])
        for j, step_y in enumerate(NEAR):
            put(step_x, step_y, near_ref[i, pl.ds(j * LANES, LANES), :])


def gram_far(at, near, side, left, last, own, other):
    return pl.pallas_call(
        far_kernel,
        in_specs=[SCALARS] + [LOCAL] * 6,
        out_specs=LOCAL,
        out_shape=jax.ShapeDtypeStruct((NX * NCORE, NY * LANES, LANES), near.dtype),
        compiler_params=pltpu.CompilerParams(vmem_limit_bytes=16 * MIB),
        cost_estimate=cost(own.shape[0], NY),
        name="gram_far",
    )(at, near, side, left, last, own, other)


def finish_kernel(scale, parts_ref, out_ref):
    for i in range(out_ref.shape[1] // LANES):
        part = pl.ds(i * LANES, LANES)
        total = parts_ref[0, part].astype(jnp.float32)
        for k in range(1, parts_ref.shape[0]):
            total = total + parts_ref[k, part].astype(jnp.float32)
        out_ref[:, part] = (total * scale).T


def finish(parts, scale):
    count, width, rows = parts.shape
    return pl.pallas_call(
        lambda parts_ref, out_ref: finish_kernel(scale, parts_ref, out_ref),
        out_shape=jax.ShapeDtypeStruct((rows, width), jnp.float32),
        compiler_params=pltpu.CompilerParams(vmem_limit_bytes=16 * MIB),
        name="finish",
    )(parts)


def on_device(grads, signs, picks):
    dp, col = lax.axis_index("dp"), lax.axis_index("col")
    y, z = lax.div(dp, NZ), lax.rem(dp, NZ)
    x, core = lax.div(col, NCORE), lax.rem(col, NCORE)
    at = jnp.stack([x, core, lax.rem(z - y + x + NY, NY), lax.rem(z - y + NY, NY)])

    outgoing = pack(grads, signs, at).reshape(NY * NZ, PER_DEV, CHUNK, LANES)
    raw = lax.all_to_all(outgoing, "dp", split_axis=0, concat_axis=0, tiled=True)
    sketch = mix(raw.reshape(N_BLOCKS, CHUNK, LANES), picks).reshape(-1, LANES)

    def along_x(value, step):
        return lax.ppermute(value, "col", [(i, (i + NCORE * step) % (NX * NCORE)) for i in range(NX * NCORE)])

    def along_y(value, step):
        return lax.ppermute(value, "dp", [(i, (i + NZ * step) % (NY * NZ)) for i in range(NY * NZ)])

    def swap(value):
        return lax.ppermute(value, "col", [(i, i ^ 1) for i in range(NX * NCORE)])

    x_up, x_down = along_x(sketch, 1), along_x(sketch, -1)
    y_up, y_down = along_y(sketch, 1), along_y(sketch, -1)
    home = swap(sketch)
    x_low, x_high = halves(x_up, x_down)
    y_low, y_high = halves(y_up, y_down, home, x_low)
    y_far = jnp.concatenate([along_y(y_low, 1), along_y(y_high, -1)])
    own, other = (sketch, x_up, x_down), (home, swap(x_up), swap(x_down))
    left, near = gram_near((sketch, y_up, y_down), own, other)
    x_far = join(along_x(x_low, 1), along_x(x_high, -1), left)
    last, side = gram_side(y_far, own, other)
    partial = gram_far(at, near, side, left, last, x_far, swap(x_far))

    groups = [
        [gy * NZ + (s + gy + NY * h) % NZ for gy in range(NY) for h in range(NZ // NY)]
        for s in range(NY)
    ]
    parts = lax.all_to_all(
        partial, "dp", split_axis=0, concat_axis=0, axis_index_groups=groups, tiled=True
    )
    total_rows = grads.shape[0] * NY * NZ
    scale = BLOCK / (total_rows * picks.shape[0] * BLOCK)
    return finish(parts, scale)


def solution(mesh):
    placed = (P("dp", "col"), P("dp"), P())
    return jax.shard_map(
        on_device, mesh=mesh, in_specs=placed, out_specs=P("dp", "col"), check_vma=False
    )
```

```python
import functools

import jax
import jax.numpy as jnp
from jax import lax
from jax.experimental import pallas as pl
from jax.experimental.pallas import tpu as pltpu
from jax.sharding import PartitionSpec as P

NY, NZ, NX, NCORE = 4, 8, 4, 2
BLOCK = 128
LANES = 128
PER_DEV = 16
N_BLOCKS = 512
CHUNK = BLOCK // NZ
MIB = 1 << 20
PIECES = 4


SCALARS = pl.BlockSpec(memory_space=pltpu.SMEM)
LOCAL = pl.BlockSpec(memory_space=pltpu.VMEM)


def pack_kernel(at, signs_ref, *refs):
    pieces, out_ref = refs[:-1], refs[-1]
    columns = signs_ref[...].astype(jnp.float32).T
    count = pieces[0].shape[0]
    for z in range(NZ):
        rows = pl.ds(z * CHUNK, CHUNK)
        for y in range(NY):
            quarter = lax.rem(z - y + at[0] + NY, NY)
            lanes = pl.ds(pl.multiple_of(quarter * LANES, LANES), LANES)
            for b in range(PER_DEV):
                sign = columns[z * CHUNK : (z + 1) * CHUNK, b : b + 1]
                sign = jnp.broadcast_to(sign, (CHUNK, LANES)).astype(jnp.bfloat16)
                out_ref[y, z, b] = pieces[b // count][b % count, rows, lanes] * sign


def pack(grads, signs, at):
    blocks = grads.reshape(PER_DEV, BLOCK, NY * LANES)
    count = PER_DEV // PIECES
    pieces = [blocks[i * count : (i + 1) * count] for i in range(PIECES)]
    return pl.pallas_call(
        pack_kernel,
        in_specs=[SCALARS] + [LOCAL] * (1 + PIECES),
        out_specs=LOCAL,
        out_shape=jax.ShapeDtypeStruct((NY, NZ, PER_DEV, CHUNK, LANES), jnp.bfloat16),
        compiler_params=pltpu.CompilerParams(vmem_limit_bytes=16 * MIB),
        name="pack",
    )(at, signs.reshape(PER_DEV, BLOCK), *pieces)


def hadamard(parts):
    span = 1
    while span < len(parts):
        done = list(parts)
        for i in range(len(parts)):
            if not i & span:
                done[i] = parts[i] + parts[i + span]
                done[i + span] = parts[i] - parts[i + span]
        parts = done
        span *= 2
    return parts


def mix_kernel(picks_ref, raw_ref, out_ref, work):
    half = N_BLOCKS // 2

    for base in range(0, N_BLOCKS, 16):
        parts = [raw_ref[base + b].astype(jnp.float32) for b in range(16)]
        for b, part in enumerate(hadamard(parts)):
            work[base + b] = part
    for base in [*range(16), *range(half, half + 16)]:
        parts = [work[base + 16 * e] for e in range(16)]
        for e, part in enumerate(hadamard(parts)):
            work[base + 16 * e] = part

    @pl.loop(0, out_ref.shape[0], unroll=16)
    def _(k):
        pick = picks_ref[k]
        low = jnp.bitwise_and(pick, half - 1)
        side = jnp.where(pick < half, 1.0, -1.0).astype(jnp.float32)
        out_ref[k] = (work[low] + side * work[low + half]).astype(out_ref.dtype)


def mix(raw, picks):
    return pl.pallas_call(
        mix_kernel,
        in_specs=[SCALARS, LOCAL],
        out_specs=LOCAL,
        scratch_shapes=[pltpu.VMEM((N_BLOCKS, CHUNK, LANES), jnp.float32)],
        out_shape=jax.ShapeDtypeStruct((picks.shape[0], CHUNK, LANES), jnp.bfloat16),
        compiler_params=pltpu.CompilerParams(vmem_limit_bytes=16 * MIB),
        name="mix",
    )(picks, raw)


NEAR = (0, 1, 3)
NEAR_Y = (0, 3, 1)


def halves_kernel(up, down, *refs):
    low, high = refs[-2:]
    depth = low.shape[0]
    low[...] = up[pl.ds(0, depth), :]
    high[...] = down[pl.ds(depth, depth), :]


def halves(up, down, *after):
    part = jax.ShapeDtypeStruct((up.shape[0] // 2, LANES), up.dtype)
    return pl.pallas_call(
        halves_kernel,
        in_specs=[LOCAL] * (2 + len(after)),
        out_specs=[LOCAL] * 2,
        out_shape=[part] * 2,
        compiler_params=pltpu.CompilerParams(vmem_limit_bytes=16 * MIB),
        cost_estimate=pl.CostEstimate(flops=0, bytes_accessed=MIB, transcendentals=0),
        name="halves",
    )(up, down, *after)


def join_kernel(first, second, *refs):
    joined, depth = refs[-1], first.shape[0]
    joined[pl.ds(0, depth), :] = first[...]
    joined[pl.ds(depth, depth), :] = second[...]


def join(first, second, *after):
    return pl.pallas_call(
        join_kernel,
        in_specs=[LOCAL] * (2 + len(after)),
        out_specs=LOCAL,
        out_shape=jax.ShapeDtypeStruct((2 * first.shape[0], LANES), first.dtype),
        compiler_params=pltpu.CompilerParams(vmem_limit_bytes=16 * MIB),
        cost_estimate=pl.CostEstimate(flops=0, bytes_accessed=MIB, transcendentals=0),
        name="join",
    )(first, second, *after)


def pair_dot(left, own, other):
    return jnp.dot(left, jnp.concatenate([own, other], axis=1), preferred_element_type=jnp.float32)


def near_kernel(*refs):
    cols, own, other, (left, out_ref) = refs[:3], refs[3:6], refs[6:9], refs[9:]
    for j in range(len(NEAR)):
        left[pl.ds(j * LANES, LANES), :] = cols[j][...].T
    for j in range(len(NEAR)):
        out_ref[j] = pair_dot(left[...], own[j][...], other[j][...]).astype(out_ref.dtype)


def cost(depth, blocks):
    flops = 2 * depth * blocks * LANES * NCORE * LANES
    return pl.CostEstimate(flops=flops, bytes_accessed=8 * MIB, transcendentals=0)


def gram_near(cols, own, other):
    depth, near = cols[0].shape[0], len(NEAR)
    return pl.pallas_call(
        near_kernel,
        in_specs=[LOCAL] * 9,
        out_specs=[LOCAL] * 2,
        out_shape=[
            jax.ShapeDtypeStruct((near * LANES, depth), jnp.bfloat16),
            jax.ShapeDtypeStruct((near, near * LANES, NCORE * LANES), jnp.bfloat16),
        ],
        compiler_params=pltpu.CompilerParams(vmem_limit_bytes=16 * MIB),
        cost_estimate=cost(depth, near * near),
        name="gram_near",
    )(*cols, *own, *other)


def side_kernel(*refs):
    col, own, other, (last, out_ref) = refs[0], refs[1:4], refs[4:7], refs[7:]
    last[...] = col[...].T
    for j in range(len(NEAR)):
        out_ref[j] = pair_dot(last[...], own[j][...], other[j][...]).astype(out_ref.dtype)


def gram_side(col, own, other):
    depth, near = col.shape[0], len(NEAR)
    return pl.pallas_call(
        side_kernel,
        in_specs=[LOCAL] * 7,
        out_specs=[LOCAL] * 2,
        out_shape=[
            jax.ShapeDtypeStruct((LANES, depth), jnp.bfloat16),
            jax.ShapeDtypeStruct((near, LANES, NCORE * LANES), jnp.bfloat16),
        ],
        compiler_params=pltpu.CompilerParams(vmem_limit_bytes=16 * MIB),
        cost_estimate=cost(depth, near),
        name="gram_side",
    )(col, *own, *other)


def far_kernel(at, near_ref, side_ref, left, last, own, other, out_ref):
    x, core, turn, group = at[0], at[1], at[2], at[3]

    def put(step_x, step_y, block):
        panel = lax.rem(x + NX - step_x, NX)
        flip = lax.rem(core + lax.div(group + panel, NY), NCORE)
        quarter = pl.multiple_of(lax.rem(turn + step_y, NY) * LANES, LANES)
        out_ref[panel * NCORE + flip, pl.ds(quarter, LANES), :] = block[:, :LANES]
        out_ref[panel * NCORE + 1 - flip, pl.ds(quarter, LANES), :] = block[:, LANES:]

    whole = jnp.concatenate([left[...], last[...]], axis=0)
    block = pair_dot(whole, own[...], other[...]).astype(out_ref.dtype)
    for j, step in enumerate((*NEAR_Y, 2)):
        put(2, step, block[j * LANES : (j + 1) * LANES])
    for i, step_x in enumerate(NEAR):
        put(step_x, 2, side_ref[i])
        for j, step_y in enumerate(NEAR_Y):
            put(step_x, step_y, near_ref[i, pl.ds(j * LANES, LANES), :])


def gram_far(at, near, side, left, last, own, other):
    return pl.pallas_call(
        far_kernel,
        in_specs=[SCALARS] + [LOCAL] * 6,
        out_specs=LOCAL,
        out_shape=jax.ShapeDtypeStruct((NX * NCORE, NY * LANES, LANES), near.dtype),
        compiler_params=pltpu.CompilerParams(vmem_limit_bytes=16 * MIB),
        cost_estimate=cost(own.shape[0], NY),
        name="gram_far",
    )(at, near, side, left, last, own, other)


def finish_kernel(scale, parts_ref, out_ref):
    for i in range(out_ref.shape[1] // LANES):
        part = pl.ds(i * LANES, LANES)
        total = parts_ref[0, part].astype(jnp.float32)
        for k in range(1, parts_ref.shape[0]):
            total = total + parts_ref[k, part].astype(jnp.float32)
        out_ref[:, part] = (total * scale).T


def finish(parts, scale):
    count, width, rows = parts.shape
    return pl.pallas_call(
        lambda parts_ref, out_ref: finish_kernel(scale, parts_ref, out_ref),
        out_shape=jax.ShapeDtypeStruct((rows, width), jnp.float32),
        compiler_params=pltpu.CompilerParams(vmem_limit_bytes=16 * MIB),
        name="finish",
    )(parts)


def on_device(grads, signs, picks):
    dp, col = lax.axis_index("dp"), lax.axis_index("col")
    y, z = lax.div(dp, NZ), lax.rem(dp, NZ)
    x, core = lax.div(col, NCORE), lax.rem(col, NCORE)
    at = jnp.stack([x, core, lax.rem(z - y + x + NY, NY), lax.rem(z - y + NY, NY)])

    outgoing = pack(grads, signs, at).reshape(NY * NZ, PER_DEV, CHUNK, LANES)
    raw = lax.all_to_all(outgoing, "dp", split_axis=0, concat_axis=0, tiled=True)
    sketch = mix(raw.reshape(N_BLOCKS, CHUNK, LANES), picks).reshape(-1, LANES)

    def along_x(value, step):
        return lax.ppermute(value, "col", [(i, (i + NCORE * step) % (NX * NCORE)) for i in range(NX * NCORE)])

    def along_y(value, step):
        return lax.ppermute(value, "dp", [(i, (i + NZ * step) % (NY * NZ)) for i in range(NY * NZ)])

    def swap(value):
        return lax.ppermute(value, "col", [(i, i ^ 1) for i in range(NX * NCORE)])

    x_up, x_down = along_x(sketch, 1), along_x(sketch, -1)
    y_up, y_down = along_y(sketch, 1), along_y(sketch, -1)
    home = swap(sketch)
    x_low, x_high = halves(x_up, x_down)
    y_low, y_high = halves(y_up, y_down, home, x_low)
    y_far = jnp.concatenate([along_y(y_low, 1), along_y(y_high, -1)])
    own, other = (sketch, x_up, x_down), (home, swap(x_up), swap(x_down))
    left, near = gram_near((sketch, y_down, y_up), own, other)
    x_far = join(along_x(x_low, 1), along_x(x_high, -1), left)
    last, side = gram_side(y_far, own, other)
    partial = gram_far(at, near, side, left, last, x_far, swap(x_far))

    groups = [
        [gy * NZ + (s + gy + NY * h) % NZ for gy in range(NY) for h in range(NZ // NY)]
        for s in range(NY)
    ]
    parts = lax.all_to_all(
        partial, "dp", split_axis=0, concat_axis=0, axis_index_groups=groups, tiled=True
    )
    total_rows = grads.shape[0] * NY * NZ
    scale = BLOCK / (total_rows * picks.shape[0] * BLOCK)
    return finish(parts, scale)


def solution(mesh):
    placed = (P("dp", "col"), P("dp"), P())
    return jax.shard_map(
        on_device, mesh=mesh, in_specs=placed, out_specs=P("dp", "col"), check_vma=False
    )
```

```python
import functools

import jax
import jax.numpy as jnp
from jax import lax
from jax.experimental import pallas as pl
from jax.experimental.pallas import tpu as pltpu
from jax.sharding import PartitionSpec as P

NY, NZ, NX, NCORE = 4, 8, 4, 2
BLOCK = 128
LANES = 128
PER_DEV = 16
N_BLOCKS = 512
CHUNK = BLOCK // NZ
MIB = 1 << 20
PIECES = 4


SCALARS = pl.BlockSpec(memory_space=pltpu.SMEM)
LOCAL = pl.BlockSpec(memory_space=pltpu.VMEM)


def pack_kernel(at, signs_ref, *refs):
    pieces, out_ref = refs[:-1], refs[-1]
    columns = signs_ref[...].astype(jnp.float32).T
    count = pieces[0].shape[0]
    for z in range(NZ):
        rows = pl.ds(z * CHUNK, CHUNK)
        for y in range(NY):
            quarter = lax.rem(z - y + at[0] + NY, NY)
            lanes = pl.ds(pl.multiple_of(quarter * LANES, LANES), LANES)
            for b in range(PER_DEV):
                sign = columns[z * CHUNK : (z + 1) * CHUNK, b : b + 1]
                sign = jnp.broadcast_to(sign, (CHUNK, LANES)).astype(jnp.bfloat16)
                out_ref[y, z, b] = pieces[b // count][b % count, rows, lanes] * sign


def pack(grads, signs, at):
    blocks = grads.reshape(PER_DEV, BLOCK, NY * LANES)
    count = PER_DEV // PIECES
    pieces = [blocks[i * count : (i + 1) * count] for i in range(PIECES)]
    return pl.pallas_call(
        pack_kernel,
        in_specs=[SCALARS] + [LOCAL] * (1 + PIECES),
        out_specs=LOCAL,
        out_shape=jax.ShapeDtypeStruct((NY, NZ, PER_DEV, CHUNK, LANES), jnp.bfloat16),
        compiler_params=pltpu.CompilerParams(vmem_limit_bytes=16 * MIB),
        name="pack",
    )(at, signs.reshape(PER_DEV, BLOCK), *pieces)


def hadamard(parts):
    span = 1
    while span < len(parts):
        done = list(parts)
        for i in range(len(parts)):
            if not i & span:
                done[i] = parts[i] + parts[i + span]
                done[i + span] = parts[i] - parts[i + span]
        parts = done
        span *= 2
    return parts


def mix_kernel(picks_ref, raw_ref, out_ref, work):
    half = N_BLOCKS // 2

    for base in range(0, N_BLOCKS, 16):
        parts = [raw_ref[base + b].astype(jnp.float32) for b in range(16)]
        for b, part in enumerate(hadamard(parts)):
            work[base + b] = part
    for base in [*range(16), *range(half, half + 16)]:
        parts = [work[base + 16 * e] for e in range(16)]
        for e, part in enumerate(hadamard(parts)):
            work[base + 16 * e] = part

    @pl.loop(0, out_ref.shape[0], unroll=16)
    def _(k):
        pick = picks_ref[k]
        low = jnp.bitwise_and(pick, half - 1)
        side = jnp.where(pick < half, 1.0, -1.0).astype(jnp.float32)
        out_ref[k] = (work[low] + side * work[low + half]).astype(out_ref.dtype)


def mix(raw, picks):
    return pl.pallas_call(
        mix_kernel,
        in_specs=[SCALARS, LOCAL],
        out_specs=LOCAL,
        scratch_shapes=[pltpu.VMEM((N_BLOCKS, CHUNK, LANES), jnp.float32)],
        out_shape=jax.ShapeDtypeStruct((picks.shape[0], CHUNK, LANES), jnp.bfloat16),
        compiler_params=pltpu.CompilerParams(vmem_limit_bytes=16 * MIB),
        name="mix",
    )(picks, raw)


NEAR = (0, 1, 3)
NEAR_Y = (0, 3, 1)


def halves_kernel(up, down, *refs):
    low, high = refs[-2:]
    depth = low.shape[0]
    low[...] = up[pl.ds(0, depth), :]
    high[...] = down[pl.ds(depth, depth), :]


def halves(up, down, *after):
    part = jax.ShapeDtypeStruct((up.shape[0] // 2, LANES), up.dtype)
    return pl.pallas_call(
        halves_kernel,
        in_specs=[LOCAL] * (2 + len(after)),
        out_specs=[LOCAL] * 2,
        out_shape=[part] * 2,
        compiler_params=pltpu.CompilerParams(vmem_limit_bytes=16 * MIB),
        cost_estimate=pl.CostEstimate(flops=0, bytes_accessed=MIB, transcendentals=0),
        name="halves",
    )(up, down, *after)


def join_kernel(first, second, *refs):
    joined, depth = refs[-1], first.shape[0]
    joined[pl.ds(0, depth), :] = first[...]
    joined[pl.ds(depth, depth), :] = second[...]


def join(first, second, *after):
    return pl.pallas_call(
        join_kernel,
        in_specs=[LOCAL] * (2 + len(after)),
        out_specs=LOCAL,
        out_shape=jax.ShapeDtypeStruct((2 * first.shape[0], LANES), first.dtype),
        compiler_params=pltpu.CompilerParams(vmem_limit_bytes=16 * MIB),
        cost_estimate=pl.CostEstimate(flops=0, bytes_accessed=MIB, transcendentals=0),
        name="join",
    )(first, second, *after)


def pair_dot(left, own, other):
    return jnp.dot(left, jnp.concatenate([own, other], axis=1), preferred_element_type=jnp.float32)


def near_kernel(*refs):
    cols, own, other, (left, out_ref) = refs[:3], refs[3:6], refs[6:9], refs[9:]
    for j in range(len(NEAR)):
        left[pl.ds(j * LANES, LANES), :] = cols[j][...].T
    for j in range(len(NEAR)):
        out_ref[j] = pair_dot(left[...], own[j][...], other[j][...]).astype(out_ref.dtype)


def cost(depth, blocks):
    flops = 2 * depth * blocks * LANES * NCORE * LANES
    return pl.CostEstimate(flops=flops, bytes_accessed=8 * MIB, transcendentals=0)


def gram_near(cols, own, other):
    depth, near = cols[0].shape[0], len(NEAR)
    return pl.pallas_call(
        near_kernel,
        in_specs=[LOCAL] * 9,
        out_specs=[LOCAL] * 2,
        out_shape=[
            jax.ShapeDtypeStruct((near * LANES, depth), jnp.bfloat16),
            jax.ShapeDtypeStruct((near, near * LANES, NCORE * LANES), jnp.bfloat16),
        ],
        compiler_params=pltpu.CompilerParams(vmem_limit_bytes=16 * MIB),
        cost_estimate=cost(depth, near * near),
        name="gram_near",
    )(*cols, *own, *other)


def side_kernel(*refs):
    col, own, other, (last, out_ref) = refs[0], refs[1:4], refs[4:7], refs[7:]
    last[...] = col[...].T
    for j in range(len(NEAR)):
        out_ref[j] = pair_dot(last[...], own[j][...], other[j][...]).astype(out_ref.dtype)


def gram_side(col, own, other):
    depth, near = col.shape[0], len(NEAR)
    return pl.pallas_call(
        side_kernel,
        in_specs=[LOCAL] * 7,
        out_specs=[LOCAL] * 2,
        out_shape=[
            jax.ShapeDtypeStruct((LANES, depth), jnp.bfloat16),
            jax.ShapeDtypeStruct((near, LANES, NCORE * LANES), jnp.bfloat16),
        ],
        compiler_params=pltpu.CompilerParams(vmem_limit_bytes=16 * MIB),
        cost_estimate=cost(depth, near),
        name="gram_side",
    )(col, *own, *other)


def far_kernel(at, near_ref, side_ref, left, last, own, other, out_ref):
    x, core, turn, group = at[0], at[1], at[2], at[3]

    def put(step_x, step_y, block):
        panel = lax.rem(x + NX - step_x, NX)
        flip = lax.rem(core + lax.div(group + panel, NY), NCORE)
        quarter = pl.multiple_of(lax.rem(turn + step_y, NY) * LANES, LANES)
        out_ref[panel * NCORE + flip, pl.ds(quarter, LANES), :] = block[:, :LANES]
        out_ref[panel * NCORE + 1 - flip, pl.ds(quarter, LANES), :] = block[:, LANES:]

    whole = jnp.concatenate([left[...], last[...]], axis=0)
    block = pair_dot(whole, own[...], other[...]).astype(out_ref.dtype)
    for j, step in enumerate((*NEAR_Y, 2)):
        put(2, step, block[j * LANES : (j + 1) * LANES])
    for i, step_x in enumerate(NEAR):
        put(step_x, 2, side_ref[i])
        for j, step_y in enumerate(NEAR_Y):
            put(step_x, step_y, near_ref[i, pl.ds(j * LANES, LANES), :])


def gram_far(at, near, side, left, last, own, other):
    return pl.pallas_call(
        far_kernel,
        in_specs=[SCALARS] + [LOCAL] * 6,
        out_specs=LOCAL,
        out_shape=jax.ShapeDtypeStruct((NX * NCORE, NY * LANES, LANES), near.dtype),
        compiler_params=pltpu.CompilerParams(vmem_limit_bytes=16 * MIB),
        cost_estimate=cost(own.shape[0], NY),
        name="gram_far",
    )(at, near, side, left, last, own, other)


def finish_kernel(scale, parts_ref, out_ref, done, sems):
    copies = []
    for i in range(done.shape[0]):
        part = pl.ds(i * LANES, LANES)
        total = parts_ref[0, part].astype(jnp.float32)
        for k in range(1, parts_ref.shape[0]):
            total = total + parts_ref[k, part].astype(jnp.float32)
        done[i] = (total * scale).T
        copies.append(pltpu.make_async_copy(done.at[i], out_ref.at[:, part], sems.at[i]))
        copies[-1].start()
    for copy in copies:
        copy.wait()


def finish(parts, scale):
    count, width, rows = parts.shape
    pieces = width // LANES
    return pl.pallas_call(
        functools.partial(finish_kernel, scale),
        in_specs=[LOCAL],
        out_specs=pl.BlockSpec(memory_space=pl.ANY),
        out_shape=jax.ShapeDtypeStruct((rows, width), jnp.float32),
        scratch_shapes=[
            pltpu.VMEM((pieces, rows, LANES), jnp.float32),
            pltpu.SemaphoreType.DMA((pieces,)),
        ],
        compiler_params=pltpu.CompilerParams(vmem_limit_bytes=16 * MIB),
        name="finish",
    )(parts)


def on_device(grads, signs, picks):
    dp, col = lax.axis_index("dp"), lax.axis_index("col")
    y, z = lax.div(dp, NZ), lax.rem(dp, NZ)
    x, core = lax.div(col, NCORE), lax.rem(col, NCORE)
    at = jnp.stack([x, core, lax.rem(z - y + x + NY, NY), lax.rem(z - y + NY, NY)])

    outgoing = pack(grads, signs, at).reshape(NY * NZ, PER_DEV, CHUNK, LANES)
    raw = lax.all_to_all(outgoing, "dp", split_axis=0, concat_axis=0, tiled=True)
    sketch = mix(raw.reshape(N_BLOCKS, CHUNK, LANES), picks).reshape(-1, LANES)

    def along_x(value, step):
        return lax.ppermute(value, "col", [(i, (i + NCORE * step) % (NX * NCORE)) for i in range(NX * NCORE)])

    def along_y(value, step):
        return lax.ppermute(value, "dp", [(i, (i + NZ * step) % (NY * NZ)) for i in range(NY * NZ)])

    def swap(value):
        return lax.ppermute(value, "col", [(i, i ^ 1) for i in range(NX * NCORE)])

    x_up, x_down = along_x(sketch, 1), along_x(sketch, -1)
    y_up, y_down = along_y(sketch, 1), along_y(sketch, -1)
    home = swap(sketch)
    x_low, x_high = halves(x_up, x_down)
    y_low, y_high = halves(y_up, y_down, home, x_low)
    y_far = jnp.concatenate([along_y(y_low, 1), along_y(y_high, -1)])
    own, other = (sketch, x_up, x_down), (home, swap(x_up), swap(x_down))
    left, near = gram_near((sketch, y_down, y_up), own, other)
    x_far = join(along_x(x_low, 1), along_x(x_high, -1), left)
    last, side = gram_side(y_far, own, other)
    partial = gram_far(at, near, side, left, last, x_far, swap(x_far))

    groups = [
        [gy * NZ + (s + gy + NY * h) % NZ for gy in range(NY) for h in range(NZ // NY)]
        for s in range(NY)
    ]
    parts = lax.all_to_all(
        partial, "dp", split_axis=0, concat_axis=0, axis_index_groups=groups, tiled=True
    )
    total_rows = grads.shape[0] * NY * NZ
    scale = BLOCK / (total_rows * picks.shape[0] * BLOCK)
    return finish(parts, scale)


def solution(mesh):
    placed = (P("dp", "col"), P("dp"), P())
    return jax.shard_map(
        on_device, mesh=mesh, in_specs=placed, out_specs=P("dp", "col"), check_vma=False
    )
```

```python
import functools

import jax
import jax.numpy as jnp
from jax import lax
from jax.experimental import pallas as pl
from jax.experimental.pallas import tpu as pltpu
from jax.sharding import PartitionSpec as P

NY, NZ, NX, NCORE = 4, 8, 4, 2
BLOCK = 128
LANES = 128
PER_DEV = 16
N_BLOCKS = 512
CHUNK = BLOCK // NZ
MIB = 1 << 20
PIECES = 4


SCALARS = pl.BlockSpec(memory_space=pltpu.SMEM)
LOCAL = pl.BlockSpec(memory_space=pltpu.VMEM)


def pack_kernel(at, signs_ref, *refs):
    pieces, out_ref = refs[:-1], refs[-1]
    columns = signs_ref[...].astype(jnp.float32).T
    count = pieces[0].shape[0]
    for z in range(NZ):
        rows = pl.ds(z * CHUNK, CHUNK)
        for y in range(NY):
            quarter = lax.rem(z - y + at[0] + NY, NY)
            lanes = pl.ds(pl.multiple_of(quarter * LANES, LANES), LANES)
            for b in range(PER_DEV):
                sign = columns[z * CHUNK : (z + 1) * CHUNK, b : b + 1]
                sign = jnp.broadcast_to(sign, (CHUNK, LANES)).astype(jnp.bfloat16)
                out_ref[y, z, b] = pieces[b // count][b % count, rows, lanes] * sign


def pack(grads, signs, at):
    blocks = grads.reshape(PER_DEV, BLOCK, NY * LANES)
    count = PER_DEV // PIECES
    pieces = [blocks[i * count : (i + 1) * count] for i in range(PIECES)]
    return pl.pallas_call(
        pack_kernel,
        in_specs=[SCALARS] + [LOCAL] * (1 + PIECES),
        out_specs=LOCAL,
        out_shape=jax.ShapeDtypeStruct((NY, NZ, PER_DEV, CHUNK, LANES), jnp.bfloat16),
        compiler_params=pltpu.CompilerParams(vmem_limit_bytes=16 * MIB),
        name="pack",
    )(at, signs.reshape(PER_DEV, BLOCK), *pieces)


def hadamard(parts):
    span = 1
    while span < len(parts):
        done = list(parts)
        for i in range(len(parts)):
            if not i & span:
                done[i] = parts[i] + parts[i + span]
                done[i + span] = parts[i] - parts[i + span]
        parts = done
        span *= 2
    return parts


def mix_kernel(picks_ref, raw_ref, out_ref, work):
    half = N_BLOCKS // 2

    for base in range(0, N_BLOCKS, 16):
        parts = [raw_ref[base + b].astype(jnp.float32) for b in range(16)]
        for b, part in enumerate(hadamard(parts)):
            work[base + b] = part
    for base in [*range(16), *range(half, half + 16)]:
        parts = [work[base + 16 * e] for e in range(16)]
        for e, part in enumerate(hadamard(parts)):
            work[base + 16 * e] = part

    @pl.loop(0, out_ref.shape[0], unroll=16)
    def _(k):
        pick = picks_ref[k]
        low = jnp.bitwise_and(pick, half - 1)
        side = jnp.where(pick < half, 1.0, -1.0).astype(jnp.float32)
        out_ref[k] = (work[low] + side * work[low + half]).astype(out_ref.dtype)


def mix(raw, picks):
    return pl.pallas_call(
        mix_kernel,
        in_specs=[SCALARS, LOCAL],
        out_specs=LOCAL,
        scratch_shapes=[pltpu.VMEM((N_BLOCKS, CHUNK, LANES), jnp.float32)],
        out_shape=jax.ShapeDtypeStruct((picks.shape[0], CHUNK, LANES), jnp.bfloat16),
        compiler_params=pltpu.CompilerParams(vmem_limit_bytes=16 * MIB),
        name="mix",
    )(picks, raw)


NEAR = (0, 3, 1)


def halves_kernel(up, down, *refs):
    low, high = refs[-2:]
    depth = low.shape[0]
    low[...] = up[pl.ds(0, depth), :]
    high[...] = down[pl.ds(depth, depth), :]


def halves(up, down, *after):
    part = jax.ShapeDtypeStruct((up.shape[0] // 2, LANES), up.dtype)
    return pl.pallas_call(
        halves_kernel,
        in_specs=[LOCAL] * (2 + len(after)),
        out_specs=[LOCAL] * 2,
        out_shape=[part] * 2,
        compiler_params=pltpu.CompilerParams(vmem_limit_bytes=16 * MIB),
        cost_estimate=pl.CostEstimate(flops=0, bytes_accessed=MIB, transcendentals=0),
        name="halves",
    )(up, down, *after)


def join_kernel(first, second, *refs):
    joined, depth = refs[-1], first.shape[0]
    joined[pl.ds(0, depth), :] = first[...]
    joined[pl.ds(depth, depth), :] = second[...]


def join(first, second, *after):
    return pl.pallas_call(
        join_kernel,
        in_specs=[LOCAL] * (2 + len(after)),
        out_specs=LOCAL,
        out_shape=jax.ShapeDtypeStruct((2 * first.shape[0], LANES), first.dtype),
        compiler_params=pltpu.CompilerParams(vmem_limit_bytes=16 * MIB),
        cost_estimate=pl.CostEstimate(flops=0, bytes_accessed=MIB, transcendentals=0),
        name="join",
    )(first, second, *after)


def pair_dot(left, own, other):
    return jnp.dot(left, jnp.concatenate([own, other], axis=1), preferred_element_type=jnp.float32)


def near_kernel(*refs):
    cols, own, other, (left, out_ref) = refs[:3], refs[3:6], refs[6:9], refs[9:]
    for j in range(len(NEAR)):
        left[pl.ds(j * LANES, LANES), :] = cols[j][...].T
    for j in range(len(NEAR)):
        out_ref[j] = pair_dot(left[...], own[j][...], other[j][...]).astype(out_ref.dtype)


def cost(depth, blocks):
    flops = 2 * depth * blocks * LANES * NCORE * LANES
    return pl.CostEstimate(flops=flops, bytes_accessed=8 * MIB, transcendentals=0)


def gram_near(cols, own, other):
    depth, near = cols[0].shape[0], len(NEAR)
    return pl.pallas_call(
        near_kernel,
        in_specs=[LOCAL] * 9,
        out_specs=[LOCAL] * 2,
        out_shape=[
            jax.ShapeDtypeStruct((near * LANES, depth), jnp.bfloat16),
            jax.ShapeDtypeStruct((near, near * LANES, NCORE * LANES), jnp.bfloat16),
        ],
        compiler_params=pltpu.CompilerParams(vmem_limit_bytes=16 * MIB),
        cost_estimate=cost(depth, near * near),
        name="gram_near",
    )(*cols, *own, *other)


def side_kernel(*refs):
    col, own, other, (last, out_ref) = refs[0], refs[1:4], refs[4:7], refs[7:]
    last[...] = col[...].T
    for j in range(len(NEAR)):
        out_ref[j] = pair_dot(last[...], own[j][...], other[j][...]).astype(out_ref.dtype)


def gram_side(col, own, other):
    depth, near = col.shape[0], len(NEAR)
    return pl.pallas_call(
        side_kernel,
        in_specs=[LOCAL] * 7,
        out_specs=[LOCAL] * 2,
        out_shape=[
            jax.ShapeDtypeStruct((LANES, depth), jnp.bfloat16),
            jax.ShapeDtypeStruct((near, LANES, NCORE * LANES), jnp.bfloat16),
        ],
        compiler_params=pltpu.CompilerParams(vmem_limit_bytes=16 * MIB),
        cost_estimate=cost(depth, near),
        name="gram_side",
    )(col, *own, *other)


def far_kernel(at, near_ref, side_ref, left, last, own, other, out_ref):
    x, core, turn, group = at[0], at[1], at[2], at[3]

    def put(step_x, step_y, block):
        panel = lax.rem(x + NX - step_x, NX)
        flip = lax.rem(core + lax.div(group + panel, NY), NCORE)
        quarter = pl.multiple_of(lax.rem(turn + step_y, NY) * LANES, LANES)
        out_ref[panel * NCORE + flip, pl.ds(quarter, LANES), :] = block[:, :LANES]
        out_ref[panel * NCORE + 1 - flip, pl.ds(quarter, LANES), :] = block[:, LANES:]

    whole = jnp.concatenate([left[...], last[...]], axis=0)
    block = pair_dot(whole, own[...], other[...]).astype(out_ref.dtype)
    for j, step in enumerate((*NEAR, 2)):
        put(2, step, block[j * LANES : (j + 1) * LANES])
    for i, step_x in enumerate(NEAR):
        put(step_x, 2, side_ref[i])
        for j, step_y in enumerate(NEAR):
            put(step_x, step_y, near_ref[i, pl.ds(j * LANES, LANES), :])


def gram_far(at, near, side, left, last, own, other):
    return pl.pallas_call(
        far_kernel,
        in_specs=[SCALARS] + [LOCAL] * 6,
        out_specs=LOCAL,
        out_shape=jax.ShapeDtypeStruct((NX * NCORE, NY * LANES, LANES), near.dtype),
        compiler_params=pltpu.CompilerParams(vmem_limit_bytes=16 * MIB),
        cost_estimate=cost(own.shape[0], NY),
        name="gram_far",
    )(at, near, side, left, last, own, other)


def finish_kernel(scale, parts_ref, out_ref):
    for i in range(out_ref.shape[1] // LANES):
        part = pl.ds(i * LANES, LANES)
        total = parts_ref[0, part].astype(jnp.float32)
        for k in range(1, parts_ref.shape[0]):
            total = total + parts_ref[k, part].astype(jnp.float32)
        out_ref[:, part] = (total * scale).T


def finish(parts, scale):
    count, width, rows = parts.shape
    return pl.pallas_call(
        lambda parts_ref, out_ref: finish_kernel(scale, parts_ref, out_ref),
        out_shape=jax.ShapeDtypeStruct((rows, width), jnp.float32),
        compiler_params=pltpu.CompilerParams(vmem_limit_bytes=16 * MIB),
        name="finish",
    )(parts)


def on_device(grads, signs, picks):
    dp, col = lax.axis_index("dp"), lax.axis_index("col")
    y, z = lax.div(dp, NZ), lax.rem(dp, NZ)
    x, core = lax.div(col, NCORE), lax.rem(col, NCORE)
    at = jnp.stack([x, core, lax.rem(z - y + x + NY, NY), lax.rem(z - y + NY, NY)])

    outgoing = pack(grads, signs, at).reshape(NY * NZ, PER_DEV, CHUNK, LANES)
    raw = lax.all_to_all(outgoing, "dp", split_axis=0, concat_axis=0, tiled=True)
    sketch = mix(raw.reshape(N_BLOCKS, CHUNK, LANES), picks).reshape(-1, LANES)

    def along_x(value, step):
        return lax.ppermute(value, "col", [(i, (i + NCORE * step) % (NX * NCORE)) for i in range(NX * NCORE)])

    def along_y(value, step):
        return lax.ppermute(value, "dp", [(i, (i + NZ * step) % (NY * NZ)) for i in range(NY * NZ)])

    def swap(value):
        return lax.ppermute(value, "col", [(i, i ^ 1) for i in range(NX * NCORE)])

    x_up, x_down = along_x(sketch, 1), along_x(sketch, -1)
    y_up, y_down = along_y(sketch, 1), along_y(sketch, -1)
    home = swap(sketch)
    x_low, x_high = halves(x_up, x_down)
    y_low, y_high = halves(y_up, y_down, home, x_low)
    y_far = jnp.concatenate([along_y(y_low, 1), along_y(y_high, -1)])
    own, other = (sketch, x_down, x_up), (home, swap(x_down), swap(x_up))
    left, near = gram_near((sketch, y_down, y_up), own, other)
    x_far = join(along_x(x_low, 1), along_x(x_high, -1), left)
    last, side = gram_side(y_far, own, other)
    partial = gram_far(at, near, side, left, last, x_far, swap(x_far))

    groups = [
        [gy * NZ + (s + gy + NY * h) % NZ for gy in range(NY) for h in range(NZ // NY)]
        for s in range(NY)
    ]
    parts = lax.all_to_all(
        partial, "dp", split_axis=0, concat_axis=0, axis_index_groups=groups, tiled=True
    )
    total_rows = grads.shape[0] * NY * NZ
    scale = BLOCK / (total_rows * picks.shape[0] * BLOCK)
    return finish(parts, scale)


def solution(mesh):
    placed = (P("dp", "col"), P("dp"), P())
    return jax.shard_map(
        on_device, mesh=mesh, in_specs=placed, out_specs=P("dp", "col"), check_vma=False
    )
```

```python
import functools

import jax
import jax.numpy as jnp
from jax import lax
from jax.experimental import pallas as pl
from jax.experimental.pallas import tpu as pltpu
from jax.sharding import PartitionSpec as P

NY, NZ, NX, NCORE = 4, 8, 4, 2
BLOCK = 128
LANES = 128
PER_DEV = 16
N_BLOCKS = 512
CHUNK = BLOCK // NZ
MIB = 1 << 20
PIECES = 4


SCALARS = pl.BlockSpec(memory_space=pltpu.SMEM)
LOCAL = pl.BlockSpec(memory_space=pltpu.VMEM)


def pack_kernel(at, signs_ref, *refs):
    pieces, out_ref = refs[:-1], refs[-1]
    columns = signs_ref[...].astype(jnp.float32).T
    count = pieces[0].shape[0]
    for z in range(NZ):
        rows = pl.ds(z * CHUNK, CHUNK)
        for y in range(NY):
            quarter = lax.rem(z - y + at[0] + NY, NY)
            lanes = pl.ds(pl.multiple_of(quarter * LANES, LANES), LANES)
            for b in range(PER_DEV):
                sign = columns[z * CHUNK : (z + 1) * CHUNK, b : b + 1]
                sign = jnp.broadcast_to(sign, (CHUNK, LANES)).astype(jnp.bfloat16)
                out_ref[y, z, b] = pieces[b // count][b % count, rows, lanes] * sign


def pack(grads, signs, at):
    blocks = grads.reshape(PER_DEV, BLOCK, NY * LANES)
    count = PER_DEV // PIECES
    pieces = [blocks[i * count : (i + 1) * count] for i in range(PIECES)]
    return pl.pallas_call(
        pack_kernel,
        in_specs=[SCALARS] + [LOCAL] * (1 + PIECES),
        out_specs=LOCAL,
        out_shape=jax.ShapeDtypeStruct((NY, NZ, PER_DEV, CHUNK, LANES), jnp.bfloat16),
        compiler_params=pltpu.CompilerParams(vmem_limit_bytes=16 * MIB),
        name="pack",
    )(at, signs.reshape(PER_DEV, BLOCK), *pieces)


def hadamard(parts):
    span = 1
    while span < len(parts):
        done = list(parts)
        for i in range(len(parts)):
            if not i & span:
                done[i] = parts[i] + parts[i + span]
                done[i + span] = parts[i] - parts[i + span]
        parts = done
        span *= 2
    return parts


def mix_kernel(picks_ref, raw_ref, out_ref, work):
    half = N_BLOCKS // 2

    for base in range(0, N_BLOCKS, 16):
        parts = [raw_ref[base + b].astype(jnp.float32) for b in range(16)]
        for b, part in enumerate(hadamard(parts)):
            work[base + b] = part
    for base in [*range(16), *range(half, half + 16)]:
        parts = [work[base + 16 * e] for e in range(16)]
        for e, part in enumerate(hadamard(parts)):
            work[base + 16 * e] = part

    @pl.loop(0, out_ref.shape[0], unroll=16)
    def _(k):
        pick = picks_ref[k]
        low = jnp.bitwise_and(pick, half - 1)
        side = jnp.where(pick < half, 1.0, -1.0).astype(jnp.float32)
        out_ref[k] = (work[low] + side * work[low + half]).astype(out_ref.dtype)


def mix(raw, picks):
    return pl.pallas_call(
        mix_kernel,
        in_specs=[SCALARS, LOCAL],
        out_specs=LOCAL,
        scratch_shapes=[pltpu.VMEM((N_BLOCKS, CHUNK, LANES), jnp.float32)],
        out_shape=jax.ShapeDtypeStruct((picks.shape[0], CHUNK, LANES), jnp.bfloat16),
        compiler_params=pltpu.CompilerParams(vmem_limit_bytes=16 * MIB),
        name="mix",
    )(picks, raw)


NEAR = (0, 1, 3)
NEAR_Y = (0, 3, 1)


def halves_kernel(up, down, *refs):
    low, high = refs[-2:]
    depth = low.shape[0]
    low[...] = up[pl.ds(0, depth), :]
    high[...] = down[pl.ds(depth, depth), :]


def halves(up, down, *after):
    part = jax.ShapeDtypeStruct((up.shape[0] // 2, LANES), up.dtype)
    return pl.pallas_call(
        halves_kernel,
        in_specs=[LOCAL] * (2 + len(after)),
        out_specs=[LOCAL] * 2,
        out_shape=[part] * 2,
        compiler_params=pltpu.CompilerParams(vmem_limit_bytes=16 * MIB),
        cost_estimate=pl.CostEstimate(flops=0, bytes_accessed=MIB, transcendentals=0),
        name="halves",
    )(up, down, *after)


def join_kernel(first, second, *refs):
    joined, depth = refs[-1], first.shape[0]
    joined[pl.ds(0, depth), :] = first[...]
    joined[pl.ds(depth, depth), :] = second[...]


def join(first, second, *after):
    return pl.pallas_call(
        join_kernel,
        in_specs=[LOCAL] * (2 + len(after)),
        out_specs=LOCAL,
        out_shape=jax.ShapeDtypeStruct((2 * first.shape[0], LANES), first.dtype),
        compiler_params=pltpu.CompilerParams(vmem_limit_bytes=16 * MIB),
        cost_estimate=pl.CostEstimate(flops=0, bytes_accessed=MIB, transcendentals=0),
        name="join",
    )(first, second, *after)


def pair_dot(left, own, other):
    return jnp.dot(left, jnp.concatenate([own, other], axis=1), preferred_element_type=jnp.float32)


def near_kernel(*refs):
    cols, own, other, (left, out_ref) = refs[:3], refs[3:6], refs[6:9], refs[9:]
    for j in range(len(NEAR)):
        left[pl.ds(j * LANES, LANES), :] = cols[j][...].T
    for j in range(len(NEAR)):
        out_ref[j] = pair_dot(left[...], own[j][...], other[j][...]).astype(out_ref.dtype)


def cost(depth, blocks):
    flops = 2 * depth * blocks * LANES * NCORE * LANES
    return pl.CostEstimate(flops=flops, bytes_accessed=8 * MIB, transcendentals=0)


def gram_near(cols, own, other):
    depth, near = cols[0].shape[0], len(NEAR)
    return pl.pallas_call(
        near_kernel,
        in_specs=[LOCAL] * 9,
        out_specs=[LOCAL] * 2,
        out_shape=[
            jax.ShapeDtypeStruct((near * LANES, depth), jnp.bfloat16),
            jax.ShapeDtypeStruct((near, near * LANES, NCORE * LANES), jnp.bfloat16),
        ],
        compiler_params=pltpu.CompilerParams(vmem_limit_bytes=16 * MIB),
        cost_estimate=cost(depth, near * near),
        name="gram_near",
    )(*cols, *own, *other)


def side_kernel(*refs):
    col, own, other, (last, out_ref) = refs[0], refs[1:4], refs[4:7], refs[7:]
    last[...] = col[...].T
    for j in range(len(NEAR)):
        out_ref[j] = pair_dot(last[...], own[j][...], other[j][...]).astype(out_ref.dtype)


def gram_side(col, own, other):
    depth, near = col.shape[0], len(NEAR)
    return pl.pallas_call(
        side_kernel,
        in_specs=[LOCAL] * 7,
        out_specs=[LOCAL] * 2,
        out_shape=[
            jax.ShapeDtypeStruct((LANES, depth), jnp.bfloat16),
            jax.ShapeDtypeStruct((near, LANES, NCORE * LANES), jnp.bfloat16),
        ],
        compiler_params=pltpu.CompilerParams(vmem_limit_bytes=16 * MIB),
        cost_estimate=cost(depth, near),
        name="gram_side",
    )(col, *own, *other)


def far_kernel(at, near_ref, side_ref, left, last, own, other, out_ref):
    x, core, turn, group = at[0], at[1], at[2], at[3]

    def put(step_x, step_y, block):
        panel = lax.rem(x + NX - step_x, NX)
        flip = lax.rem(core + lax.div(group + panel, NY), NCORE)
        quarter = pl.multiple_of(lax.rem(turn + step_y, NY) * LANES, LANES)
        out_ref[panel * NCORE + flip, pl.ds(quarter, LANES), :] = block[:, :LANES]
        out_ref[panel * NCORE + 1 - flip, pl.ds(quarter, LANES), :] = block[:, LANES:]

    whole = jnp.concatenate([left[...], last[...]], axis=0)
    block = pair_dot(whole, own[...], other[...]).astype(out_ref.dtype)
    for j, step in enumerate((*NEAR_Y, 2)):
        put(2, step, block[j * LANES : (j + 1) * LANES])
    for i, step_x in enumerate(NEAR):
        put(step_x, 2, side_ref[i])
        for j, step_y in enumerate(NEAR_Y):
            put(step_x, step_y, near_ref[i, pl.ds(j * LANES, LANES), :])


def gram_far(at, near, side, left, last, own, other):
    return pl.pallas_call(
        far_kernel,
        in_specs=[SCALARS] + [LOCAL] * 6,
        out_specs=LOCAL,
        out_shape=jax.ShapeDtypeStruct((NX * NCORE, NY * LANES, LANES), near.dtype),
        compiler_params=pltpu.CompilerParams(vmem_limit_bytes=16 * MIB),
        cost_estimate=cost(own.shape[0], NY),
        name="gram_far",
    )(at, near, side, left, last, own, other)


def finish_kernel(scale, parts_ref, out_ref):
    for i in range(out_ref.shape[1] // LANES):
        part = pl.ds(i * LANES, LANES)
        total = parts_ref[0, part].astype(jnp.float32)
        for k in range(1, parts_ref.shape[0]):
            total = total + parts_ref[k, part].astype(jnp.float32)
        out_ref[:, part] = (total * scale).T


def finish(parts, scale):
    count, width, rows = parts.shape
    return pl.pallas_call(
        lambda parts_ref, out_ref: finish_kernel(scale, parts_ref, out_ref),
        out_shape=jax.ShapeDtypeStruct((rows, width), jnp.float32),
        compiler_params=pltpu.CompilerParams(vmem_limit_bytes=16 * MIB),
        name="finish",
    )(parts)


def on_device(grads, signs, picks):
    dp, col = lax.axis_index("dp"), lax.axis_index("col")
    y, z = lax.div(dp, NZ), lax.rem(dp, NZ)
    x, core = lax.div(col, NCORE), lax.rem(col, NCORE)
    at = jnp.stack([x, core, lax.rem(z - y + x + NY, NY), lax.rem(z - y + NY, NY)])

    outgoing = pack(grads, signs, at).reshape(NY * NZ, PER_DEV, CHUNK, LANES)
    raw = lax.all_to_all(outgoing, "dp", split_axis=0, concat_axis=0, tiled=True)
    sketch = mix(raw.reshape(N_BLOCKS, CHUNK, LANES), picks).reshape(-1, LANES)

    def along_x(value, step):
        return lax.ppermute(value, "col", [(i, (i + NCORE * step) % (NX * NCORE)) for i in range(NX * NCORE)])

    def along_y(value, step):
        return lax.ppermute(value, "dp", [(i, (i + NZ * step) % (NY * NZ)) for i in range(NY * NZ)])

    def swap(value):
        return lax.ppermute(value, "col", [(i, i ^ 1) for i in range(NX * NCORE)])

    x_up, x_down = along_x(sketch, 1), along_x(sketch, -1)
    y_up, y_down = along_y(sketch, 1), along_y(sketch, -1)
    home = swap(sketch)
    x_low, x_high = halves(x_up, x_down)
    y_low, y_high = halves(y_down, y_up, home, x_low)
    y_far = jnp.concatenate([along_y(y_low, -1), along_y(y_high, 1)])
    own, other = (sketch, x_up, x_down), (home, swap(x_up), swap(x_down))
    left, near = gram_near((sketch, y_down, y_up), own, other)
    x_far = join(along_x(x_low, 1), along_x(x_high, -1), left)
    last, side = gram_side(y_far, own, other)
    partial = gram_far(at, near, side, left, last, x_far, swap(x_far))

    groups = [
        [gy * NZ + (s + gy + NY * h) % NZ for gy in range(NY) for h in range(NZ // NY)]
        for s in range(NY)
    ]
    parts = lax.all_to_all(
        partial, "dp", split_axis=0, concat_axis=0, axis_index_groups=groups, tiled=True
    )
    total_rows = grads.shape[0] * NY * NZ
    scale = BLOCK / (total_rows * picks.shape[0] * BLOCK)
    return finish(parts, scale)


def solution(mesh):
    placed = (P("dp", "col"), P("dp"), P())
    return jax.shard_map(
        on_device, mesh=mesh, in_specs=placed, out_specs=P("dp", "col"), check_vma=False
    )
```

```python
import functools

import jax
import jax.numpy as jnp
from jax import lax
from jax.experimental import pallas as pl
from jax.experimental.pallas import tpu as pltpu
from jax.sharding import PartitionSpec as P

NY, NZ, NX, NCORE = 4, 8, 4, 2
BLOCK = 128
LANES = 128
PER_DEV = 16
N_BLOCKS = 512
CHUNK = BLOCK // NZ
MIB = 1 << 20
PIECES = 2


SCALARS = pl.BlockSpec(memory_space=pltpu.SMEM)
LOCAL = pl.BlockSpec(memory_space=pltpu.VMEM)


def pack_kernel(at, signs_ref, *refs):
    pieces, out_ref = refs[:-1], refs[-1]
    columns = signs_ref[...].astype(jnp.float32).T
    count = pieces[0].shape[0]
    for z in range(NZ):
        rows = pl.ds(z * CHUNK, CHUNK)
        for y in range(NY):
            quarter = lax.rem(z - y + at[0] + NY, NY)
            lanes = pl.ds(pl.multiple_of(quarter * LANES, LANES), LANES)
            for b in range(PER_DEV):
                sign = columns[z * CHUNK : (z + 1) * CHUNK, b : b + 1]
                sign = jnp.broadcast_to(sign, (CHUNK, LANES)).astype(jnp.bfloat16)
                out_ref[y, z, b] = pieces[b // count][b % count, rows, lanes] * sign


def pack(grads, signs, at):
    blocks = grads.reshape(PER_DEV, BLOCK, NY * LANES)
    count = PER_DEV // PIECES
    pieces = [blocks[i * count : (i + 1) * count] for i in range(PIECES)]
    return pl.pallas_call(
        pack_kernel,
        in_specs=[SCALARS] + [LOCAL] * (1 + PIECES),
        out_specs=LOCAL,
        out_shape=jax.ShapeDtypeStruct((NY, NZ, PER_DEV, CHUNK, LANES), jnp.bfloat16),
        compiler_params=pltpu.CompilerParams(vmem_limit_bytes=16 * MIB),
        name="pack",
    )(at, signs.reshape(PER_DEV, BLOCK), *pieces)


def hadamard(parts):
    span = 1
    while span < len(parts):
        done = list(parts)
        for i in range(len(parts)):
            if not i & span:
                done[i] = parts[i] + parts[i + span]
                done[i + span] = parts[i] - parts[i + span]
        parts = done
        span *= 2
    return parts


def mix_kernel(picks_ref, raw_ref, out_ref, work):
    half = N_BLOCKS // 2

    for base in range(0, N_BLOCKS, 16):
        parts = [raw_ref[base + b].astype(jnp.float32) for b in range(16)]
        for b, part in enumerate(hadamard(parts)):
            work[base + b] = part
    for base in [*range(16), *range(half, half + 16)]:
        parts = [work[base + 16 * e] for e in range(16)]
        for e, part in enumerate(hadamard(parts)):
            work[base + 16 * e] = part

    @pl.loop(0, out_ref.shape[0], unroll=16)
    def _(k):
        pick = picks_ref[k]
        low = jnp.bitwise_and(pick, half - 1)
        side = jnp.where(pick < half, 1.0, -1.0).astype(jnp.float32)
        out_ref[k] = (work[low] + side * work[low + half]).astype(out_ref.dtype)


def mix(raw, picks):
    return pl.pallas_call(
        mix_kernel,
        in_specs=[SCALARS, LOCAL],
        out_specs=LOCAL,
        scratch_shapes=[pltpu.VMEM((N_BLOCKS, CHUNK, LANES), jnp.float32)],
        out_shape=jax.ShapeDtypeStruct((picks.shape[0], CHUNK, LANES), jnp.bfloat16),
        compiler_params=pltpu.CompilerParams(vmem_limit_bytes=16 * MIB),
        name="mix",
    )(picks, raw)


NEAR = (0, 1, 3)
NEAR_Y = (0, 3, 1)


def halves_kernel(up, down, *refs):
    low, high = refs[-2:]
    depth = low.shape[0]
    low[...] = up[pl.ds(0, depth), :]
    high[...] = down[pl.ds(depth, depth), :]


def halves(up, down, *after):
    part = jax.ShapeDtypeStruct((up.shape[0] // 2, LANES), up.dtype)
    return pl.pallas_call(
        halves_kernel,
        in_specs=[LOCAL] * (2 + len(after)),
        out_specs=[LOCAL] * 2,
        out_shape=[part] * 2,
        compiler_params=pltpu.CompilerParams(vmem_limit_bytes=16 * MIB),
        cost_estimate=pl.CostEstimate(flops=0, bytes_accessed=MIB, transcendentals=0),
        name="halves",
    )(up, down, *after)


def join_kernel(first, second, *refs):
    joined, depth = refs[-1], first.shape[0]
    joined[pl.ds(0, depth), :] = first[...]
    joined[pl.ds(depth, depth), :] = second[...]


def join(first, second, *after):
    return pl.pallas_call(
        join_kernel,
        in_specs=[LOCAL] * (2 + len(after)),
        out_specs=LOCAL,
        out_shape=jax.ShapeDtypeStruct((2 * first.shape[0], LANES), first.dtype),
        compiler_params=pltpu.CompilerParams(vmem_limit_bytes=16 * MIB),
        cost_estimate=pl.CostEstimate(flops=0, bytes_accessed=MIB, transcendentals=0),
        name="join",
    )(first, second, *after)


def pair_dot(left, own, other):
    return jnp.dot(left, jnp.concatenate([own, other], axis=1), preferred_element_type=jnp.float32)


def near_kernel(*refs):
    cols, own, other, (left, out_ref) = refs[:3], refs[3:6], refs[6:9], refs[9:]
    for j in range(len(NEAR)):
        left[pl.ds(j * LANES, LANES), :] = cols[j][...].T
    for j in range(len(NEAR)):
        out_ref[j] = pair_dot(left[...], own[j][...], other[j][...]).astype(out_ref.dtype)


def cost(depth, blocks):
    flops = 2 * depth * blocks * LANES * NCORE * LANES
    return pl.CostEstimate(flops=flops, bytes_accessed=8 * MIB, transcendentals=0)


def gram_near(cols, own, other):
    depth, near = cols[0].shape[0], len(NEAR)
    return pl.pallas_call(
        near_kernel,
        in_specs=[LOCAL] * 9,
        out_specs=[LOCAL] * 2,
        out_shape=[
            jax.ShapeDtypeStruct((near * LANES, depth), jnp.bfloat16),
            jax.ShapeDtypeStruct((near, near * LANES, NCORE * LANES), jnp.bfloat16),
        ],
        compiler_params=pltpu.CompilerParams(vmem_limit_bytes=16 * MIB),
        cost_estimate=cost(depth, near * near),
        name="gram_near",
    )(*cols, *own, *other)


def side_kernel(*refs):
    col, own, other, (last, out_ref) = refs[0], refs[1:4], refs[4:7], refs[7:]
    last[...] = col[...].T
    for j in range(len(NEAR)):
        out_ref[j] = pair_dot(last[...], own[j][...], other[j][...]).astype(out_ref.dtype)


def gram_side(col, own, other):
    depth, near = col.shape[0], len(NEAR)
    return pl.pallas_call(
        side_kernel,
        in_specs=[LOCAL] * 7,
        out_specs=[LOCAL] * 2,
        out_shape=[
            jax.ShapeDtypeStruct((LANES, depth), jnp.bfloat16),
            jax.ShapeDtypeStruct((near, LANES, NCORE * LANES), jnp.bfloat16),
        ],
        compiler_params=pltpu.CompilerParams(vmem_limit_bytes=16 * MIB),
        cost_estimate=cost(depth, near),
        name="gram_side",
    )(col, *own, *other)


def far_kernel(at, near_ref, side_ref, left, last, own, other, out_ref):
    x, core, turn, group = at[0], at[1], at[2], at[3]

    def put(step_x, step_y, block):
        panel = lax.rem(x + NX - step_x, NX)
        flip = lax.rem(core + lax.div(group + panel, NY), NCORE)
        quarter = pl.multiple_of(lax.rem(turn + step_y, NY) * LANES, LANES)
        out_ref[panel * NCORE + flip, pl.ds(quarter, LANES), :] = block[:, :LANES]
        out_ref[panel * NCORE + 1 - flip, pl.ds(quarter, LANES), :] = block[:, LANES:]

    whole = jnp.concatenate([left[...], last[...]], axis=0)
    block = pair_dot(whole, own[...], other[...]).astype(out_ref.dtype)
    for j, step in enumerate((*NEAR_Y, 2)):
        put(2, step, block[j * LANES : (j + 1) * LANES])
    for i, step_x in enumerate(NEAR):
        put(step_x, 2, side_ref[i])
        for j, step_y in enumerate(NEAR_Y):
            put(step_x, step_y, near_ref[i, pl.ds(j * LANES, LANES), :])


def gram_far(at, near, side, left, last, own, other):
    return pl.pallas_call(
        far_kernel,
        in_specs=[SCALARS] + [LOCAL] * 6,
        out_specs=LOCAL,
        out_shape=jax.ShapeDtypeStruct((NX * NCORE, NY * LANES, LANES), near.dtype),
        compiler_params=pltpu.CompilerParams(vmem_limit_bytes=16 * MIB),
        cost_estimate=cost(own.shape[0], NY),
        name="gram_far",
    )(at, near, side, left, last, own, other)


def finish_kernel(scale, parts_ref, out_ref):
    for i in range(out_ref.shape[1] // LANES):
        part = pl.ds(i * LANES, LANES)
        total = parts_ref[0, part].astype(jnp.float32)
        for k in range(1, parts_ref.shape[0]):
            total = total + parts_ref[k, part].astype(jnp.float32)
        out_ref[:, part] = (total * scale).T


def finish(parts, scale):
    count, width, rows = parts.shape
    return pl.pallas_call(
        lambda parts_ref, out_ref: finish_kernel(scale, parts_ref, out_ref),
        out_shape=jax.ShapeDtypeStruct((rows, width), jnp.float32),
        compiler_params=pltpu.CompilerParams(vmem_limit_bytes=16 * MIB),
        name="finish",
    )(parts)


def on_device(grads, signs, picks):
    dp, col = lax.axis_index("dp"), lax.axis_index("col")
    y, z = lax.div(dp, NZ), lax.rem(dp, NZ)
    x, core = lax.div(col, NCORE), lax.rem(col, NCORE)
    at = jnp.stack([x, core, lax.rem(z - y + x + NY, NY), lax.rem(z - y + NY, NY)])

    outgoing = pack(grads, signs, at).reshape(NY * NZ, PER_DEV, CHUNK, LANES)
    raw = lax.all_to_all(outgoing, "dp", split_axis=0, concat_axis=0, tiled=True)
    sketch = mix(raw.reshape(N_BLOCKS, CHUNK, LANES), picks).reshape(-1, LANES)

    def along_x(value, step):
        return lax.ppermute(value, "col", [(i, (i + NCORE * step) % (NX * NCORE)) for i in range(NX * NCORE)])

    def along_y(value, step):
        return lax.ppermute(value, "dp", [(i, (i + NZ * step) % (NY * NZ)) for i in range(NY * NZ)])

    def swap(value):
        return lax.ppermute(value, "col", [(i, i ^ 1) for i in range(NX * NCORE)])

    x_up, x_down = along_x(sketch, 1), along_x(sketch, -1)
    y_up, y_down = along_y(sketch, 1), along_y(sketch, -1)
    home = swap(sketch)
    x_low, x_high = halves(x_up, x_down)
    y_low, y_high = halves(y_up, y_down, home, x_low)
    y_far = jnp.concatenate([along_y(y_low, 1), along_y(y_high, -1)])
    own, other = (sketch, x_up, x_down), (home, swap(x_up), swap(x_down))
    left, near = gram_near((sketch, y_down, y_up), own, other)
    x_far = join(along_x(x_low, 1), along_x(x_high, -1), left)
    last, side = gram_side(y_far, own, other)
    partial = gram_far(at, near, side, left, last, x_far, swap(x_far))

    groups = [
        [gy * NZ + (s + gy + NY * h) % NZ for gy in range(NY) for h in range(NZ // NY)]
        for s in range(NY)
    ]
    parts = lax.all_to_all(
        partial, "dp", split_axis=0, concat_axis=0, axis_index_groups=groups, tiled=True
    )
    total_rows = grads.shape[0] * NY * NZ
    scale = BLOCK / (total_rows * picks.shape[0] * BLOCK)
    return finish(parts, scale)


def solution(mesh):
    placed = (P("dp", "col"), P("dp"), P())
    return jax.shard_map(
        on_device, mesh=mesh, in_specs=placed, out_specs=P("dp", "col"), check_vma=False
    )
```
